32 devices in a mesh: expert: 4 (over y, core), hidden: 8 (over z, x).
Axes of the slice: x: 2, y: 2, z: 4, core: 2. Of those that a mesh axis runs over, the one named last changes fastest.
Arguments:
- tokens: bfloat16 [16384, 512], P(('expert', 'hidden')), may hold values from -6 to 6
- lengths: int32 [32, 32], P(('expert', 'hidden')), may hold values from 1 to 128, 512 in all within a row
- task_ids: int32 [32, 32], P(('expert', 'hidden')), may hold values from 0 to 29
- expert_table: int32 [30, 2], replicated, may hold values from 0 to 7, all different within a row
- norm_gain: float32 [512, 3], P('hidden'), may hold values from 0.25 to 1.75
- norm_bias: float32 [512, 3], P('hidden'), may hold values from -1.5 to 1.5
- w_qkv: float32 [512, 1536], P('hidden', 'expert'), may hold values from -0.25 to 0.25
- w_out: float32 [512, 512], P('hidden', 'expert'), may hold values from -0.75 to 0.75
- w_in: float32 [512, 2048], P('hidden', 'expert'), may hold values from -0.25 to 0.25
- w_down: float32 [2048, 512], P('hidden', 'expert'), may hold values from -0.1875 to 0.1875
- w_router: float32 [512, 8], P('hidden', 'expert'), may hold values from -0.1875 to 0.1875
- expert_up: float32 [8, 512, 2048], P('expert', None, 'hidden'), may hold values from -0.25 to 0.25
- expert_down: float32 [8, 2048, 512], P('expert', 'hidden'), may hold values from -0.1875 to 0.1875
- cotangent: bfloat16 [16384, 512], P(('expert', 'hidden')), may hold values from -6 to 6
Outputs:
- layer_out: bfloat16 [16384, 512], P(('expert', 'hidden'))
- grad_tokens: float32 [16384, 512], P(('expert', 'hidden'))
- grad_gain: float32 [512, 3], P('hidden')
- grad_bias: float32 [512, 3], P('hidden')
- grad_qkv: float32 [512, 1536], P('hidden', 'expert')
- grad_out: float32 [512, 512], P('hidden', 'expert')
- grad_in: float32 [512, 2048], P('hidden', 'expert')
- grad_down: float32 [2048, 512], P('hidden', 'expert')
- grad_router: float32 [512, 8], P('hidden', 'expert')
- grad_expert_up: float32 [8, 512, 2048], P('expert', None, 'hidden')
- grad_expert_down: float32 [8, 2048, 512], P('expert', 'hidden')
The draws below stay inside these ranges and needn't reach their ends.
Inputs may be any that keep to these rules, and one draw needn't show every extreme that they name: Each row holds the sentence lengths of one pack in order; they sum to 512, and the largest of every row is 128. `task_ids`: some tasks are much more frequent than others. `expert_table`: each row names two different experts; every expert is named by some task.
All inputs are finite; a program needn't handle non-finite values.
Results may differ from the reference program's by a relative error of at most 0.014.
The reference program's roundings to bfloat16 on the way count: a program that leaves them out, or rounds other values in their place, can miss the bound.
Values may be sent and summed in bfloat16 or wider, within the bound.
No kernel may reach another device: no remote copies, remote signals or barrier semaphores. Data moves between devices by JAX's collectives and lax.ppermute only.
A program may use at most 256 MiB of HBM per device.

```python
import math
import jax
import jax.numpy as jnp
import numpy as np
from jax import lax

D = 512
FF = 2048
HEADS = 8
HEAD_DIM = 64
TOK_DEV = 512
SENTS = 32
TASKS = 30
MAXLEN = 128
EXPERTS = 8
CAP = 128
PACKS = 32
TOKENS = 16384


def set_ends(entries, key, least, largest):
    index_at = [jax.random.randint(jax.random.fold_in(key, axis), (), 0, length) for axis, length in enumerate(entries.shape)]
    main_axis = entries.shape.index(max(entries.shape))
    beside = index_at[:main_axis] + [(index_at[main_axis] + 1) % entries.shape[main_axis]] + index_at[main_axis + 1:]
    return entries.at[tuple(index_at)].set(least).at[tuple(beside)].set(largest)


def shard_levels(own_key, shape, cuts, least, top_value):
    loudness = 1.0
    for position, blocks in cuts:
        draws = jax.random.uniform(jax.random.fold_in(jax.random.fold_in(own_key, 6), position), (blocks,), jnp.float32, least / len(cuts), top_value / len(cuts))
        loudness = loudness * jnp.repeat(jnp.exp(draws), shape[position] // blocks).reshape((-1,) + (1,) * (len(shape) - 1 - position))
    return loudness


def cumulative_ranks(amount, lean):
    weights = [(1 << 20) // math.isqrt(standing ** lean) + 1 for standing in range(1, amount + 1)]
    width = 1 + sum(weights) // (1 << 30)
    return np.cumsum(np.array([max(1, weight // width) for weight in weights]))


def ranked_ids(key, dims, count, lean):
    listing = cumulative_ranks(count, lean)
    lot = jax.random.randint(jax.random.fold_in(key, 1), dims, 0, int(listing[count - 1]))
    standing = jnp.searchsorted(jnp.asarray(listing, jnp.int32), lot, side="right")
    return jax.random.permutation(jax.random.fold_in(key, 2), count)[standing].astype(jnp.int32)


def different_ones(own_key, rows, count, top, lift):
    ranking = jax.random.permutation(jax.random.fold_in(own_key, 1), count)
    pull = ranking
    for power in range(3):
        pull = pull * pull // count
    pull = pull * lift // count
    lots = jax.random.randint(jax.random.fold_in(own_key, 2), (rows, count), 0, 4096) + pull
    sure = jax.random.permutation(jax.random.fold_in(own_key, 3), rows)[jnp.arange(count) % rows]
    lots = jnp.where(jnp.arange(rows)[:, None] == sure[None, :], 1 << 14, lots)
    merit = lots * count + jnp.arange(count)
    return lax.top_k(merit.astype(jnp.int32), top)[1].astype(jnp.int32)


def profile(count, total, most, slope):
    portions = [(1 << 20) // math.isqrt(rank ** slope) + 1 for rank in range(2, count + 1)]
    spare, holding = total - most - (count - 1), [1] * (count - 1)
    while spare > 0:
        candidates = [i for i in range(count - 1) if holding[i] < most]
        pool, budget = sum([portions[i] for i in candidates]), spare
        for i in candidates:
            more = min(most - holding[i], max(1, budget * portions[i] // pool), spare)
            holding[i] = holding[i] + more
            spare = spare - more
    return np.array([most] + holding)


def uneven_parts(rng, count, total, limit, lean):
    if count == 2:
        one = jax.random.randint(rng, (), max(1, total - limit), min(limit, total - 1) + 1)
        return jnp.stack([one, total - one])
    tallies = jnp.asarray(profile(count, total, limit, lean), jnp.int32)
    twos = (count - 1) // 2
    giver, receiver = tallies[1:1 + 2 * twos:2], tallies[2:2 + 2 * twos:2]
    slack = jnp.minimum(giver - 1, limit - receiver)
    moved = jax.random.randint(jax.random.fold_in(rng, 1), (twos,), 0, 1 << 20) % (slack + 1)
    tallies = tallies.at[1:1 + 2 * twos:2].set(giver - moved).at[2:2 + 2 * twos:2].set(receiver + moved)
    return tallies[jax.random.permutation(jax.random.fold_in(rng, 2), count)]


def bell_draw(stream_key, extent, deviation, most, pieces=(), kind=jnp.bfloat16):
    drawn = deviation * jax.random.normal(stream_key, extent, jnp.float32)
    if pieces:
        drawn = drawn * shard_levels(stream_key, extent, pieces, -0.22, 0.18)
    return jnp.clip(drawn, -most, most).astype(kind)


def setup_inputs(seed: int = 0) -> dict:
    seeds = jax.random.split(jax.random.key(seed), 15)
    return {
        "tokens": bell_draw(seeds[0], (TOKENS, D), 1.0, 6.0, ((0, 32),)),
        "lengths": jax.vmap(lambda own: uneven_parts(own, SENTS, TOK_DEV, MAXLEN, 2))(jax.random.split(seeds[1], PACKS)).reshape((PACKS, SENTS)).astype(jnp.int32),
        "task_ids": set_ends(ranked_ids(seeds[2], (PACKS, SENTS), TASKS, 2), jax.random.fold_in(seeds[2], 3), 0, TASKS - 1).astype(jnp.int32),
        "expert_table": different_ones(seeds[3], TASKS, EXPERTS, 2, 0),
        "norm_gain": jnp.clip(1.0 + 0.15 * jax.random.normal(seeds[4], (D, 3), jnp.float32), 0.25, 1.75),
        "norm_bias": bell_draw(seeds[5], (D, 3), 0.3, 1.5, ((0, 8),), jnp.float32),
        "w_qkv": bell_draw(seeds[6], (D, 3 * D), D ** -0.5, 0.25, ((0, 8), (1, 4)), jnp.float32),
        "w_out": bell_draw(seeds[7], (D, D), (D // 8) ** -0.5, 0.75, ((0, 8), (1, 4)), jnp.float32),
        "w_in": bell_draw(seeds[8], (D, FF), D ** -0.5, 0.25, ((0, 8), (1, 4)), jnp.float32),
        "w_down": bell_draw(seeds[9], (FF, D), (FF // 2) ** -0.5, 0.1875, ((0, 8), (1, 4)), jnp.float32),
        "w_router": bell_draw(seeds[10], (D, EXPERTS), (2 * D) ** -0.5, 0.1875, ((0, 8), (1, 4)), jnp.float32),
        "expert_up": bell_draw(seeds[11], (EXPERTS, D, FF), D ** -0.5, 0.25, ((0, 4), (2, 8)), jnp.float32),
        "expert_down": bell_draw(seeds[12], (EXPERTS, FF, D), (FF // 2) ** -0.5, 0.1875, ((0, 4), (1, 8)), jnp.float32),
        "cotangent": bell_draw(seeds[13], (TOKENS, D), 1.0, 6.0, ((0, 32),)),
    }


EPSILON = 1e-05
FILL_SCORE = -1000000000.0
PRECISE = lax.Precision.HIGHEST

@jax.custom_vjp
def low(v):
    return lax.optimization_barrier(v.astype(jnp.bfloat16)).astype(jnp.float32)

@jax.custom_vjp
def low_back(v):
    return v

def low_keep(v):
    return (low(v), None)

def low_pass(kept, grad):
    return (grad,)

def back_keep(v):
    return (v, None)

def back_low(kept, grad):
    return (low(grad),)
low.defvjp(low_keep, low_pass)
low_back.defvjp(back_keep, back_low)

def layer_norm(values, gain_vec, bias_vec):
    center = values - lax.optimization_barrier(jnp.mean(values, axis=-1, keepdims=True))
    spread = lax.optimization_barrier(jnp.mean(center * center, axis=-1, keepdims=True))
    return center * lax.rsqrt(spread + EPSILON) * gain_vec + bias_vec

def gelu_tanh(values):
    return jax.nn.gelu(values, approximate=True)

def token_routes(length_row, task_row, route_table, tok_count):
    sent_ends = jnp.cumsum(length_row).astype(jnp.int32)
    tok_index = jnp.arange(tok_count, dtype=jnp.int32)
    segment = lax.optimization_barrier(jnp.sum((tok_index[:, None] >= sent_ends[None, :]).astype(jnp.int32), axis=1)).astype(jnp.int32)
    sent_hot = (segment[:, None] == jnp.arange(length_row.shape[0], dtype=jnp.int32)[None, :]).astype(jnp.int32)
    task_tok = lax.optimization_barrier(jnp.sum(sent_hot * task_row[None, :], axis=1)).astype(jnp.int32)
    task_hot = (task_tok[:, None] == jnp.arange(route_table.shape[0], dtype=jnp.int32)[None, :]).astype(jnp.int32)
    pair_ids = lax.optimization_barrier(jnp.sum(task_hot[:, :, None] * route_table[None, :, :], axis=1)).astype(jnp.int32)
    return (segment, pair_ids)

def place_rows(pair_ids, expert_count, capacity):
    tok_count = pair_ids.shape[0]
    flat_ids = jnp.concatenate([pair_ids[:, 0], pair_ids[:, 1]])
    expert_hot = (flat_ids[:, None] == jnp.arange(expert_count, dtype=jnp.int32)[None, :]).astype(jnp.int32)
    earlier = (jnp.cumsum(expert_hot, axis=0) - expert_hot).astype(jnp.int32)
    row_rank = lax.optimization_barrier(jnp.sum(earlier * expert_hot, axis=1)).astype(jnp.int32)
    slot_of_row = jnp.where(row_rank < capacity, flat_ids * capacity + row_rank, expert_count * capacity).astype(jnp.int32)
    filler = jnp.full((expert_count * capacity + 1,), 2 * tok_count, jnp.int32)
    slot_row = filler.at[slot_of_row].set(jnp.arange(2 * tok_count, dtype=jnp.int32))
    return (slot_of_row, slot_row[:expert_count * capacity])

def dense_layer(block_in, segment, params):
    gain_vec, bias_vec, qkv_mat, out_mat, in_mat, down_mat = params
    row_count = block_in.shape[0]
    normed = low(layer_norm(block_in, gain_vec[:, 0], bias_vec[:, 0]))
    qkv_rows = low(low_back(jnp.dot(normed, qkv_mat, precision=PRECISE)))
    queries = qkv_rows[:, :D].reshape(row_count, HEADS, HEAD_DIM)
    key_rows = qkv_rows[:, D:2 * D].reshape(row_count, HEADS, HEAD_DIM)
    values = qkv_rows[:, 2 * D:].reshape(row_count, HEADS, HEAD_DIM)
    scores = low_back(jnp.einsum('qhd,khd->hqk', queries, key_rows, precision=PRECISE) * (1.0 / math.sqrt(HEAD_DIM)))
    same_sent = segment[:, None] == segment[None, :]
    scores = jnp.where(same_sent[None], scores, FILL_SCORE)
    row_peak = lax.optimization_barrier(jnp.max(scores, axis=-1, keepdims=True))
    exp_scores = jnp.exp(scores - row_peak)
    prob_rows = low(exp_scores / lax.optimization_barrier(jnp.sum(exp_scores, axis=-1, keepdims=True)))
    attended = low(low_back(jnp.einsum('hqk,khd->qhd', prob_rows, values, precision=PRECISE))).reshape(row_count, D)
    after_attn = block_in + low_back(jnp.dot(attended, out_mat, precision=PRECISE))
    normed_two = low(layer_norm(after_attn, gain_vec[:, 1], bias_vec[:, 1]))
    hidden = low(gelu_tanh(low_back(jnp.dot(normed_two, in_mat, precision=PRECISE))))
    return after_attn + low_back(jnp.dot(hidden, down_mat, precision=PRECISE))

def reference(tokens, lengths, task_ids, expert_table, norm_gain, norm_bias, w_qkv, w_out, w_in, w_down, w_router, expert_up, expert_down, cotangent):

    def routes_of(length_row, task_row):
        return token_routes(length_row, task_row, expert_table, TOK_DEV)

    def places_of(pair_rows):
        return place_rows(pair_rows, EXPERTS, CAP)
    segments, pair_ids = jax.vmap(routes_of)(lengths, task_ids)
    slot_ids, slot_rows = jax.vmap(places_of)(pair_ids)
    pack_index = jnp.arange(PACKS, dtype=jnp.int32)[:, None]
    sources = jnp.where(slot_rows < 2 * TOK_DEV, slot_rows % TOK_DEV + pack_index * TOK_DEV, TOKENS).astype(jnp.int32).reshape(-1)
    targets = jnp.where(slot_ids < EXPERTS * CAP, slot_ids + pack_index * (EXPERTS * CAP), PACKS * EXPERTS * CAP).astype(jnp.int32)
    targets = targets.reshape(PACKS, 2, TOK_DEV).transpose(0, 2, 1).reshape(TOKENS, 2)
    pair_flat = pair_ids.reshape(TOKENS, 2)

    def forward(inputs, gain_vec, bias_vec, qkv_mat, out_mat, in_mat, down_mat, route_mat, up_experts, down_experts):
        params = (low(gain_vec), low(bias_vec), low(qkv_mat), low(out_mat), low(in_mat), low(down_mat))

        def dense_step(carried, element):
            return (carried, jax.checkpoint(dense_layer)(element[0], element[1], params))
        _, layer_two = lax.scan(dense_step, None, (inputs.reshape(PACKS, TOK_DEV, D), segments))
        layer_two = layer_two.reshape(TOKENS, D)
        normed = low(layer_norm(layer_two, params[0][:, 2], params[1][:, 2]))
        logits = low_back(jnp.dot(normed, low(route_mat), precision=PRECISE))
        chosen = jnp.take_along_axis(logits, pair_flat, axis=1)
        gate_vals = jax.nn.softmax(chosen, axis=-1)
        padded = jnp.concatenate([normed, jnp.zeros((1, D), jnp.float32)])
        sent_rows = low_back(padded[sources]).reshape(PACKS, EXPERTS, CAP, D)
        expert_rows = sent_rows.transpose(1, 0, 2, 3).reshape(EXPERTS, PACKS * CAP, D)

        def expert_apply(element):
            rows_in, up_mat, down_mat_e = element
            expert_pre = low_back(jnp.dot(rows_in, up_mat, precision=PRECISE))
            return low(low_back(jnp.dot(low(gelu_tanh(expert_pre)), down_mat_e, precision=PRECISE)))
        returned = lax.map(jax.checkpoint(expert_apply), (expert_rows, low(up_experts), low(down_experts)))
        flat_rows = returned.reshape(EXPERTS, PACKS, CAP, D).transpose(1, 0, 2, 3).reshape(PACKS * EXPERTS * CAP, D)
        flat_rows = jnp.concatenate([flat_rows, jnp.zeros((1, D), jnp.float32)])
        first = gate_vals[:, 0:1] * flat_rows[targets[:, 0]]
        second = gate_vals[:, 1:2] * flat_rows[targets[:, 1]]
        return layer_two + first + second
    outputs, pullback = jax.vjp(forward, tokens.astype(jnp.float32), norm_gain, norm_bias, w_qkv, w_out, w_in, w_down, w_router, expert_up, expert_down)
    all_grads = pullback(cotangent.astype(jnp.float32))
    return (outputs.astype(jnp.bfloat16), all_grads[0], all_grads[1], all_grads[2], all_grads[3], all_grads[4], all_grads[5], all_grads[6], all_grads[7], all_grads[8], all_grads[9])
```

```python
import functools
import math

import jax
import jax.numpy as jnp
from jax import lax
from jax.experimental import pallas as pl
from jax.experimental.pallas import tpu as pltpu
from jax.sharding import Mesh, PartitionSpec as P

HEAD_DIM = 64
MAXLEN = 128
LANES = 128
EPSILON = 1e-05
FILL_SCORE = -1000000000.0
AXES = ("y", "c", "z", "x")
VMEM_BYTES = 56 * 1024 * 1024
GELU_A = math.sqrt(2.0 / math.pi)
GELU_B = 0.044715

F32 = jnp.float32
BF16 = jnp.bfloat16

NN = (((1,), (0,)), ((), ()))
NT = (((1,), (1,)), ((), ()))
TN = (((0,), (0,)), ((), ()))


def mm(a, b, dims=NN):
    return lax.dot_general(a, b, dims, preferred_element_type=F32)


def gelu(v):
    t = jnp.tanh(GELU_A * (v + GELU_B * (v * v * v)))
    return 0.5 * v * (1.0 + t)


def gelu_both(v):
    v2 = v * v
    t = jnp.tanh(GELU_A * (v + GELU_B * (v2 * v)))
    half = 0.5 * (1.0 + t)
    slope = half + 0.5 * v * (1.0 - t * t) * (GELU_A + (3.0 * GELU_A * GELU_B) * v2)
    return v * half, slope


def norm_parts(v):
    center = v - jnp.mean(v, axis=-1, keepdims=True)
    r = lax.rsqrt(jnp.mean(center * center, axis=-1, keepdims=True) + EPSILON)
    return center * r, r


def norm_back(xhat, r, gain, h):
    hg = h * gain
    inner = jnp.mean(hg * xhat, axis=-1, keepdims=True)
    dv = r * (hg - jnp.mean(hg, axis=-1, keepdims=True) - xhat * inner)
    return dv, jnp.sum(h * xhat, axis=0, keepdims=True), jnp.sum(h, axis=0, keepdims=True)


def params(**kw):
    return pltpu.CompilerParams(vmem_limit_bytes=VMEM_BYTES, **kw)


def vmem():
    return pl.BlockSpec(memory_space=pltpu.VMEM)


def smem():
    return pl.BlockSpec(memory_space=pltpu.SMEM)


def anywhere():
    return pl.BlockSpec(memory_space=pl.ANY)


class Layout:
    def __init__(self, sizes):
        self.sizes = sizes
        self.count = math.prod(sizes.values())

    def owner(self, me_ref, k, order):
        at = {}
        for axis in reversed(order):
            n = self.sizes[axis]
            at[axis] = lax.bitwise_xor(me_ref[AXES.index(axis)], lax.rem(k, n))
            k = lax.div(k, n)
        return at["y"] * self.sizes["c"] + at["c"], at["z"] * self.sizes["x"] + at["x"]


def move_pieces(layout, me_ref, order, stack_ref, parts, sem, inward):
    @pl.loop(0, layout.count)
    def _(k):
        e, h = layout.owner(me_ref, k, order)
        for whole, rows, cols, first in parts:
            piece = stack_ref.at[k, :, pl.ds(first, cols)]
            block = whole.at[
                pl.ds(pl.multiple_of(h * rows, rows), rows),
                pl.ds(pl.multiple_of(e * cols, cols), cols),
            ]
            src, dst = (piece, block) if inward else (block, piece)
            pltpu.make_async_copy(src, dst, sem).start()


def wait_all(ref, sem):
    pltpu.make_async_copy(ref, ref, sem).wait()


def routes_kernel(capacity, experts, len_row, len_col, task_row, task_col, table, table_t, rows_out, cols_out):
    sents = len_row.shape[1]
    tasks = table.shape[0]
    toks = rows_out.shape[1]
    f = lambda v: v.astype(F32)
    i0 = lax.broadcasted_iota(jnp.int32, (sents, sents), 0)
    i1 = lax.broadcasted_iota(jnp.int32, (sents, sents), 1)
    ends_row = jnp.sum(jnp.where(i0 <= i1, f(len_col[...]), 0.0), axis=0, keepdims=True)
    ends_col = jnp.sum(jnp.where(i1 <= i0, f(len_row[...]), 0.0), axis=1, keepdims=True)
    starts_row = ends_row - f(len_row[...])
    starts_col = ends_col - f(len_col[...])
    tok = f(lax.broadcasted_iota(jnp.int32, (toks, sents), 0))
    sent = lax.broadcasted_iota(jnp.int32, (toks, sents), 1)
    hot = (tok >= starts_row) & (tok < ends_row)
    seg_c = jnp.sum(jnp.where(hot, f(sent), 0.0), axis=1, keepdims=True)
    task_c = jnp.sum(jnp.where(hot, f(task_row[...]), 0.0), axis=1, keepdims=True)
    thot = f(lax.broadcasted_iota(jnp.int32, (toks, tasks), 1)) == task_c
    pair_c = [
        jnp.sum(jnp.where(thot, f(table_t[c : c + 1, :]), 0.0), axis=1, keepdims=True)
        for c in range(2)
    ]
    tok = f(lax.broadcasted_iota(jnp.int32, (sents, toks), 1))
    sent = lax.broadcasted_iota(jnp.int32, (sents, toks), 0)
    hot = (tok >= starts_col) & (tok < ends_col)
    seg_r = jnp.sum(jnp.where(hot, f(sent), 0.0), axis=0, keepdims=True)
    task_r = jnp.sum(jnp.where(hot, f(task_col[...]), 0.0), axis=0, keepdims=True)
    thot = f(lax.broadcasted_iota(jnp.int32, (tasks, toks), 0)) == task_r
    pair_r = [
        jnp.sum(jnp.where(thot, f(table[:, c : c + 1]), 0.0), axis=0, keepdims=True)
        for c in range(2)
    ]
    a0 = lax.broadcasted_iota(jnp.int32, (toks, toks), 0)
    a1 = lax.broadcasted_iota(jnp.int32, (toks, toks), 1)
    upper = (a0 < a1).astype(BF16)
    lower = (a1 < a0).astype(BF16)
    er = f(lax.broadcasted_iota(jnp.int32, (experts, toks), 0))
    ec = f(lax.broadcasted_iota(jnp.int32, (toks, experts), 1))
    hot_r = [(er == pair_r[c]).astype(F32) for c in range(2)]
    hot_c = [(ec == pair_c[c]).astype(F32) for c in range(2)]
    before_r = [mm(hot_r[c].astype(BF16), upper) for c in range(2)]
    before_c = [mm(lower, hot_c[c].astype(BF16)) for c in range(2)]
    before_r[1] = before_r[1] + jnp.sum(hot_r[0], axis=1, keepdims=True)
    before_c[1] = before_c[1] + jnp.sum(hot_c[0], axis=0, keepdims=True)
    slot_r, slot_c = [], []
    for c in range(2):
        rank = jnp.sum(hot_r[c] * before_r[c], axis=0, keepdims=True)
        slot_r.append(jnp.where(rank < capacity, pair_r[c] * capacity + rank, -1.0))
        rank = jnp.sum(hot_c[c] * before_c[c], axis=1, keepdims=True)
        slot_c.append(jnp.where(rank < capacity, pair_c[c] * capacity + rank, -1.0))
    at = lax.broadcasted_iota(jnp.int32, rows_out.shape, 0)
    rows_out[...] = jnp.where(
        at == 0, seg_r, jnp.where(at == 1, slot_r[0], slot_r[1])
    ).astype(jnp.int32)
    at = lax.broadcasted_iota(jnp.int32, cols_out.shape, 1)
    packed = jnp.where(at == 0, seg_c, 0.0)
    for j, v in enumerate((pair_c[0], pair_c[1], slot_c[0], slot_c[1])):
        packed = jnp.where(at == j + 1, v, packed)
    cols_out[...] = packed.astype(jnp.int32)


def find_routes(lengths, task_ids, expert_table, toks, experts, capacity):
    return pl.pallas_call(
        functools.partial(routes_kernel, capacity, experts),
        out_shape=(
            jax.ShapeDtypeStruct((8, toks), jnp.int32),
            jax.ShapeDtypeStruct((toks, 8), jnp.int32),
        ),
        in_specs=[vmem()] * 6,
        out_specs=(vmem(), vmem()),
        compiler_params=params(),
        name="routes",
    )(lengths, lengths.T, task_ids, task_ids.T, expert_table, expert_table.T)


def head_blocks(toks):
    n = toks // MAXLEN
    return [(i * MAXLEN, max(i - 1, 0) * MAXLEN, min(i + 2, n) * MAXLEN) for i in range(n)]


def two_heads(block, low_half):
    zero = jnp.zeros_like(block)
    return jnp.concatenate([jnp.where(low_half, block, zero), jnp.where(low_half, zero, block)], axis=0)


def pick_heads(stacked, low_half):
    n = stacked.shape[0] // 2
    return jnp.where(low_half, stacked[:n], stacked[n:])


def probabilities(q2, keys, mask):
    scores = mm(q2, keys, NT) * (1.0 / math.sqrt(HEAD_DIM))
    scores = jnp.where(mask, scores, FILL_SCORE)
    exps = jnp.exp(scores - jnp.max(scores, axis=-1, keepdims=True))
    return exps * (1.0 / jnp.sum(exps, axis=-1, keepdims=True))


def same_sentence(cols_ref, rows_ref, q0, k0, k1):
    seg = cols_ref[q0 : q0 + MAXLEN, 0:1]
    return jnp.concatenate([seg, seg], axis=0) == rows_ref[0:1, k0:k1]


def load_qo(layout, me_ref, refs, qkv_w, out_w, sem):
    if len(refs) == 1:
        rows = refs[0].shape[1]
        share = layout.sizes["y"] * layout.sizes["c"]
        move_pieces(
            layout,
            me_ref,
            ("c", "y", "x", "z"),
            refs[0],
            [
                (qkv_w, rows, qkv_w.shape[1] // share, 0),
                (out_w, rows, out_w.shape[1] // share, qkv_w.shape[1] // share),
            ],
            sem,
            True,
        )
    else:
        pltpu.make_async_copy(refs[0], qkv_w, sem).start()
        pltpu.make_async_copy(refs[1], out_w, sem).start()


def load_ff(layout, me_ref, refs, stacked, in_w, down_w, sem):
    if stacked:
        share = layout.sizes["y"] * layout.sizes["c"]
        move_pieces(
            layout, me_ref, ("c", "y", "x", "z"), refs[0],
            [(in_w, refs[0].shape[1], in_w.shape[1] // share, 0)], sem, True,
        )
        move_pieces(
            layout, me_ref, ("c", "x", "y", "z"), refs[1],
            [(down_w, refs[1].shape[1], down_w.shape[1] // share, 0)], sem, True,
        )
    else:
        pltpu.make_async_copy(refs[0], in_w, sem).start()
        pltpu.make_async_copy(refs[1], down_w, sem).start()


def attend_kernel(layout, n_w, me_ref, tok_ref, gb_ref, cols_ref, rows_ref, *rest):
    w_refs = rest[:n_w]
    qkv_ref, att_ref, after_ref, n2_ref, qkv_w, out_w, sems = rest[n_w:]
    load_qo(layout, me_ref, w_refs, qkv_w, out_w, sems.at[0])
    d = tok_ref.shape[1]
    inputs = tok_ref[...].astype(F32)
    xhat, _ = norm_parts(inputs)
    n1 = (xhat * gb_ref[0:1, :] + gb_ref[3:4, :]).astype(BF16)
    wait_all(qkv_w, sems.at[0])
    wait_all(out_w, sems.at[0])
    for j in range(3):
        qkv_ref[:, j * d : (j + 1) * d] = mm(n1, qkv_w[:, j * d : (j + 1) * d]).astype(BF16)
    low_half = lax.broadcasted_iota(jnp.int32, (MAXLEN, LANES), 1) < HEAD_DIM
    for q0, k0, k1 in head_blocks(tok_ref.shape[0]):
        mask = same_sentence(cols_ref, rows_ref, q0, k0, k1)
        for p in range(d // LANES):
            at = lambda j: slice(j * d + p * LANES, j * d + (p + 1) * LANES)
            q2 = two_heads(qkv_ref[q0 : q0 + MAXLEN, at(0)], low_half)
            prob = probabilities(q2, qkv_ref[k0:k1, at(1)], mask).astype(BF16)
            out = mm(prob, qkv_ref[k0:k1, at(2)])
            att_ref[q0 : q0 + MAXLEN, at(0)] = pick_heads(out, low_half).astype(BF16)
    after = inputs + mm(att_ref[...], out_w[...])
    after_ref[...] = after
    xhat, _ = norm_parts(after)
    n2_ref[...] = (xhat * gb_ref[1:2, :] + gb_ref[4:5, :]).astype(BF16)


def attend_back_kernel(layout, n_w, stacked, me_ref, tok_ref, gb_ref, cols_ref, rows_ref, qkv_ref, att_ref, ag_ref, *rest):
    w_refs = rest[:n_w]
    rest = rest[n_w:]
    gtok_ref, gb1_ref = rest[:2]
    g_refs = rest[2 : 2 + n_w]
    qkv_w, out_w, dq_s, dk_s, dv_s, gqkv_s, gout_s, sems = rest[2 + n_w :]
    load_qo(layout, me_ref, w_refs, qkv_w, out_w, sems.at[0])
    d = tok_ref.shape[1]
    scale = 1.0 / math.sqrt(HEAD_DIM)
    after_grad = ag_ref[...]
    attn_grad = after_grad.astype(BF16)
    wait_all(qkv_w, sems.at[0])
    wait_all(out_w, sems.at[0])
    gout_s[...] = mm(att_ref[...], attn_grad, TN).astype(BF16)
    att_grad = mm(attn_grad, out_w[...], NT).astype(BF16)
    dk_s[...] = jnp.zeros_like(dk_s)
    dv_s[...] = jnp.zeros_like(dv_s)
    low_half = lax.broadcasted_iota(jnp.int32, (MAXLEN, LANES), 1) < HEAD_DIM
    for q0, k0, k1 in head_blocks(tok_ref.shape[0]):
        mask = same_sentence(cols_ref, rows_ref, q0, k0, k1)
        for p in range(d // LANES):
            at = lambda j: slice(j * d + p * LANES, j * d + (p + 1) * LANES)
            lanes = at(0)
            q2 = two_heads(qkv_ref[q0 : q0 + MAXLEN, lanes], low_half)
            keys, values = qkv_ref[k0:k1, at(1)], qkv_ref[k0:k1, at(2)]
            prob = probabilities(q2, keys, mask)
            a2 = two_heads(att_grad[q0 : q0 + MAXLEN, lanes], low_half)
            prob_grad = mm(a2, values, NT)
            dv_s[k0:k1, lanes] += mm(prob.astype(BF16), a2, TN)
            inner = jnp.sum(prob_grad * prob, axis=-1, keepdims=True)
            score_grad = (prob * (prob_grad - inner)).astype(BF16)
            dq_s[q0 : q0 + MAXLEN, lanes] = pick_heads(mm(score_grad, keys), low_half)
            dk_s[k0:k1, lanes] += mm(score_grad, q2, TN)
    grads = [
        (dq_s[...] * scale).astype(BF16),
        (dk_s[...] * scale).astype(BF16),
        dv_s[...].astype(BF16),
    ]
    inputs = tok_ref[...].astype(F32)
    xhat, r = norm_parts(inputs)
    n1 = (xhat * gb_ref[0:1, :] + gb_ref[3:4, :]).astype(BF16)
    for j in range(3):
        gqkv_s[:, j * d : (j + 1) * d] = mm(n1, grads[j], TN).astype(BF16)
    if stacked:
        share = layout.sizes["y"] * layout.sizes["c"]
        rows = g_refs[0].shape[1]
        qc, oc = 3 * d // share, d // share
        move_pieces(
            layout, me_ref, ("c", "y", "x", "z"), g_refs[0],
            [(gqkv_s, rows, qc, 0), (gout_s, rows, oc, qc)], sems.at[1], False,
        )
    else:
        pltpu.make_async_copy(gqkv_s, g_refs[0], sems.at[1]).start()
        pltpu.make_async_copy(gout_s, g_refs[1], sems.at[1]).start()
    n1_grad = sum(mm(grads[j], qkv_w[:, j * d : (j + 1) * d], NT) for j in range(3))
    dv, gain, bias = norm_back(xhat, r, gb_ref[0:1, :], n1_grad)
    gtok_ref[...] = after_grad + dv
    gb1_ref[...] = jnp.concatenate([gain, bias], axis=0)
    for ref in g_refs:
        wait_all(ref, sems.at[1])


def feed_kernel(layout, stacked, experts, capacity, me_ref, after_ref, n2_ref, gb_ref, cols_ref, rows_ref, route_ref, cot_ref, in_ref, down_ref, two_ref, gate_ref, send_ref, in_w, down_w, sems):
    load_ff(layout, me_ref, (in_ref, down_ref), stacked, in_w, down_w, sems.at[0])
    ff = in_w.shape[1]
    wait_all(in_w, sems.at[0])
    wait_all(down_w, sems.at[0])
    n2 = n2_ref[...]
    step = 512
    total = after_ref[...]
    for j in range(ff // step):
        hidden = gelu(mm(n2, in_w[:, j * step : (j + 1) * step])).astype(BF16)
        part = mm(hidden, down_w[j * step : (j + 1) * step, :])
        total = part if j == 0 else total + part
    layer_two = after_ref[...] + total
    two_ref[...] = layer_two
    xhat, _ = norm_parts(layer_two)
    n3 = (xhat * gb_ref[2:3, :] + gb_ref[5:6, :]).astype(BF16)
    logits = mm(n3, route_ref[...])
    lane = lax.broadcasted_iota(jnp.int32, logits.shape, 1)
    chosen = [
        jnp.sum(jnp.where(lane == cols_ref[:, c + 1 : c + 2], logits, 0.0), axis=1, keepdims=True)
        for c in range(2)
    ]
    peak = jnp.maximum(chosen[0], chosen[1])
    exps = [jnp.exp(v - peak) for v in chosen]
    gates = [v / (exps[0] + exps[1]) for v in exps]
    gate_ref[...] = jnp.where(lane == 0, gates[0], jnp.where(lane == 1, gates[1], 0.0))
    upstream = cot_ref[...].astype(F32)
    row_grads = [(gates[c] * upstream).astype(BF16) for c in range(2)]
    toks = n2.shape[0]
    chunk = min(512, experts * capacity)
    per = chunk // capacity
    for j in range(experts * capacity // chunk):
        slot = lax.broadcasted_iota(jnp.int32, (chunk, toks), 0) + j * chunk
        hot = [(slot == rows_ref[c + 1 : c + 2, :]).astype(BF16) for c in range(2)]
        rows_in = mm(hot[0] + hot[1], n3).astype(BF16)
        rows_grad = (mm(hot[0], row_grads[0]) + mm(hot[1], row_grads[1])).astype(BF16)
        for e in range(per):
            send_ref[j * per + e, 0] = rows_in[e * capacity : (e + 1) * capacity]
            send_ref[j * per + e, 1] = rows_grad[e * capacity : (e + 1) * capacity]


def feed_back_kernel(layout, stacked, me_ref, after_ref, n2_ref, two_ref, gate_ref, gb_ref, cols_ref, route_ref, cot_ref, ret_ref, in_ref, down_ref, lout_ref, ag_ref, gb23_ref, grout_ref, gin_ref, gdown_ref, in_w, down_w, gin_s, gdown_s, sems):
    load_ff(layout, me_ref, (in_ref, down_ref), stacked, in_w, down_w, sems.at[0])
    toks, d = n2_ref.shape
    ff = in_w.shape[1]
    slots = ret_ref.shape[0] * ret_ref.shape[2]
    slot = lax.broadcasted_iota(jnp.int32, (toks, slots), 1)
    hot = [(slot == cols_ref[:, c + 3 : c + 4]).astype(BF16) for c in range(2)]
    results = ret_ref[:, 0].reshape(slots, d)
    in_grads = ret_ref[:, 1].reshape(slots, d)
    picked = [mm(hot[c], results) for c in range(2)]
    three_grad = mm(hot[0] + hot[1], in_grads)
    gates = [gate_ref[:, c : c + 1] for c in range(2)]
    layer_two = two_ref[...]
    lout_ref[...] = (layer_two + gates[0] * picked[0] + gates[1] * picked[1]).astype(BF16)
    upstream = cot_ref[...].astype(F32)
    gate_grad = [jnp.sum(upstream * v, axis=1, keepdims=True) for v in picked]
    mean = gates[0] * gate_grad[0] + gates[1] * gate_grad[1]
    chosen_grad = [gates[c] * (gate_grad[c] - mean) for c in range(2)]
    lane = lax.broadcasted_iota(jnp.int32, (toks, route_ref.shape[1]), 1)
    logit_grad = sum(
        jnp.where(lane == cols_ref[:, c + 1 : c + 2], chosen_grad[c], 0.0) for c in range(2)
    ).astype(BF16)
    three_grad = three_grad + mm(logit_grad, route_ref[...], NT)
    xhat, r = norm_parts(layer_two)
    n3 = (xhat * gb_ref[2:3, :] + gb_ref[5:6, :]).astype(BF16)
    grout_ref[...] = mm(n3, logit_grad, TN)
    dv, gain3, bias3 = norm_back(xhat, r, gb_ref[2:3, :], three_grad)
    two_grad = upstream + dv
    ffn_grad = two_grad.astype(BF16)
    n2 = n2_ref[...]
    wait_all(in_w, sems.at[0])
    wait_all(down_w, sems.at[0])
    step = 512
    n2_grad = None
    for j in range(ff // step):
        at = slice(j * step, (j + 1) * step)
        hidden, slope = gelu_both(mm(n2, in_w[:, at]))
        gdown_s[at, :] = mm(hidden.astype(BF16), ffn_grad, TN).astype(BF16)
        pre_grad = (mm(ffn_grad, down_w[at, :], NT) * slope).astype(BF16)
        gin_s[:, at] = mm(n2, pre_grad, TN).astype(BF16)
        part = mm(pre_grad, in_w[:, at], NT)
        n2_grad = part if n2_grad is None else n2_grad + part
    if stacked:
        share = layout.sizes["y"] * layout.sizes["c"]
        move_pieces(
            layout, me_ref, ("c", "y", "x", "z"), gin_ref,
            [(gin_s, gin_ref.shape[1], ff // share, 0)], sems.at[1], False,
        )
        move_pieces(
            layout, me_ref, ("c", "x", "y", "z"), gdown_ref,
            [(gdown_s, gdown_ref.shape[1], d // share, 0)], sems.at[1], False,
        )
    else:
        pltpu.make_async_copy(gin_s, gin_ref, sems.at[1]).start()
        pltpu.make_async_copy(gdown_s, gdown_ref, sems.at[1]).start()
    xhat, r = norm_parts(after_ref[...])
    dv, gain2, bias2 = norm_back(xhat, r, gb_ref[1:2, :], n2_grad)
    ag_ref[...] = two_grad + dv
    gb23_ref[...] = jnp.concatenate([gain2, gain3, bias2, bias3], axis=0)
    wait_all(gin_ref, sems.at[1])
    wait_all(gdown_ref, sems.at[1])


def expert_kernel(n_ring, recv_ref, *rest):
    w_refs = rest[:n_ring]
    ret_ref, hid_ref, pg_ref, w_s, acc_s, gacc_s, sems = rest[n_ring:]
    per = w_refs[0].shape[0]
    for s in range(n_ring):
        pltpu.make_async_copy(w_refs[s], w_s.at[pl.ds(s * per, per)], sems.at[s]).start()
    n_src, _, cap, d = recv_ref.shape
    rows = n_src * cap
    f = w_refs[0].shape[2]
    step = min(512, rows)
    acc_s[...] = jnp.zeros_like(acc_s)
    gacc_s[...] = jnp.zeros_like(gacc_s)
    for s in range(n_ring):
        wait_all(w_s.at[pl.ds(s * per, per)], sems.at[s])

    @pl.loop(0, n_ring * per)
    def _(k):
        for j in range(rows // step):
            src = slice(j * step // cap, (j + 1) * step // cap)
            at = slice(j * step, (j + 1) * step)
            x = recv_ref[src, 0].reshape(step, d)
            g = recv_ref[src, 1].reshape(step, d)
            up = w_s[k, 0:d, :]
            hidden, slope = gelu_both(mm(x, up))
            hidden = hidden.astype(BF16)
            hid_ref[k, at, :] = hidden
            hidden_grad = None
            for b in range(d // f):
                down = w_s[k, d + b * f : d + (b + 1) * f, :]
                lanes = slice(b * f, (b + 1) * f)
                acc_s[at, lanes] += mm(hidden, down)
                part = mm(g[:, lanes], down, NT)
                hidden_grad = part if hidden_grad is None else hidden_grad + part
            pre_grad = (hidden_grad * slope).astype(BF16)
            pg_ref[k, at, :] = pre_grad
            gacc_s[at, :] += mm(pre_grad, up, NT)

    for i in range(n_src):
        ret_ref[i, 0] = acc_s[i * cap : (i + 1) * cap, :].astype(BF16)
        ret_ref[i, 1] = gacc_s[i * cap : (i + 1) * cap, :].astype(BF16)


def expert_grad_kernel(recv_ref, hid_ref, pg_ref, out_ref):
    n_src, _, cap, d = recv_ref.shape
    rows = n_src * cap
    f = hid_ref.shape[2]
    x = recv_ref[:, 0].reshape(rows, d)
    g = recv_ref[:, 1].reshape(rows, d)
    out_ref[0, 0:d, :] = mm(x, pg_ref[0], TN).astype(BF16)
    down = mm(hid_ref[0], g, TN).astype(BF16)
    for b in range(d // f):
        out_ref[0, d + b * f : d + (b + 1) * f, :] = down[:, b * f : (b + 1) * f]


def local(sizes, tokens, lengths, task_ids, expert_table, norm_gain, norm_bias, w_qkv, w_out, w_in, w_down, w_router, expert_up, expert_down, cotangent):
    layout = Layout(sizes)
    toks, d = tokens.shape
    local_experts, _, f = expert_up.shape
    assert local_experts == sizes["x"] == 2
    share = sizes["y"] * sizes["c"]
    n_hid = sizes["z"] * sizes["x"]
    experts = share * local_experts
    capacity = 2 * toks // experts
    ff = w_in.shape[1] * share
    stacked = all(w.shape[1] % LANES == 0 for w in (w_qkv, w_out, w_in, w_down))

    def swap(v, axis, by=1):
        return lax.ppermute(v, axis, [(i, i ^ by) for i in range(sizes[axis])])

    def gather_stack(piece, order):
        t = piece[None]
        for axis in order:
            t = jnp.concatenate([t] + [swap(t, axis, by) for by in range(1, sizes[axis])])
        return t

    def reduce_stack(t, order):
        for axis in order:
            n = sizes[axis]
            t = t.reshape((n, t.shape[0] // n) + t.shape[1:])
            total = t[0].astype(F32)
            for by in range(1, n):
                total = total + swap(t[by].astype(BF16), axis, by).astype(F32)
            t = total
        return t[0]

    def gather_whole(w):
        w = lax.all_gather(w.astype(BF16), ("y", "c"), axis=1, tiled=True)
        return lax.all_gather(w, ("z", "x"), axis=0, tiled=True)

    def reduce_whole(g):
        g = lax.psum_scatter(g.astype(F32), ("z", "x"), scatter_dimension=0, tiled=True)
        return lax.psum_scatter(g, ("y", "c"), scatter_dimension=1, tiled=True)

    me = jnp.stack([lax.axis_index(a) for a in AXES]).astype(jnp.int32)
    x_at = lax.axis_index("x")

    small = jnp.concatenate([w_router, norm_gain, norm_bias], axis=1).astype(BF16)
    small = lax.all_gather(small, AXES)
    rc = w_router.shape[1]
    route = small[:, :, :rc].reshape(share, d, rc).transpose(1, 0, 2).reshape(d, experts)
    route = jnp.pad(route, ((0, 0), (0, LANES - experts)))
    gb = small[:n_hid, :, rc:].reshape(d, 6).T.astype(F32)
    gb = jnp.pad(gb, ((0, 2), (0, 0)))

    if stacked:
        qo = (gather_stack(jnp.concatenate([w_qkv, w_out], axis=1).astype(BF16), "zxyc"),)
        ffw = (gather_stack(w_in.astype(BF16), "zxyc"), gather_stack(w_down.astype(BF16), "zyxc"))
    else:
        qo = (gather_whole(w_qkv), gather_whole(w_out))
        ffw = (gather_whole(w_in), gather_whole(w_down))

    def piece_of(at):
        up = lax.dynamic_index_in_dim(expert_up, at, 0, keepdims=False)
        down = lax.dynamic_index_in_dim(expert_down, at, 0, keepdims=False)
        return jnp.concatenate(
            [up] + [down[:, b * f : (b + 1) * f] for b in range(d // f)], axis=0
        ).astype(BF16)

    ring = [(i, (i + 1) % sizes["z"]) for i in range(sizes["z"])]
    blocks = [jnp.stack([piece_of(x_at), swap(piece_of(1 - x_at), "x")])]
    for _ in range(sizes["z"] - 1):
        blocks.append(lax.ppermute(blocks[-1], "z", ring))

    rows, cols = find_routes(lengths, task_ids, expert_table, toks, experts, capacity)

    def sds(shape, dtype):
        return jax.ShapeDtypeStruct(shape, dtype)

    n_w = len(qo)
    w_scratch = [pltpu.VMEM((d, 3 * d), BF16), pltpu.VMEM((d, d), BF16)]
    qkv, attended, after, n2 = pl.pallas_call(
        functools.partial(attend_kernel, layout, n_w),
        out_shape=(sds((toks, 3 * d), BF16), sds((toks, d), BF16), sds((toks, d), F32), sds((toks, d), BF16)),
        in_specs=[smem()] + [vmem()] * 4 + [anywhere()] * n_w,
        out_specs=(vmem(),) * 4,
        scratch_shapes=w_scratch + [pltpu.SemaphoreType.DMA((1,))],
        compiler_params=params(),
        name="attend",
    )(me, tokens, gb, cols, rows, *qo)

    f_scratch = [pltpu.VMEM((d, ff), BF16), pltpu.VMEM((ff, d), BF16)]
    layer_two, gates, send = pl.pallas_call(
        functools.partial(feed_kernel, layout, stacked, experts, capacity),
        out_shape=(sds((toks, d), F32), sds((toks, LANES), F32), sds((experts, 2, capacity, d), BF16)),
        in_specs=[smem()] + [vmem()] * 7 + [anywhere()] * 2,
        out_specs=(vmem(),) * 3,
        scratch_shapes=f_scratch + [pltpu.SemaphoreType.DMA((1,))],
        compiler_params=params(),
        name="feed",
    )(me, after, n2, gb, cols, rows, route, cotangent, *ffw)

    recv = lax.all_to_all(send, ("y", "c", "x"), split_axis=0, concat_axis=0, tiled=True)
    n_ring = sizes["z"]
    pieces = n_ring * 2
    slots = experts * capacity
    ret, hid, pre_grad = pl.pallas_call(
        functools.partial(expert_kernel, n_ring),
        out_shape=(sds(recv.shape, BF16), sds((pieces, slots, f), BF16), sds((pieces, slots, f), BF16)),
        in_specs=[vmem()] + [anywhere()] * n_ring,
        out_specs=(vmem(),) * 3,
        scratch_shapes=[
            pltpu.VMEM((pieces, 2 * d, f), BF16),
            pltpu.VMEM((slots, d), F32),
            pltpu.VMEM((slots, d), F32),
            pltpu.SemaphoreType.DMA((n_ring,)),
        ],
        compiler_params=params(),
        name="experts",
    )(recv, *blocks)
    back = lax.all_to_all(ret, ("y", "c", "x"), split_axis=0, concat_axis=0, tiled=True)

    expert_grads = pl.pallas_call(
        expert_grad_kernel,
        grid=(pieces,),
        out_shape=sds((pieces, 2 * d, f), BF16),
        in_specs=[
            pl.BlockSpec(recv.shape, lambda k: (0, 0, 0, 0)),
            pl.BlockSpec((1, slots, f), lambda k: (k, 0, 0)),
            pl.BlockSpec((1, slots, f), lambda k: (k, 0, 0)),
        ],
        out_specs=pl.BlockSpec((1, 2 * d, f), lambda k: (k, 0, 0)),
        compiler_params=params(),
        name="expert_grads",
    )(recv, hid, pre_grad)
    expert_grads = expert_grads.reshape(n_ring, 2, 2 * d, f)
    moving = None
    for t in range(1, n_ring):
        mine = expert_grads[t]
        moving = mine if moving is None else (moving.astype(F32) + mine.astype(F32)).astype(BF16)
        moving = lax.ppermute(moving, "z", ring)
    summed = expert_grads[0].astype(F32)
    if moving is not None:
        summed = summed + moving.astype(F32)
    other = swap(summed[1].astype(BF16), "x").astype(F32)

    def unpiece(p):
        return p[:d], jnp.concatenate([p[d + b * f : d + (b + 1) * f] for b in range(d // f)], axis=1)

    own_up, own_down = unpiece(summed[0])
    oth_up, oth_down = unpiece(other)
    first = x_at == 0
    grad_up = jnp.where(first, jnp.stack([own_up, oth_up]), jnp.stack([oth_up, own_up]))
    grad_edown = jnp.where(first, jnp.stack([own_down, oth_down]), jnp.stack([oth_down, own_down]))

    if stacked:
        ff_out = (sds(ffw[0].shape, BF16), sds(ffw[1].shape, BF16))
        qo_out = (sds(qo[0].shape, BF16),)
    else:
        ff_out = (sds((d, ff), BF16), sds((ff, d), BF16))
        qo_out = (sds((d, 3 * d), BF16), sds((d, d), BF16))
    layer_out, after_grad, gb23, grad_route, g_in, g_down = pl.pallas_call(
        functools.partial(feed_back_kernel, layout, stacked),
        out_shape=(sds((toks, d), BF16), sds((toks, d), F32), sds((4, d), F32), sds((d, LANES), F32)) + ff_out,
        in_specs=[smem()] + [vmem()] * 9 + [anywhere()] * 2,
        out_specs=(vmem(),) * 4 + (anywhere(),) * 2,
        scratch_shapes=f_scratch + f_scratch + [pltpu.SemaphoreType.DMA((2,))],
        compiler_params=params(),
        name="feed_back",
    )(me, after, n2, layer_two, gates, gb, cols, route, cotangent, back, *ffw)

    out = pl.pallas_call(
        functools.partial(attend_back_kernel, layout, n_w, stacked),
        out_shape=(sds((toks, d), F32), sds((2, d), F32)) + qo_out,
        in_specs=[smem()] + [vmem()] * 7 + [anywhere()] * n_w,
        out_specs=(vmem(),) * 2 + (anywhere(),) * n_w,
        scratch_shapes=w_scratch
        + [pltpu.VMEM((toks, d), F32)] * 3
        + w_scratch
        + [pltpu.SemaphoreType.DMA((2,))],
        compiler_params=params(),
        name="attend_back",
    )(me, tokens, gb, cols, rows, qkv, attended, after_grad, *qo)
    grad_tokens, gb1 = out[:2]

    if stacked:
        grad_in = reduce_stack(g_in, "cyxz")
        grad_down = reduce_stack(g_down, "cxyz")
        g_qo = reduce_stack(out[2], "cyxz")
        qc = w_qkv.shape[1]
        grad_qkv, grad_out = g_qo[:, :qc], g_qo[:, qc:]
    else:
        grad_in, grad_down = reduce_whole(g_in), reduce_whole(g_down)
        grad_qkv, grad_out = reduce_whole(out[2]), reduce_whole(out[3])

    small_grad = jnp.concatenate(
        [gb1[0:1], gb23[0:2], gb1[1:2], gb23[2:4], grad_route[:, :experts].T], axis=0
    )
    small_grad = lax.psum(small_grad, AXES)
    h_at = lax.axis_index("z") * sizes["x"] + x_at
    e_at = lax.axis_index("y") * sizes["c"] + lax.axis_index("c")
    rows_dev = d // n_hid
    mine = lax.dynamic_slice_in_dim(small_grad, h_at * rows_dev, rows_dev, axis=1)
    grad_gain, grad_bias = mine[0:3].T, mine[3:6].T
    grad_router = lax.dynamic_slice_in_dim(mine, 6 + e_at * rc, rc, axis=0).T
    return (
        layer_out,
        grad_tokens,
        grad_gain,
        grad_bias,
        grad_qkv,
        grad_out,
        grad_in,
        grad_down,
        grad_router,
        grad_up,
        grad_edown,
    )


def solution(mesh):
    n_exp, n_hid = mesh.shape["expert"], mesh.shape["hidden"]
    sizes = {"y": n_exp // 2, "c": 2, "z": n_hid // 2, "x": 2}
    fine = Mesh(mesh.devices.reshape(tuple(sizes[a] for a in AXES)), AXES)
    both, exp, hid = AXES, ("y", "c"), ("z", "x")
    return jax.shard_map(
        functools.partial(local, sizes),
        mesh=fine,
        in_specs=(
            P(both, None),
            P(both, None),
            P(both, None),
            P(),
            P(hid, None),
            P(hid, None),
            P(hid, exp),
            P(hid, exp),
            P(hid, exp),
            P(hid, exp),
            P(hid, exp),
            P(exp, None, hid),
            P(exp, hid, None),
            P(both, None),
        ),
        out_specs=(
            P(both, None),
            P(both, None),
            P(hid, None),
            P(hid, None),
            P(hid, exp),
            P(hid, exp),
            P(hid, exp),
            P(hid, exp),
            P(hid, exp),
            P(exp, None, hid),
            P(exp, hid, None),
        ),
        check_vma=False,
    )
```

```python
import functools
import math

import jax
import jax.numpy as jnp
from jax import lax
from jax.experimental import pallas as pl
from jax.experimental.pallas import tpu as pltpu
from jax.sharding import Mesh, PartitionSpec as P

HEAD_DIM = 64
MAXLEN = 128
LANES = 128
EPSILON = 1e-05
FILL_SCORE = -1000000000.0
AXES = ("y", "c", "z", "x")
VMEM_BYTES = 56 * 1024 * 1024
GELU_A = math.sqrt(2.0 / math.pi)
GELU_B = 0.044715

F32 = jnp.float32
BF16 = jnp.bfloat16

NN = (((1,), (0,)), ((), ()))
NT = (((1,), (1,)), ((), ()))
TN = (((0,), (0,)), ((), ()))


def mm(a, b, dims=NN):
    return lax.dot_general(a, b, dims, preferred_element_type=F32)


def gelu(v):
    t = jnp.tanh(GELU_A * (v + GELU_B * (v * v * v)))
    return 0.5 * v * (1.0 + t)


def gelu_both(v):
    v2 = v * v
    t = jnp.tanh(GELU_A * (v + GELU_B * (v2 * v)))
    half = 0.5 * (1.0 + t)
    slope = half + 0.5 * v * (1.0 - t * t) * (GELU_A + (3.0 * GELU_A * GELU_B) * v2)
    return v * half, slope


def norm_parts(v):
    center = v - jnp.mean(v, axis=-1, keepdims=True)
    r = lax.rsqrt(jnp.mean(center * center, axis=-1, keepdims=True) + EPSILON)
    return center * r, r


def norm_back(xhat, r, gain, h):
    hg = h * gain
    inner = jnp.mean(hg * xhat, axis=-1, keepdims=True)
    dv = r * (hg - jnp.mean(hg, axis=-1, keepdims=True) - xhat * inner)
    return dv, jnp.sum(h * xhat, axis=0, keepdims=True), jnp.sum(h, axis=0, keepdims=True)


K = dict(scale=0.35, routes=60, attend=13, feed=11, probs=3, hidden=6, experts=4, experts_back=10, expert_grads=3, combine=5, feed_back=14, first=4, attend_back=9, add1=2, add2=14, sum_ff=2, sum_qkv=2, finish_ff=2, finish=2, pack=3, ring1=1, ringff=0, tie_near=1, tie_ffz=1, x_first=1, ff_a2a=1, tie_qkv=1, tie_ring3=1, tie_ring2=1, tie_ring1=1, tie_x=0, tie_ffc=1)


def cost(us):
    return pl.CostEstimate(flops=int(K["scale"] * us * 1.15e9), bytes_accessed=0, transcendentals=0)


def vmem():
    return pl.BlockSpec(memory_space=pltpu.VMEM)


class Late:
    def __init__(self, ref, buffer, sem):
        self.buffer, self.shape, self.dtype = buffer, buffer.shape, buffer.dtype
        self.copy = pltpu.make_async_copy(ref, buffer, sem)
        self.copy.start()
        self.waited = False

    def ready(self):
        if not self.waited:
            self.copy.wait()
            self.waited = True
        return self.buffer

    finish = ready

    def __getitem__(self, at):
        return self.ready()[at]


class Early:
    def __init__(self, ref, buffer, sem):
        self.buffer, self.shape, self.dtype = buffer, buffer.shape, buffer.dtype
        self.ref, self.sem = ref, sem
        self.copy = pltpu.make_async_copy(buffer, ref, sem)
        self.sent = False

    def send(self):
        self.copy.start()
        self.sent = True

    def part(self, i):
        pltpu.make_async_copy(self.buffer.at[i], self.ref.at[i], self.sem).start()
        self.sent = True

    def finish(self):
        if not self.sent:
            self.send()
        self.copy.wait()

    def __setitem__(self, at, value):
        self.buffer[at] = value


def call(kernel, name, us, out_shape, in_specs, out_specs, scratch=()):
    single = not isinstance(out_shape, list)
    outs, out_specs = ([out_shape], [out_specs]) if single else (out_shape, out_specs)
    specs = list(in_specs) + list(out_specs)

    def run(*args):
        arrays = list(args) + outs
        moving = [i for i, spec in enumerate(specs) if spec in ("late", "early")]

        def body(*refs):
            refs = list(refs)
            buffers, sems = refs[len(specs) + len(scratch) : -1], refs[-1]
            for j, i in enumerate(moving):
                kind = Late if specs[i] == "late" else Early
                refs[i] = kind(refs[i], buffers[j], sems.at[j])
            kernel(*refs[: len(specs) + len(scratch)])
            for i in moving:
                refs[i].finish()

        buffers = [pltpu.VMEM(arrays[i].shape, arrays[i].dtype) for i in moving]
        places = [anywhere() if spec in ("late", "early") else spec for spec in specs]
        results = pl.pallas_call(
            body,
            out_shape=outs,
            in_specs=places[: len(in_specs)],
            out_specs=places[len(in_specs) :],
            scratch_shapes=list(scratch) + buffers + [pltpu.SemaphoreType.DMA((max(len(moving), 1),))],
            compiler_params=pltpu.CompilerParams(vmem_limit_bytes=VMEM_BYTES),
            cost_estimate=cost(us),
            name=name,
        )(*args)
        return results[0] if single else results

    return run


def smem():
    return pl.BlockSpec(memory_space=pltpu.SMEM)


def anywhere():
    return pl.BlockSpec(memory_space=pl.ANY)


PLANE = ((0, 0), (0, 1), (1, 0), (1, 1))
OFFSETS = tuple((c, y, x) for c in (0, 1) for y, x in PLANE)


def move_pieces(sizes, me_ref, stacks, parts, sem, inward):
    at = {axis: me_ref[i] for i, axis in enumerate(AXES)}
    for (dc, dy, dx), stack in zip(OFFSETS, stacks):
        e = lax.bitwise_xor(at["y"], dy) * sizes["c"] + lax.bitwise_xor(at["c"], dc)
        x = lax.bitwise_xor(at["x"], dx)

        @pl.loop(0, sizes["z"])
        def _(dz):
            h = lax.bitwise_xor(at["z"], dz) * sizes["x"] + x
            for whole, rows, cols, first, folds in parts:
                step = rows // folds
                for i in range(folds):
                    piece = stack.at[dz, :, pl.ds(first + i * cols, cols)]
                    top = pl.multiple_of(h * rows + i * step, step)
                    if len(whole.shape) == 3:
                        block = whole.at[e, pl.ds(top, step), :]
                    elif whole.shape[1] == cols:
                        block = whole.at[pl.ds(top, step), :]
                    else:
                        block = whole.at[pl.ds(top, step), pl.ds(pl.multiple_of(e * cols, cols), cols)]
                    src, dst = (piece, block) if inward else (block, piece)
                    pltpu.make_async_copy(src, dst, sem).start()


def wait_all(ref, sem):
    pltpu.make_async_copy(ref, ref, sem).wait()


def routes_kernel(capacity, experts, len_row, task_row, table, rows_out, cols_out):
    sents = len_row.shape[1]
    tasks = table.shape[0]
    toks = rows_out.shape[1]
    f = lambda v: v.astype(F32)
    i0 = lax.broadcasted_iota(jnp.int32, (sents, sents), 0)
    i1 = lax.broadcasted_iota(jnp.int32, (sents, sents), 1)
    turn = lambda row: jnp.sum(jnp.where(i0 == i1, row, 0.0), axis=1, keepdims=True)
    len_r, task_r = f(len_row[...]), f(task_row[...])
    len_c, task_c = turn(len_r), turn(task_r)
    ends_row = jnp.sum(jnp.where(i0 <= i1, len_c, 0.0), axis=0, keepdims=True)
    ends_col = jnp.sum(jnp.where(i1 <= i0, len_r, 0.0), axis=1, keepdims=True)
    starts_row = ends_row - len_r
    starts_col = ends_col - len_c
    t0 = lax.broadcasted_iota(jnp.int32, (tasks, tasks), 0)
    t1 = lax.broadcasted_iota(jnp.int32, (tasks, tasks), 1)
    table_c = [f(table[:, c : c + 1]) for c in range(2)]
    table_r = [jnp.sum(jnp.where(t0 == t1, v, 0.0), axis=0, keepdims=True) for v in table_c]
    tok = f(lax.broadcasted_iota(jnp.int32, (toks, sents), 0))
    sent = lax.broadcasted_iota(jnp.int32, (toks, sents), 1)
    hot = (tok >= starts_row) & (tok < ends_row)
    seg_c = jnp.sum(jnp.where(hot, f(sent), 0.0), axis=1, keepdims=True)
    own = jnp.sum(jnp.where(hot, task_r, 0.0), axis=1, keepdims=True)
    thot = f(lax.broadcasted_iota(jnp.int32, (toks, tasks), 1)) == own
    pair_c = [
        jnp.sum(jnp.where(thot, table_r[c], 0.0), axis=1, keepdims=True)
        for c in range(2)
    ]
    tok = f(lax.broadcasted_iota(jnp.int32, (sents, toks), 1))
    sent = lax.broadcasted_iota(jnp.int32, (sents, toks), 0)
    hot = (tok >= starts_col) & (tok < ends_col)
    seg_r = jnp.sum(jnp.where(hot, f(sent), 0.0), axis=0, keepdims=True)
    own = jnp.sum(jnp.where(hot, task_c, 0.0), axis=0, keepdims=True)
    thot = f(lax.broadcasted_iota(jnp.int32, (tasks, toks), 0)) == own
    pair_r = [
        jnp.sum(jnp.where(thot, table_c[c], 0.0), axis=0, keepdims=True)
        for c in range(2)
    ]
    a0 = lax.broadcasted_iota(jnp.int32, (toks, toks), 0)
    a1 = lax.broadcasted_iota(jnp.int32, (toks, toks), 1)
    upper = (a0 < a1).astype(BF16)
    lower = (a1 < a0).astype(BF16)
    er = f(lax.broadcasted_iota(jnp.int32, (experts, toks), 0))
    ec = f(lax.broadcasted_iota(jnp.int32, (toks, experts), 1))
    hot_r = [(er == pair_r[c]).astype(F32) for c in range(2)]
    hot_c = [(ec == pair_c[c]).astype(F32) for c in range(2)]
    before_r = [mm(hot_r[c].astype(BF16), upper) for c in range(2)]
    before_c = [mm(lower, hot_c[c].astype(BF16)) for c in range(2)]
    before_r[1] = before_r[1] + jnp.sum(hot_r[0], axis=1, keepdims=True)
    before_c[1] = before_c[1] + jnp.sum(hot_c[0], axis=0, keepdims=True)
    place = lambda pair, rank: jnp.where(rank < capacity, pair * capacity + rank, -1.0)
    slot_r = [place(pair_r[c], jnp.sum(hot_r[c] * before_r[c], axis=0, keepdims=True)) for c in range(2)]
    slot_c = [place(pair_c[c], jnp.sum(hot_c[c] * before_c[c], axis=1, keepdims=True)) for c in range(2)]
    at = lax.broadcasted_iota(jnp.int32, rows_out.shape, 0)
    rows_out[...] = jnp.where(
        at == 0, seg_r, jnp.where(at == 1, slot_r[0], slot_r[1])
    ).astype(jnp.int32)
    at = lax.broadcasted_iota(jnp.int32, cols_out.shape, 1)
    packed = jnp.where(at == 0, seg_c, 0.0)
    for j, v in enumerate((pair_c[0], pair_c[1], slot_c[0], slot_c[1])):
        packed = jnp.where(at == j + 1, v, packed)
    cols_out[...] = packed.astype(jnp.int32)


def find_routes(lengths, task_ids, expert_table, toks, experts, capacity):
    return call(
        functools.partial(routes_kernel, capacity, experts),
        "routes",
        K["routes"],
        [jax.ShapeDtypeStruct((8, toks), jnp.int32), jax.ShapeDtypeStruct((toks, 8), jnp.int32)],
        [vmem()] * 3,
        [vmem()] * 2,
    )(lengths, task_ids, expert_table)


def pack_kernel(me_ref, qkv_ref, small_ref, out_ref, in_ref, down_ref, up_ref, edown_ref, qkv_out, ff_out, own_out, other_out):
    d, f = up_ref.shape[1:]
    x = me_ref[AXES.index("x")]
    for out, e in ((other_out, 1 - x), (own_out, x)):
        out[0:d, :] = up_ref[e].astype(BF16)
        for b in range(d // f):
            out[d + b * f : d + (b + 1) * f, :] = edown_ref[e, :, b * f : (b + 1) * f].astype(BF16)
        out.send()
    rows, cols = qkv_ref.shape
    qkv_out[:, 0:cols] = qkv_ref[...].astype(BF16)
    qkv_out[:, cols:] = small_ref[...].astype(BF16)
    qkv_out.send()
    at = 0
    for ref in (out_ref, in_ref):
        ff_out[:, at : at + ref.shape[1]] = ref[...].astype(BF16)
        at += ref.shape[1]
    cols = down_ref.shape[1]
    for i in range(down_ref.shape[0] // rows):
        ff_out[:, at + i * cols : at + (i + 1) * cols] = down_ref[i * rows : (i + 1) * rows, :].astype(BF16)


def add_kernel(a_ref, b_ref, out_ref):
    out_ref[...] = (a_ref[...].astype(F32) + b_ref[...].astype(F32)).astype(out_ref.dtype)


def sum_cores_kernel(placed, me_ref, *refs):
    n = len(PLANE)
    near, far, outs = refs[:n], refs[n : 2 * n], refs[2 * n :]
    own = near[0][...].astype(F32) + far[0][...].astype(F32)
    if placed:
        send = outs[0]
        for i, (dy, dx) in enumerate(PLANE):
            at = lax.bitwise_xor(me_ref[AXES.index("y")], dy) * 2 + lax.bitwise_xor(me_ref[AXES.index("x")], dx)
            total = own if i == 0 else near[i][...].astype(F32) + far[i][...].astype(F32)
            send[at] = total.astype(BF16)
    else:
        outs[0][...] = own
        for i in range(1, n):
            outs[i][...] = (near[i][...].astype(F32) + far[i][...].astype(F32)).astype(BF16)
            outs[i].send()


def total_of(refs):
    total = refs[0][...]
    for v in refs[1:]:
        total = total + v[...].astype(F32)
    return total


def finish_ff_kernel(n_z, *refs):
    total = total_of(refs[:n_z])
    gout_ref, gin_ref, gdown_ref, small_ref = refs[n_z:]
    at = 0
    for ref in (gout_ref, gin_ref):
        ref[...] = total[:, at : at + ref.shape[1]]
        at += ref.shape[1]
    rows, cols = total.shape[0], gdown_ref.shape[1]
    for i in range(gdown_ref.shape[0] // rows):
        gdown_ref[i * rows : (i + 1) * rows, :] = total[:, at : at + cols]
        at += cols
    small_ref[...] = total[:, at:]


def finish_kernel(n_z, route_cols, n_route, e_ref, small_ref, *refs):
    total = total_of(refs[:n_z])
    gqkv_ref, grouter_ref, ggain_ref, gbias_ref = refs[n_z:]
    cols = gqkv_ref.shape[1]
    gqkv_ref[...] = total[:, 0:cols]
    first, small = total[:, cols:].T, small_ref[...].T
    at = lax.broadcasted_iota(jnp.int32, small.shape, 0)
    pick = lambda i: jnp.sum(jnp.where(at == i, small, 0.0), axis=0, keepdims=True)
    for j in range(route_cols):
        grouter_ref[j : j + 1, :] = pick(e_ref[0] * route_cols + j)
    for ref, i in ((ggain_ref, 0), (gbias_ref, 1)):
        ref[0:1, :] = first[i : i + 1]
        ref[1:3, :] = small[n_route + 2 * i : n_route + 2 * i + 2]


def head_blocks(toks):
    n = toks // MAXLEN
    return [(i * MAXLEN, max(i - 1, 0) * MAXLEN, min(i + 2, n) * MAXLEN) for i in range(n)]


def two_heads(block, low_half):
    zero = jnp.zeros_like(block)
    return jnp.concatenate([jnp.where(low_half, block, zero), jnp.where(low_half, zero, block)], axis=0)


def pick_heads(stacked, low_half):
    n = stacked.shape[0] // 2
    return jnp.where(low_half, stacked[:n], stacked[n:])


def probabilities(q2, keys, mask):
    scores = mm(q2, keys, NT) * (1.0 / math.sqrt(HEAD_DIM))
    scores = jnp.where(mask, scores, FILL_SCORE)
    exps = jnp.exp(scores - jnp.max(scores, axis=-1, keepdims=True))
    return exps * (1.0 / jnp.sum(exps, axis=-1, keepdims=True))


def same_sentence(cols_ref, rows_ref, q0, k0, k1):
    seg = cols_ref[q0 : q0 + MAXLEN, 0:1]
    return jnp.concatenate([seg, seg], axis=0) == rows_ref[0:1, k0:k1]


def load_qkv(sizes, me_ref, refs, qkv_w, sem):
    if len(refs) == 1:
        pltpu.make_async_copy(refs[0], qkv_w, sem).start()
        return
    share = sizes["y"] * sizes["c"]
    parts = [(qkv_w, refs[0].shape[1], qkv_w.shape[1] // share, 0, 1)]
    move_pieces(sizes, me_ref, refs, parts, sem, True)


def load_ff(sizes, me_ref, refs, stacked, wholes, sems):
    if stacked:
        for i, part in enumerate(ff_parts(sizes, refs[0].shape[1], *wholes)):
            move_pieces(sizes, me_ref, refs, [part], sems.at[i], True)
    else:
        for i, (ref, whole) in enumerate(zip(refs, wholes)):
            pltpu.make_async_copy(ref, whole, sems.at[i]).start()


def ff_parts(sizes, rows, out_w, in_w, down_w):
    share = sizes["y"] * sizes["c"]
    oc, ic, dc = out_w.shape[1] // share, in_w.shape[1] // share, down_w.shape[1] // share
    folds = down_w.shape[0] // out_w.shape[0]
    return [
        (out_w, rows, oc, 0, 1),
        (in_w, rows, ic, oc, 1),
        (down_w, rows * folds, dc, oc + ic, folds),
    ]


def unpack_small(small_s, route_cols, experts_rows):
    share, d, _ = small_s.shape
    i0 = lax.broadcasted_iota(jnp.int32, (8, LANES), 0)
    i1 = lax.broadcasted_iota(jnp.int32, (8, LANES), 1)
    gb = mm((i1 == i0 + route_cols).astype(BF16), small_s[0], NT)
    route = None
    for e in range(share):
        i0 = lax.broadcasted_iota(jnp.int32, (experts_rows, LANES), 0)
        i1 = lax.broadcasted_iota(jnp.int32, (experts_rows, LANES), 1)
        pick = ((i0 - e * route_cols == i1) & (i1 < route_cols)).astype(BF16)
        part = mm(pick, small_s[e], NT)
        route = part if route is None else route + part
    return gb, route.astype(BF16)


def attend_kernel(sizes, stacked, route_cols, me_ref, tok_ref, cols_ref, rows_ref, *rest):
    if not stacked:
        gb_in, rest = rest[0], rest[1:]
    n_w = len(OFFSETS) if stacked else 1
    w_refs = rest[:n_w]
    rest = rest[n_w:]
    qkv_ref, att_ref = rest[:2]
    d = tok_ref.shape[1]
    if stacked:
        gb_ref, route_ref, qkv_w, small_s, sems = rest[2:]
        first = qkv_w.shape[1] // (sizes["y"] * sizes["c"])
        move_pieces(sizes, me_ref, w_refs, [(small_s, w_refs[0].shape[1], LANES, first, 1)], sems.at[1], True)
        load_qkv(sizes, me_ref, w_refs, qkv_w, sems.at[0])
        wait_all(small_s, sems.at[1])
        gb, route = unpack_small(small_s, route_cols, route_ref.shape[0])
        gb_ref[...] = gb
        route_ref[...] = route
    else:
        qkv_w, sems = rest[2:]
        load_qkv(sizes, me_ref, w_refs, qkv_w, sems.at[0])
        gb = gb_in[...]
    xhat, _ = norm_parts(tok_ref[...].astype(F32))
    n1 = (xhat * gb[0:1, :] + gb[3:4, :]).astype(BF16)
    wait_all(qkv_w, sems.at[0])
    for j in range(3):
        qkv_ref[:, j * d : (j + 1) * d] = mm(n1, qkv_w[:, j * d : (j + 1) * d]).astype(BF16)
    qkv_ref.send()
    qkv_ref = qkv_ref.buffer
    low_half = lax.broadcasted_iota(jnp.int32, (MAXLEN, LANES), 1) < HEAD_DIM
    for q0, k0, k1 in head_blocks(tok_ref.shape[0]):
        mask = same_sentence(cols_ref, rows_ref, q0, k0, k1)
        for p in range(d // LANES):
            at = lambda j: slice(j * d + p * LANES, j * d + (p + 1) * LANES)
            q2 = two_heads(qkv_ref[q0 : q0 + MAXLEN, at(0)], low_half)
            prob = probabilities(q2, qkv_ref[k0:k1, at(1)], mask).astype(BF16)
            out = mm(prob, qkv_ref[k0:k1, at(2)])
            att_ref[q0 : q0 + MAXLEN, at(0)] = pick_heads(out, low_half).astype(BF16)


def probs_kernel(cols_ref, rows_ref, qkv_ref, *prob_refs):
    d = qkv_ref.shape[1] // 3
    low_half = lax.broadcasted_iota(jnp.int32, (MAXLEN, LANES), 1) < HEAD_DIM
    n = len(prob_refs) // 2
    for prob_ref, (q0, k0, k1) in zip(zip(prob_refs[:n], prob_refs[n:]), head_blocks(qkv_ref.shape[0])):
        mask = same_sentence(cols_ref, rows_ref, q0, k0, k1)
        pairs = d // LANES
        for p in range(pairs):
            lanes = slice(p * LANES, (p + 1) * LANES)
            q2 = two_heads(qkv_ref[q0 : q0 + MAXLEN, lanes], low_half)
            prob = probabilities(q2, qkv_ref[k0:k1, d + p * LANES : d + (p + 1) * LANES], mask)
            prob_ref[2 * p // pairs][2 * p % pairs // 2] = prob
        for ref in prob_ref:
            ref.send()


def attend_back_blocks(pairs, prob_refs, qkv_ref, atg_ref, dq_s, dk_s, dv_s):
    toks, d = atg_ref.shape
    scale = 1.0 / math.sqrt(HEAD_DIM)
    dk_s[...] = jnp.zeros_like(dk_s)
    dv_s[...] = jnp.zeros_like(dv_s)
    low_half = lax.broadcasted_iota(jnp.int32, (MAXLEN, LANES), 1) < HEAD_DIM
    for prob_ref, (q0, k0, k1) in zip(prob_refs, head_blocks(toks)):
        for i, p in enumerate(pairs):
            at = lambda j: slice(j * d + p * LANES, j * d + (p + 1) * LANES)
            lanes = slice(i * LANES, (i + 1) * LANES)
            q2 = two_heads(qkv_ref[q0 : q0 + MAXLEN, at(0)], low_half)
            keys, values = qkv_ref[k0:k1, at(1)], qkv_ref[k0:k1, at(2)]
            prob = prob_ref[i]
            a2 = two_heads(atg_ref[q0 : q0 + MAXLEN, at(0)], low_half)
            prob_grad = mm(a2, values, NT)
            dv_s[k0:k1, lanes] += mm(prob.astype(BF16), a2, TN)
            inner = jnp.sum(prob_grad * prob, axis=-1, keepdims=True)
            score_grad = (prob * (prob_grad - inner)).astype(BF16)
            dq_s[q0 : q0 + MAXLEN, lanes] = pick_heads(mm(score_grad, keys), low_half)
            dk_s[k0:k1, lanes] += mm(score_grad, q2, TN)
    return [
        (dq_s[...] * scale).astype(BF16),
        (dk_s[...] * scale).astype(BF16),
        dv_s[...].astype(BF16),
    ]


def attend_back_first_kernel(n_prob, *refs):
    prob_refs = refs[:n_prob]
    qkv_ref, atg_ref, out_ref, dq_s, dk_s, dv_s = refs[n_prob:]
    pairs = range(out_ref.shape[2] // LANES)
    grads = attend_back_blocks(pairs, prob_refs, qkv_ref, atg_ref, dq_s, dk_s, dv_s)
    for j in range(3):
        out_ref[j] = grads[j]


def attend_back_kernel(sizes, stacked, n_prob, me_ref, tok_ref, gb_ref, *rest):
    prob_refs = rest[:n_prob]
    qkv_ref, atg_ref, ag_ref, first_ref = rest[n_prob : n_prob + 4]
    rest = rest[n_prob + 4 :]
    n_w = len(OFFSETS) if stacked else 1
    w_refs = rest[:n_w]
    gtok_ref = rest[n_w]
    g_refs = rest[n_w + 1 : -7]
    qkv_w, dq_s, dk_s, dv_s, gqkv_s, small_s, sems = rest[-7:]
    load_qkv(sizes, me_ref, w_refs, qkv_w, sems.at[0])
    d = tok_ref.shape[1]
    pairs = range(first_ref.shape[2] // LANES, d // LANES)
    grads = attend_back_blocks(pairs, prob_refs, qkv_ref, atg_ref, dq_s, dk_s, dv_s)
    grads = [jnp.concatenate([first_ref[j], grads[j]], axis=1) for j in range(3)]
    wait_all(qkv_w, sems.at[0])
    xhat, r = norm_parts(tok_ref[...].astype(F32))
    n1 = (xhat * gb_ref[0:1, :] + gb_ref[3:4, :]).astype(BF16)
    n1_grad = sum(mm(grads[j], qkv_w[:, j * d : (j + 1) * d], NT) for j in range(3))
    dv, gain, bias = norm_back(xhat, r, gb_ref[0:1, :], n1_grad)
    small_s[...] = as_columns([gain, bias]).astype(BF16)
    for j in range(3):
        gqkv_s[:, j * d : (j + 1) * d] = mm(n1, grads[j], TN).astype(BF16)
    if stacked:
        rows = g_refs[0].shape[1]
        cols = 3 * d // (sizes["y"] * sizes["c"])
        move_pieces(sizes, me_ref, g_refs, [(gqkv_s, rows, cols, 0, 1), (small_s, rows, LANES, cols, 1)], sems.at[1], False)
    else:
        for src, dst in zip((gqkv_s, small_s), g_refs):
            pltpu.make_async_copy(src, dst, sems.at[1]).start()
    gtok_ref[...] = ag_ref[...] + dv
    for ref in g_refs:
        wait_all(ref, sems.at[1])


def as_columns(rows):
    n = len(rows)
    block = jnp.concatenate(rows + [jnp.zeros((16 - n, rows[0].shape[1]), F32)], axis=0).astype(BF16)
    i0 = lax.broadcasted_iota(jnp.int32, (16, LANES), 0)
    i1 = lax.broadcasted_iota(jnp.int32, (16, LANES), 1)
    return mm(block, (i0 == i1).astype(BF16), TN)


def feed_kernel(sizes, stacked, me_ref, tok_ref, att_ref, gb_ref, cols_ref, rows_ref, route_ref, cot_ref, *rest):
    n_w = len(OFFSETS) if stacked else 3
    w_refs = rest[:n_w]
    rest = rest[n_w:]
    after_ref, two_ref, gate_ref, sendx_ref, sendg_ref = rest[:5]
    out_w, in_w, down_w, sems = rest[-4:]
    load_ff(sizes, me_ref, w_refs, stacked, (out_w, in_w, down_w), sems)
    ff = in_w.shape[1]
    toks, d = tok_ref.shape
    wait_all(out_w, sems.at[0])
    after = tok_ref[...].astype(F32) + mm(att_ref[...], out_w[...])
    after_ref[...] = after
    after_ref.send()
    xhat, _ = norm_parts(after)
    n2 = (xhat * gb_ref[1:2, :] + gb_ref[4:5, :]).astype(BF16)
    wait_all(in_w, sems.at[1])
    step = 512
    total = None
    for j in range(ff // step):
        hidden = gelu(mm(n2, in_w[:, j * step : (j + 1) * step])).astype(BF16)
        if j == 0:
            wait_all(down_w, sems.at[2])
        part = mm(hidden, down_w[j * step : (j + 1) * step, :])
        total = part if total is None else total + part
    layer_two = after + total
    two_ref[...] = layer_two
    two_ref.send()
    xhat, _ = norm_parts(layer_two)
    n3 = (xhat * gb_ref[2:3, :] + gb_ref[5:6, :]).astype(BF16)
    logits = mm(n3, route_ref[...], NT)
    lane = lax.broadcasted_iota(jnp.int32, logits.shape, 1)
    chosen = [
        jnp.sum(jnp.where(lane == cols_ref[:, c + 1 : c + 2], logits, 0.0), axis=1, keepdims=True)
        for c in range(2)
    ]
    peak = jnp.maximum(chosen[0], chosen[1])
    exps = [jnp.exp(v - peak) for v in chosen]
    gates = [v / (exps[0] + exps[1]) for v in exps]
    lane = lax.broadcasted_iota(jnp.int32, gate_ref.shape, 1)
    gate_ref[...] = jnp.where(lane == 0, gates[0], jnp.where(lane == 1, gates[1], 0.0))
    upstream = cot_ref[...].astype(F32)
    row_grads = [(gates[c] * upstream).astype(BF16) for c in range(2)]
    experts, cap, _ = sendx_ref.shape
    chunk = min(512, experts * cap)
    per = chunk // cap
    for j in range(experts * cap // chunk):
        slot = lax.broadcasted_iota(jnp.int32, (chunk, toks), 0) + j * chunk
        hot = [(slot == rows_ref[c + 1 : c + 2, :]).astype(BF16) for c in range(2)]
        at = pl.ds(j * per, per)
        shape = (per, cap, sendx_ref.shape[2])
        sendx_ref[at] = mm(hot[0] + hot[1], n3).astype(BF16).reshape(shape)
        if (j + 1) * chunk == experts * cap:
            sendx_ref.send()
        sendg_ref[at] = (mm(hot[0], row_grads[0]) + mm(hot[1], row_grads[1])).astype(BF16).reshape(shape)


def hidden_kernel(sizes, stacked, me_ref, after_ref, gb_ref, *rest):
    n_w = len(OFFSETS) if stacked else 1
    w_refs = rest[:n_w]
    hid_ref, slope_ref, in_w, sems = rest[n_w:]
    d, ff = in_w.shape
    if stacked:
        oc = d // (sizes["y"] * sizes["c"])
        parts = [(in_w, w_refs[0].shape[1], ff // (sizes["y"] * sizes["c"]), oc, 1)]
        move_pieces(sizes, me_ref, w_refs, parts, sems.at[0], True)
    else:
        pltpu.make_async_copy(w_refs[0], in_w, sems.at[0]).start()
    xhat, _ = norm_parts(after_ref[...])
    n2 = (xhat * gb_ref[1:2, :] + gb_ref[4:5, :]).astype(BF16)
    wait_all(in_w, sems.at[0])
    step = 512
    for j in range(ff // step):
        at = slice(j * step, (j + 1) * step)
        hidden, slope = gelu_both(mm(n2, in_w[:, at]))
        hid_ref[j] = hidden.astype(BF16)
        hid_ref.part(j)
        slope_ref[j] = slope
        slope_ref.part(j)


def combine_kernel(two_ref, gate_ref, gb_ref, cols_ref, cot_ref, back_ref, lout_ref, lgrad_ref, groute_ref):
    toks, d = two_ref.shape
    experts, cap, _ = back_ref.shape
    slots = experts * cap
    slot = lax.broadcasted_iota(jnp.int32, (toks, slots), 1)
    results = back_ref[...].reshape(slots, d)
    picked = [mm((slot == cols_ref[:, c + 3 : c + 4]).astype(BF16), results) for c in range(2)]
    gates = [gate_ref[:, c : c + 1] for c in range(2)]
    layer_two = two_ref[...]
    lout_ref[...] = (layer_two + gates[0] * picked[0] + gates[1] * picked[1]).astype(BF16)
    upstream = cot_ref[...].astype(F32)
    gate_grad = [jnp.sum(upstream * v, axis=1, keepdims=True) for v in picked]
    mean = gates[0] * gate_grad[0] + gates[1] * gate_grad[1]
    lane = lax.broadcasted_iota(jnp.int32, (toks, LANES), 1)
    logit_grad = sum(
        jnp.where(lane == cols_ref[:, c + 1 : c + 2], gates[c] * (gate_grad[c] - mean), 0.0) for c in range(2)
    ).astype(BF16)
    lgrad_ref[...] = logit_grad
    xhat, _ = norm_parts(layer_two)
    n3 = (xhat * gb_ref[2:3, :] + gb_ref[5:6, :]).astype(BF16)
    groute_ref[...] = mm(n3, logit_grad, TN)


def feed_back_kernel(sizes, stacked, me_ref, after_ref, two_ref, att_ref, gb_ref, cols_ref, route_ref, cot_ref, lgrad_ref, groute_ref, hid_ref, slope_ref, back_ref, *rest):
    n_w = len(OFFSETS) if stacked else 3
    w_refs = rest[:n_w]
    rest = rest[n_w:]
    ag_ref, atg_ref = rest[:2]
    g_refs = rest[2:-9]
    out_w, in_w, down_w, gout_s, gin_s, gdown_s, small_s, wait_sem, sems = rest[-9:]
    load_ff(sizes, me_ref, w_refs, stacked, (out_w, in_w, down_w), wait_sem)
    toks, d = after_ref.shape
    ff = in_w.shape[1]
    experts, cap, _ = back_ref.shape
    slots = experts * cap
    slot = lax.broadcasted_iota(jnp.int32, (toks, slots), 1)
    hot = ((slot == cols_ref[:, 3:4]) | (slot == cols_ref[:, 4:5])).astype(BF16)
    three_grad = mm(hot, back_ref[...].reshape(slots, d)) + mm(lgrad_ref[...], route_ref[...])
    xhat, r = norm_parts(two_ref[...])
    dv, gain3, bias3 = norm_back(xhat, r, gb_ref[2:3, :], three_grad)
    two_grad = cot_ref[...].astype(F32) + dv
    ffn_grad = two_grad.astype(BF16)
    xhat, r = norm_parts(after_ref[...])
    n2 = (xhat * gb_ref[1:2, :] + gb_ref[4:5, :]).astype(BF16)
    wait_all(down_w, wait_sem.at[2])
    wait_all(in_w, wait_sem.at[1])
    step = 512
    n2_grad = None
    for j in range(ff // step):
        at = slice(j * step, (j + 1) * step)
        gdown_s[at, :] = mm(hid_ref[j], ffn_grad, TN).astype(BF16)
        pre_grad = (mm(ffn_grad, down_w[at, :], NT) * slope_ref[j]).astype(BF16)
        gin_s[:, at] = mm(n2, pre_grad, TN).astype(BF16)
        part = mm(pre_grad, in_w[:, at], NT)
        n2_grad = part if n2_grad is None else n2_grad + part
    dv, gain2, bias2 = norm_back(xhat, r, gb_ref[1:2, :], n2_grad)
    after_grad = two_grad + dv
    ag_ref[...] = after_grad
    ag_ref.send()
    attn_grad = after_grad.astype(BF16)
    gout_s[...] = mm(att_ref[...], attn_grad, TN).astype(BF16)
    lanes = lax.broadcasted_iota(jnp.int32, (16, LANES), 1)
    lanes = lanes - lax.broadcasted_iota(jnp.int32, (16, LANES), 0)
    norms = jnp.concatenate([gain2, gain3, bias2, bias3, jnp.zeros((12, d), F32)], axis=0).astype(BF16)
    n_route = route_columns(sizes)
    small_s[...] = (groute_ref[...] + mm(norms, (lanes == n_route).astype(BF16), TN)).astype(BF16)
    if stacked:
        _, rows, width = g_refs[0].shape
        parts = ff_parts(sizes, rows, gout_s, gin_s, gdown_s)
        parts.append((small_s, rows, LANES, width - LANES, 1))
        move_pieces(sizes, me_ref, g_refs, parts, sems.at[0], False)
    else:
        for src, dst in zip((gout_s, gin_s, gdown_s, small_s), g_refs):
            pltpu.make_async_copy(src, dst, sems.at[0]).start()
    wait_all(out_w, wait_sem.at[0])
    atg_ref[...] = mm(attn_grad, out_w[...], NT).astype(BF16)
    for ref in g_refs:
        wait_all(ref, sems.at[0])


def route_columns(sizes):
    return sizes["y"] * sizes["c"] * sizes["x"]


def load_blocks(w_refs, w_s, sems):
    per = w_refs[0].shape[0]
    for s, ref in enumerate(w_refs):
        pltpu.make_async_copy(ref, w_s.at[pl.ds(s * per, per)], sems.at[s]).start()


def expert_forward_kernel(first, n_blocks, recv_ref, *rest):
    w_refs, rest = rest[:n_blocks], rest[n_blocks:]
    if not first:
        before_ref, rest = rest[0], rest[1:]
    out_ref, rest = rest[0], rest[1:]
    hid_refs, slope_refs = rest[:n_blocks], rest[n_blocks : 2 * n_blocks]
    w_s, acc_s, sems = rest[2 * n_blocks :]
    load_blocks(w_refs, w_s, sems)
    n_src, cap, d = recv_ref.shape
    rows = n_src * cap
    per, _, f = w_refs[0].shape
    step = min(512, rows)
    acc_s[...] = jnp.zeros_like(acc_s) if first else before_ref[...]
    for s in range(n_blocks):
        wait_all(w_s.at[pl.ds(s * per, per)], sems.at[s])

        @pl.loop(0, per)
        def _(k):
            for j in range(rows // step):
                at = slice(j * step, (j + 1) * step)
                x = recv_ref[j * step // cap : (j + 1) * step // cap].reshape(step, d)
                hidden, slope = gelu_both(mm(x, w_s[s * per + k, 0:d, :]))
                hidden = hidden.astype(BF16)
                hid_refs[s].buffer[k, at, :] = hidden
                slope_refs[s].buffer[k, at, :] = slope
                for b in range(d // f):
                    down = w_s[s * per + k, d + b * f : d + (b + 1) * f, :]
                    acc_s[at, b * f : (b + 1) * f] += mm(hidden, down)

        hid_refs[s].send()
        slope_refs[s].send()
    out_ref[...] = acc_s[...].astype(out_ref.dtype).reshape(out_ref.shape)


def expert_back_kernel(n_ring, recv_ref, *rest):
    w_refs = rest[:n_ring]
    slope_refs = rest[n_ring : 2 * n_ring]
    ret_ref = rest[2 * n_ring]
    pg_refs = rest[2 * n_ring + 1 : 3 * n_ring + 1]
    w_s, acc_s, sems = rest[3 * n_ring + 1 :]
    load_blocks(w_refs, w_s, sems)
    n_src, cap, d = recv_ref.shape
    rows = n_src * cap
    per, _, f = w_refs[0].shape
    step = min(512, rows)
    acc_s[...] = jnp.zeros_like(acc_s)
    for s in range(n_ring):
        wait_all(w_s.at[pl.ds(s * per, per)], sems.at[s])
        slopes = slope_refs[s].ready()

        @pl.loop(0, per)
        def _(k):
            for j in range(rows // step):
                at = slice(j * step, (j + 1) * step)
                g = recv_ref[j * step // cap : (j + 1) * step // cap].reshape(step, d)
                hidden_grad = None
                for b in range(d // f):
                    down = w_s[s * per + k, d + b * f : d + (b + 1) * f, :]
                    part = mm(g[:, b * f : (b + 1) * f], down, NT)
                    hidden_grad = part if hidden_grad is None else hidden_grad + part
                pre_grad = (hidden_grad * slopes[k, at, :]).astype(BF16)
                pg_refs[s].buffer[k, at, :] = pre_grad
                acc_s[at, :] += mm(pre_grad, w_s[s * per + k, 0:d, :], NT)

        pg_refs[s].send()
    ret_ref[...] = acc_s[...].astype(BF16).reshape(ret_ref.shape)


def expert_grad_kernel(n_places, x_ref, g_ref, *refs):
    hid_refs, pg_refs, out_refs = (refs[i * n_places : (i + 1) * n_places] for i in range(3))
    n_src, cap, d = x_ref.shape
    rows = n_src * cap
    per, _, f = hid_refs[0].shape
    x = x_ref[...].reshape(rows, d)
    g = g_ref[...].reshape(rows, d)
    for s in range(n_places):
        hid, pg, out = hid_refs[s].ready(), pg_refs[s].ready(), out_refs[s].buffer

        @pl.loop(0, per)
        def _(k):
            out[k, 0:d, :] = mm(x, pg[k], TN).astype(BF16)
            down = mm(hid[k], g, TN).astype(BF16)
            for b in range(d // f):
                out[k, d + b * f : d + (b + 1) * f, :] = down[:, b * f : (b + 1) * f]

        out_refs[s].send()


def local(sizes, tokens, lengths, task_ids, expert_table, norm_gain, norm_bias, w_qkv, w_out, w_in, w_down, w_router, expert_up, expert_down, cotangent):
    toks, d = tokens.shape
    local_experts, _, f = expert_up.shape
    assert local_experts == sizes["x"] == 2
    share = sizes["y"] * sizes["c"]
    n_hid = sizes["z"] * sizes["x"]
    experts = share * local_experts
    capacity = 2 * toks // experts
    slots = experts * capacity
    ff = w_in.shape[1] * share
    rc = w_router.shape[1]
    rows_dev = d // n_hid
    n_ring = sizes["z"]
    ring = [(i, (i + 1) % n_ring) for i in range(n_ring)]
    stacked = sizes["y"] == sizes["c"] == 2 and all(
        w.shape[1] % LANES == 0 for w in (w_qkv, w_out, w_in, w_down)
    )

    def after(v, *others):
        return lax.optimization_barrier((v,) + others)[0]

    def swap(v, axis, by=1):
        n = math.prod(sizes[a] for a in axis)
        return lax.ppermute(v, axis, [(i, i ^ by) for i in range(n)])

    def gather_z(piece):
        return [piece] + [swap(piece, ("z",), by) for by in range(1, n_ring)]

    def plane_swaps(stacks):
        return [swap(stacks[by], ("y", "x"), by) for by in range(1, len(PLANE))]

    def other_core(stacks):
        return [swap(t, ("c",)) for t in stacks]

    def add_core(near, far, name, placed=False):
        n, shape = len(PLANE), near[0].shape
        outs = [sds((n,) + shape, BF16)] if placed else [sds(shape, F32)] + [sds(shape, BF16)] * (n - 1)
        return call(
            functools.partial(sum_cores_kernel, placed),
            name,
            K[name],
            outs,
            [smem()] + ["late"] * (2 * n),
            [vmem()] if placed else ["early"] * n,
        )(me, *near[:n], *far)

    def add_plane(mine, got):
        total = sum((v.astype(F32) for v in got), mine)
        return total[0], total[1:].astype(BF16)

    def z_swaps(parts):
        return [swap(parts[by - 1], ("z",), by) for by in range(1, n_ring)]

    def add_z(mine, got):
        return sum((v.astype(F32) for v in got), mine)

    def exchange(v):
        return lax.all_to_all(v, ("y", "c", "x"), split_axis=0, concat_axis=0, tiled=True)

    def gather_whole(w):
        w = lax.all_gather(w.astype(BF16), ("y", "c"), axis=1, tiled=True)
        return lax.all_gather(w, ("z", "x"), axis=0, tiled=True)

    def reduce_whole(g):
        g = lax.psum_scatter(g.astype(F32), ("z", "x"), scatter_dimension=0, tiled=True)
        return lax.psum_scatter(g, ("y", "c"), scatter_dimension=1, tiled=True)

    def sds(shape, dtype):
        return jax.ShapeDtypeStruct(shape, dtype)

    dma = pltpu.SemaphoreType.DMA
    me = jnp.stack([lax.axis_index(a) for a in AXES]).astype(jnp.int32)
    x_at = lax.axis_index("x")

    def piece_of(at):
        up = lax.dynamic_index_in_dim(expert_up, at, 0, keepdims=False)
        down = lax.dynamic_index_in_dim(expert_down, at, 0, keepdims=False)
        return jnp.concatenate(
            [up] + [down[:, b * f : (b + 1) * f] for b in range(d // f)], axis=0
        ).astype(BF16)

    def routes(lengths):
        return find_routes(lengths, task_ids, expert_table, toks, experts, capacity)

    if stacked:
        folds = w_down.shape[0] // rows_dev
        widths = w_qkv.shape[1] + LANES, w_out.shape[1] + w_in.shape[1] + folds * w_down.shape[1]
        small = jnp.concatenate([w_router, norm_gain, norm_bias], axis=1)
        small = jnp.pad(small, ((0, 0), (0, LANES - small.shape[1])))
        qkv_piece, ff_piece, own, other = call(
            pack_kernel,
            "pack",
            K["pack"],
            [sds((rows_dev, w), BF16) for w in widths] + [sds((2 * d, f), BF16)] * 2,
            [smem()] + ["late"] * 7,
            ["early"] * 4,
        )(me, w_qkv, small, w_out, w_in, w_down, expert_up, expert_down)
        expert_x = swap(other, ("x",))
        qkv_z = gather_z(qkv_piece)
        mine = jnp.stack(qkv_z)
        qkv_w = [mine] + plane_swaps([mine] * len(PLANE))
        ff_z = gather_z(after(ff_piece, *qkv_z[1:]))
        rows, cols = routes(after(lengths, *qkv_z[1:], *([expert_x] if K["x_first"] else [])))
        if K["tie_near"]:
            qkv_w = [mine] + [after(t, rows) for t in qkv_w[1:]]
        qkv_w = qkv_w + other_core(qkv_w)
        blocks = [jnp.stack([own, expert_x])]
        if K["ring1"]:
            blocks[0] = after(blocks[0], *ff_z[1:])
        blocks.append(lax.ppermute(blocks[0], "z", ring))
        if K["tie_ffz"]:
            ff_z = [ff_z[0]] + [after(t, rows) for t in ff_z[1:]]
        mine = jnp.stack(ff_z)
        ffw = [mine] + plane_swaps([mine] * len(PLANE))
        tokens_in = after(tokens, rows)
        gb_in = []
    else:
        qkv_w = [gather_whole(w_qkv)]
        ffw = [gather_whole(w_out), gather_whole(w_in), gather_whole(w_down)]
        small = jnp.concatenate([w_router, norm_gain, norm_bias], axis=1)
        small = lax.all_gather(small.astype(BF16), AXES)
        route = small[:, :, :rc].reshape(share, d, rc).transpose(0, 2, 1).reshape(experts, d)
        route = jnp.pad(route, ((0, LANES - experts), (0, 0)))
        gb = small[:n_hid, :, rc:].reshape(d, 6).T.astype(F32)
        gb = jnp.pad(gb, ((0, 2), (0, 0)))
        gb_in = [gb]
        tokens_in = tokens
        rows, cols = routes(lengths)
        blocks = [jnp.stack([piece_of(x_at), swap(piece_of(1 - x_at), ("x",))])]
        blocks.append(lax.ppermute(blocks[0], "z", ring))

    out_shape = [sds((toks, 3 * d), BF16), sds((toks, d), BF16)]
    scratch = [pltpu.VMEM((d, 3 * d), BF16)]
    if stacked:
        out_shape += [sds((8, d), F32), sds((LANES, d), BF16)]
        scratch += [pltpu.VMEM((share, d, LANES), BF16)]
    out = call(
        functools.partial(attend_kernel, sizes, stacked, rc),
        "attend",
        K["attend"],
        out_shape,
        [smem()] + ["late"] * 3 + [vmem()] * len(gb_in) + [anywhere()] * len(qkv_w),
        ["early"] * 2 + [vmem()] * (len(out_shape) - 2),
        scratch + [dma((2,))],
    )(me, tokens_in, cols, rows, *gb_in, *qkv_w)
    qkv, attended = out[:2]
    if stacked:
        gb, route = out[2:]
        ffw = [ffw[0]] + [after(t, attended, *(blocks[-1:] if K["ringff"] else [])) for t in ffw[1:]]
        ffw = ffw + other_core(ffw)
    if n_ring > 2:
        blocks.append(lax.ppermute(after(blocks[-1], attended), "z", ring))

    f_scratch = [pltpu.VMEM((d, d), BF16), pltpu.VMEM((d, ff), BF16), pltpu.VMEM((ff, d), BF16)]
    after_attn, layer_two, gates, send_x, send_g = call(
        functools.partial(feed_kernel, sizes, stacked),
        "feed",
        K["feed"],
        [sds((toks, d), F32), sds((toks, d), F32), sds((toks, LANES), F32)]
        + [sds((experts, capacity, d), BF16)] * 2,
        [smem()] + ["late"] * 2 + [vmem()] + ["late"] * 4 + [anywhere()] * len(ffw),
        ["early"] * 5,
        f_scratch + [dma((3,))],
    )(me, tokens, attended, gb, cols, rows, route, cotangent, *ffw)
    while len(blocks) < n_ring:
        blocks.append(lax.ppermute(after(blocks[-1], after_attn), "z", ring))

    recv_x = exchange(send_x)
    prob_shapes = [sds((d // LANES // 2, 2 * MAXLEN, k1 - k0), F32) for _, k0, k1 in head_blocks(toks)] * 2
    probs = call(
        probs_kernel, "probs", K["probs"], prob_shapes, [vmem()] * 3, ["early"] * len(prob_shapes)
    )(cols, rows, after(qkv, after_attn))
    hidden, slope = call(
        functools.partial(hidden_kernel, sizes, stacked),
        "hidden",
        K["hidden"],
        [sds((ff // 512, toks, 512), BF16), sds((ff // 512, toks, 512), F32)],
        [smem()] + [vmem()] * 2 + [anywhere()] * (len(OFFSETS) if stacked else 1),
        ["early"] * 2,
        [pltpu.VMEM((d, ff), BF16), dma((1,))],
    )(me, after_attn, gb, *(ffw if stacked else ffw[1:2]))
    recv_g = exchange(after(send_g, recv_x, probs[0], hidden))
    block = [sds((2, slots, f), BF16)]
    slope_block = [sds((2, slots, f), F32)]
    e_scratch = [pltpu.VMEM((2 * n_ring, 2 * d, f), BF16), pltpu.VMEM((slots, d), F32), dma((n_ring,))]
    n_first = n_ring - 1

    def expert_forward(x, w, *before):
        n = len(w)
        return call(
            functools.partial(expert_forward_kernel, not before, n),
            "experts",
            K["experts"] * n,
            [sds(recv_x.shape, BF16) if before else sds((slots, d), F32)] + block * n + slope_block * n,
            [vmem()] + [anywhere()] * n + [vmem()] * len(before),
            [vmem()] + ["early"] * (2 * n),
            e_scratch,
        )(x, *w, *before)

    out = expert_forward(recv_x, blocks[:n_first])
    hids, slopes = out[1 : 1 + n_first], out[1 + n_first :]
    out = expert_forward(recv_x, [after(blocks[n_first], out[0])], out[0])
    hids, slopes = hids + out[1:2], slopes + out[2:]
    back_x = exchange(after(out[0], recv_g))
    out = call(
        functools.partial(expert_back_kernel, n_ring),
        "experts_back",
        K["experts_back"],
        [sds(recv_g.shape, BF16)] + block * n_ring,
        [vmem()] + [anywhere()] * n_ring + ["late"] * n_ring,
        [vmem()] + ["early"] * n_ring,
        e_scratch,
    )(recv_g, *blocks, *slopes)
    pre_grads = out[1:]
    back_g = exchange(after(out[0], back_x))

    def expert_grads(places, x):
        n = len(places)
        return call(
            functools.partial(expert_grad_kernel, n),
            "expert_grads",
            K["expert_grads"] * n,
            [sds((2, 2 * d, f), BF16)] * n,
            ["late"] * (2 + 2 * n),
            ["early"] * n,
        )(x, recv_g, *[hids[s] for s in places], *[pre_grads[s] for s in places])

    far_grads = expert_grads([1], recv_x)
    moving = lax.ppermute(far_grads[0], "z", ring)
    rest = expert_grads([s % n_ring for s in range(2, n_ring + 1)], after(recv_x, far_grads[0]))

    layer_out, logit_grad, grad_route = call(
        combine_kernel,
        "combine",
        K["combine"],
        [sds((toks, d), BF16), sds((toks, LANES), BF16), sds((d, LANES), F32)],
        ["late", "late", vmem(), "late", "late", "late"],
        ["early"] * 3,
    )(layer_two, gates, gb, cols, cotangent, after(back_x, *rest))

    if stacked:
        ff_cols, qkv_cols = ffw[0].shape[-1] + LANES, qkv_w[0].shape[-1]
        ff_out = [sds((n_ring, rows_dev, ff_cols), BF16)] * len(OFFSETS)
        qkv_out = [sds((n_ring, rows_dev, qkv_cols), BF16)] * len(OFFSETS)
    else:
        ff_out = [sds((d, d), BF16), sds((d, ff), BF16), sds((ff, d), BF16), sds((d, LANES), BF16)]
        qkv_out = [sds((d, 3 * d), BF16), sds((d, LANES), BF16)]
    out = call(
        functools.partial(feed_back_kernel, sizes, stacked),
        "feed_back",
        K["feed_back"],
        [sds((toks, d), F32), sds((toks, d), BF16)] + ff_out,
        [smem()] + ["late"] * 3 + [vmem()] + ["late"] * 8 + [anywhere()] * len(ffw),
        ["early"] * 2 + [anywhere()] * len(ff_out),
        f_scratch + f_scratch + [pltpu.VMEM((d, LANES), BF16), dma((3,)), dma((1,))],
    )(me, after_attn, layer_two, attended, gb, cols, route, cotangent, after(logit_grad, layer_out), grad_route, hidden, slope, back_g, *ffw)
    after_grad, att_grad = out[:2]
    ff_grads = out[2:]
    step = n_ring - 2

    def add_on(moving, mine, weight):
        return call(add_kernel, "add", weight, sds(mine.shape, BF16), [vmem()] * 2, vmem())(moving, mine)

    for t in range(step - 1):
        if K["tie_ring1"]:
            moving = after(moving, after_grad)
        moving = lax.ppermute(add_on(moving, rest[t], K["add1"]), "z", ring)
    if stacked:
        ff_far = other_core(ff_grads[len(PLANE) :])
    half = d // 2
    n_prob = len(probs) // 2
    acc = [pltpu.VMEM((toks, half), F32)] * 3
    first_half = call(
        functools.partial(attend_back_first_kernel, n_prob),
        "attend_back_first",
        K["first"],
        [sds((3, toks, half), BF16)],
        ["late"] * (2 + n_prob),
        [vmem()],
        acc,
    )(*probs[:n_prob], qkv, att_grad)[0]
    if stacked:
        if K["tie_ffc"]:
            ff_far = [after(v, first_half) for v in ff_far]
        ff_sums = add_core(ff_grads, ff_far, "sum_ff", K["ff_a2a"])
        if K["ff_a2a"]:
            ff_got = [lax.all_to_all(ff_sums[0], ("y", "x"), split_axis=0, concat_axis=0, tiled=True)]
        else:
            ff_got = plane_swaps(ff_sums)
        att_grad = after(att_grad, ff_sums[0])
    else:
        att_grad = after(att_grad, first_half)
    out = call(
        functools.partial(attend_back_kernel, sizes, stacked, n_prob),
        "attend_back",
        K["attend_back"],
        [sds((toks, d), F32)] + qkv_out,
        [smem(), "late", vmem()] + ["late"] * (4 + n_prob) + [anywhere()] * len(qkv_w),
        ["early"] + [anywhere()] * len(qkv_out),
        [pltpu.VMEM((d, 3 * d), BF16)]
        + acc
        + [pltpu.VMEM((d, 3 * d), BF16), pltpu.VMEM((d, LANES), BF16), dma((2,))],
    )(me, tokens, gb, *probs[n_prob:], qkv, att_grad, after_grad, first_half, *qkv_w)
    grad_tokens = out[0]
    qkv_grads = out[1:]

    e_at = lax.axis_index("y") * sizes["c"] + lax.axis_index("c")
    if step:
        if K["tie_ring2"]:
            moving = after(moving, grad_tokens)
        moving = lax.ppermute(add_on(moving, rest[step - 1], K["add2"]), "z", ring)
    if stacked:
        qkv_sums = add_core(qkv_grads, other_core(qkv_grads[len(PLANE) :]), "sum_qkv")
        qkv_got = plane_swaps(qkv_sums)
        if K["tie_qkv"]:
            qkv_got = [after(v, *ff_got) for v in qkv_got]
        if K["tie_ring3"] == 1:
            moving = after(moving, *qkv_got)
        if K["ff_a2a"]:
            ff_mine, ff_parts_z = add_plane(0.0, [ff_got[0][i] for i in range(len(PLANE))])
        else:
            ff_mine, ff_parts_z = add_plane(ff_sums[0], ff_got)
        ff_got = z_swaps(ff_parts_z)
        grad_out, grad_in, grad_down, small_ff = call(
            functools.partial(finish_ff_kernel, n_ring),
            "finish_ff",
            K["finish_ff"],
            [sds(v.shape, F32) for v in (w_out, w_in, w_down)] + [sds((rows_dev, LANES), F32)],
            [vmem()] * n_ring,
            [vmem()] * 4,
        )(ff_mine, *ff_got)
        qkv_mine, qkv_parts_z = add_plane(qkv_sums[0], qkv_got)
        qkv_got = z_swaps(qkv_parts_z)
        if K["tie_ring3"] == 2:
            moving = after(moving, small_ff)
    summed = moving.astype(F32) + rest[-1].astype(F32)
    other = swap(summed[1].astype(BF16), ("x",))
    if stacked and K["tie_x"] == 1:
        qkv_got = [after(v, other) for v in qkv_got]
    if stacked and K["tie_x"] == 2:
        other = after(other, *qkv_got)
    other = other.astype(F32)
    mine = summed[0]

    def unpiece(p):
        return p[:d], jnp.concatenate([p[d + b * f : d + (b + 1) * f] for b in range(d // f)], axis=1)

    own_up, own_down = unpiece(mine)
    oth_up, oth_down = unpiece(other)
    first = x_at == 0
    grad_up = jnp.where(first, jnp.stack([own_up, oth_up]), jnp.stack([oth_up, own_up]))
    grad_edown = jnp.where(first, jnp.stack([own_down, oth_down]), jnp.stack([oth_down, own_down]))

    if stacked:
        shapes = [w_qkv, w_router, norm_gain, norm_bias]
        grad_qkv, grad_router, grad_gain, grad_bias = call(
            functools.partial(finish_kernel, n_ring, rc, route_columns(sizes)),
            "finish",
            K["finish"],
            [sds(w_qkv.shape, F32)] + [sds(v.shape[::-1], F32) for v in shapes[1:]],
            [smem()] + [vmem()] * (1 + n_ring),
            [vmem()] * len(shapes),
        )(e_at.reshape(1).astype(jnp.int32), small_ff, qkv_mine, *qkv_got)
        grad_router, grad_gain, grad_bias = grad_router.T, grad_gain.T, grad_bias.T
    else:
        grad_out, grad_in, grad_down = (reduce_whole(g) for g in ff_grads[:3])
        grad_qkv = reduce_whole(qkv_grads[0])
        small_ff, small_qkv = (
            lax.psum(lax.psum_scatter(g.astype(F32), ("z", "x"), scatter_dimension=0, tiled=True), ("y", "c"))
            for g in (ff_grads[3], qkv_grads[1])
        )
        grad_router = lax.dynamic_slice_in_dim(small_ff, e_at * rc, rc, axis=1)
        n_route = route_columns(sizes)
        gains, biases = small_ff[:, n_route : n_route + 2], small_ff[:, n_route + 2 : n_route + 4]
        grad_gain = jnp.concatenate([small_qkv[:, 0:1], gains], axis=1)
        grad_bias = jnp.concatenate([small_qkv[:, 1:2], biases], axis=1)
    return (
        layer_out,
        grad_tokens,
        grad_gain,
        grad_bias,
        grad_qkv,
        grad_out,
        grad_in,
        grad_down,
        grad_router,
        grad_up,
        grad_edown,
    )


def solution(mesh):
    n_exp, n_hid = mesh.shape["expert"], mesh.shape["hidden"]
    sizes = {"y": n_exp // 2, "c": 2, "z": n_hid // 2, "x": 2}
    fine = Mesh(mesh.devices.reshape(tuple(sizes[a] for a in AXES)), AXES)
    both, exp, hid = AXES, ("y", "c"), ("z", "x")
    return jax.shard_map(
        functools.partial(local, sizes),
        mesh=fine,
        in_specs=(
            P(both, None),
            P(both, None),
            P(both, None),
            P(),
            P(hid, None),
            P(hid, None),
            P(hid, exp),
            P(hid, exp),
            P(hid, exp),
            P(hid, exp),
            P(hid, exp),
            P(exp, None, hid),
            P(exp, hid, None),
            P(both, None),
        ),
        out_specs=(
            P(both, None),
            P(both, None),
            P(hid, None),
            P(hid, None),
            P(hid, exp),
            P(hid, exp),
            P(hid, exp),
            P(hid, exp),
            P(hid, exp),
            P(exp, None, hid),
            P(exp, hid, None),
        ),
        check_vma=False,
    )
```

```python
import functools
import math

import jax
import jax.numpy as jnp
from jax import lax
from jax.experimental import pallas as pl
from jax.experimental.pallas import tpu as pltpu
from jax.sharding import Mesh, PartitionSpec as P

HEAD_DIM = 64
MAXLEN = 128
LANES = 128
EPSILON = 1e-05
FILL_SCORE = -1000000000.0
AXES = ("y", "c", "z", "x")
VMEM_BYTES = 56 * 1024 * 1024
GELU_A = math.sqrt(2.0 / math.pi)
GELU_B = 0.044715

F32 = jnp.float32
BF16 = jnp.bfloat16

NN = (((1,), (0,)), ((), ()))
NT = (((1,), (1,)), ((), ()))
TN = (((0,), (0,)), ((), ()))


def mm(a, b, dims=NN):
    return lax.dot_general(a, b, dims, preferred_element_type=F32)


def gelu(v):
    t = jnp.tanh(GELU_A * (v + GELU_B * (v * v * v)))
    return 0.5 * v * (1.0 + t)


def gelu_both(v):
    v2 = v * v
    t = jnp.tanh(GELU_A * (v + GELU_B * (v2 * v)))
    half = 0.5 * (1.0 + t)
    slope = half + 0.5 * v * (1.0 - t * t) * (GELU_A + (3.0 * GELU_A * GELU_B) * v2)
    return v * half, slope


def norm_parts(v):
    center = v - jnp.mean(v, axis=-1, keepdims=True)
    r = lax.rsqrt(jnp.mean(center * center, axis=-1, keepdims=True) + EPSILON)
    return center * r, r


def norm_back(xhat, r, gain, h):
    hg = h * gain
    inner = jnp.mean(hg * xhat, axis=-1, keepdims=True)
    dv = r * (hg - jnp.mean(hg, axis=-1, keepdims=True) - xhat * inner)
    return dv, jnp.sum(h * xhat, axis=0, keepdims=True), jnp.sum(h, axis=0, keepdims=True)


K = dict(scale=0.35, routes=60, attend=9, feed=11, probs=3, hidden=6, experts=18, expert_grads=3, feed_back=20, first=4, attend_back=9, add1=2, add2=14, sum_ff=2, sum_qkv=3, finish=2, pack=3, ring1=1, ringff=0, tie_near=1, tie_ffz=1, x_first=0, ff_a2a=1, tie_qkv=1, tie_ring3=1, tie_ring2=1, tie_ring1=1, tie_x=0, tie_ffc=1)


def cost(us):
    return pl.CostEstimate(flops=int(K["scale"] * us * 1.15e9), bytes_accessed=0, transcendentals=0)


def vmem():
    return pl.BlockSpec(memory_space=pltpu.VMEM)


class Late:
    def __init__(self, ref, buffer, sem):
        self.buffer, self.shape, self.dtype = buffer, buffer.shape, buffer.dtype
        self.copy = pltpu.make_async_copy(ref, buffer, sem)
        self.copy.start()
        self.waited = False

    def ready(self):
        if not self.waited:
            self.copy.wait()
            self.waited = True
        return self.buffer

    finish = ready

    def __getitem__(self, at):
        return self.ready()[at]


class Early:
    def __init__(self, ref, buffer, sem):
        self.buffer, self.shape, self.dtype = buffer, buffer.shape, buffer.dtype
        self.ref, self.sem = ref, sem
        self.copy = pltpu.make_async_copy(buffer, ref, sem)
        self.sent = False

    def send(self):
        self.copy.start()
        self.sent = True

    def part(self, i):
        pltpu.make_async_copy(self.buffer.at[i], self.ref.at[i], self.sem).start()
        self.sent = True

    def finish(self):
        if not self.sent:
            self.send()
        self.copy.wait()

    def __setitem__(self, at, value):
        self.buffer[at] = value


def call(kernel, name, us, out_shape, in_specs, out_specs, scratch=()):
    single = not isinstance(out_shape, list)
    outs, out_specs = ([out_shape], [out_specs]) if single else (out_shape, out_specs)
    specs = list(in_specs) + list(out_specs)

    def run(*args):
        arrays = list(args) + outs
        moving = [i for i, spec in enumerate(specs) if spec in ("late", "early")]

        def body(*refs):
            refs = list(refs)
            buffers, sems = refs[len(specs) + len(scratch) : -1], refs[-1]
            for j, i in enumerate(moving):
                kind = Late if specs[i] == "late" else Early
                refs[i] = kind(refs[i], buffers[j], sems.at[j])
            kernel(*refs[: len(specs) + len(scratch)])
            for i in moving:
                refs[i].finish()

        buffers = [pltpu.VMEM(arrays[i].shape, arrays[i].dtype) for i in moving]
        places = [anywhere() if spec in ("late", "early") else spec for spec in specs]
        results = pl.pallas_call(
            body,
            out_shape=outs,
            in_specs=places[: len(in_specs)],
            out_specs=places[len(in_specs) :],
            scratch_shapes=list(scratch) + buffers + [pltpu.SemaphoreType.DMA((max(len(moving), 1),))],
            compiler_params=pltpu.CompilerParams(vmem_limit_bytes=VMEM_BYTES),
            cost_estimate=cost(us),
            name=name,
        )(*args)
        return results[0] if single else results

    return run


def smem():
    return pl.BlockSpec(memory_space=pltpu.SMEM)


def anywhere():
    return pl.BlockSpec(memory_space=pl.ANY)


PLANE = ((0, 0), (0, 1), (1, 0), (1, 1))
OFFSETS = tuple((c, y, x) for c in (0, 1) for y, x in PLANE)


def move_pieces(sizes, me_ref, stacks, parts, sem, inward):
    at = {axis: me_ref[i] for i, axis in enumerate(AXES)}
    for (dc, dy, dx), stack in zip(OFFSETS, stacks):
        e = lax.bitwise_xor(at["y"], dy) * sizes["c"] + lax.bitwise_xor(at["c"], dc)
        x = lax.bitwise_xor(at["x"], dx)

        @pl.loop(0, sizes["z"])
        def _(dz):
            h = lax.bitwise_xor(at["z"], dz) * sizes["x"] + x
            for whole, rows, cols, first, folds in parts:
                step = rows // folds
                for i in range(folds):
                    piece = stack.at[dz, :, pl.ds(first + i * cols, cols)]
                    top = pl.multiple_of(h * rows + i * step, step)
                    if len(whole.shape) == 3:
                        block = whole.at[e, pl.ds(top, step), :]
                    elif whole.shape[1] == cols:
                        block = whole.at[pl.ds(top, step), :]
                    else:
                        block = whole.at[pl.ds(top, step), pl.ds(pl.multiple_of(e * cols, cols), cols)]
                    src, dst = (piece, block) if inward else (block, piece)
                    pltpu.make_async_copy(src, dst, sem).start()


def wait_all(ref, sem):
    pltpu.make_async_copy(ref, ref, sem).wait()


def routes_kernel(capacity, experts, len_row, task_row, table, rows_out, cols_out):
    sents = len_row.shape[1]
    tasks = table.shape[0]
    toks = rows_out.shape[1]
    f = lambda v: v.astype(F32)
    i0 = lax.broadcasted_iota(jnp.int32, (sents, sents), 0)
    i1 = lax.broadcasted_iota(jnp.int32, (sents, sents), 1)
    turn = lambda row: jnp.sum(jnp.where(i0 == i1, row, 0.0), axis=1, keepdims=True)
    len_r, task_r = f(len_row[...]), f(task_row[...])
    len_c, task_c = turn(len_r), turn(task_r)
    ends_row = jnp.sum(jnp.where(i0 <= i1, len_c, 0.0), axis=0, keepdims=True)
    ends_col = jnp.sum(jnp.where(i1 <= i0, len_r, 0.0), axis=1, keepdims=True)
    starts_row = ends_row - len_r
    starts_col = ends_col - len_c
    t0 = lax.broadcasted_iota(jnp.int32, (tasks, tasks), 0)
    t1 = lax.broadcasted_iota(jnp.int32, (tasks, tasks), 1)
    table_c = [f(table[:, c : c + 1]) for c in range(2)]
    table_r = [jnp.sum(jnp.where(t0 == t1, v, 0.0), axis=0, keepdims=True) for v in table_c]
    tok = f(lax.broadcasted_iota(jnp.int32, (toks, sents), 0))
    sent = lax.broadcasted_iota(jnp.int32, (toks, sents), 1)
    hot = (tok >= starts_row) & (tok < ends_row)
    seg_c = jnp.sum(jnp.where(hot, f(sent), 0.0), axis=1, keepdims=True)
    own = jnp.sum(jnp.where(hot, task_r, 0.0), axis=1, keepdims=True)
    thot = f(lax.broadcasted_iota(jnp.int32, (toks, tasks), 1)) == own
    pair_c = [
        jnp.sum(jnp.where(thot, table_r[c], 0.0), axis=1, keepdims=True)
        for c in range(2)
    ]
    tok = f(lax.broadcasted_iota(jnp.int32, (sents, toks), 1))
    sent = lax.broadcasted_iota(jnp.int32, (sents, toks), 0)
    hot = (tok >= starts_col) & (tok < ends_col)
    seg_r = jnp.sum(jnp.where(hot, f(sent), 0.0), axis=0, keepdims=True)
    own = jnp.sum(jnp.where(hot, task_c, 0.0), axis=0, keepdims=True)
    thot = f(lax.broadcasted_iota(jnp.int32, (tasks, toks), 0)) == own
    pair_r = [
        jnp.sum(jnp.where(thot, table_c[c], 0.0), axis=0, keepdims=True)
        for c in range(2)
    ]
    a0 = lax.broadcasted_iota(jnp.int32, (toks, toks), 0)
    a1 = lax.broadcasted_iota(jnp.int32, (toks, toks), 1)
    upper = (a0 < a1).astype(BF16)
    lower = (a1 < a0).astype(BF16)
    er = f(lax.broadcasted_iota(jnp.int32, (experts, toks), 0))
    ec = f(lax.broadcasted_iota(jnp.int32, (toks, experts), 1))
    hot_r = [(er == pair_r[c]).astype(F32) for c in range(2)]
    hot_c = [(ec == pair_c[c]).astype(F32) for c in range(2)]
    before_r = [mm(hot_r[c].astype(BF16), upper) for c in range(2)]
    before_c = [mm(lower, hot_c[c].astype(BF16)) for c in range(2)]
    before_r[1] = before_r[1] + jnp.sum(hot_r[0], axis=1, keepdims=True)
    before_c[1] = before_c[1] + jnp.sum(hot_c[0], axis=0, keepdims=True)
    place = lambda pair, rank: jnp.where(rank < capacity, pair * capacity + rank, -1.0)
    slot_r = [place(pair_r[c], jnp.sum(hot_r[c] * before_r[c], axis=0, keepdims=True)) for c in range(2)]
    slot_c = [place(pair_c[c], jnp.sum(hot_c[c] * before_c[c], axis=1, keepdims=True)) for c in range(2)]
    at = lax.broadcasted_iota(jnp.int32, rows_out.shape, 0)
    rows_out[...] = jnp.where(
        at == 0, seg_r, jnp.where(at == 1, slot_r[0], slot_r[1])
    ).astype(jnp.int32)
    at = lax.broadcasted_iota(jnp.int32, cols_out.shape, 1)
    packed = jnp.where(at == 0, seg_c, 0.0)
    for j, v in enumerate((pair_c[0], pair_c[1], slot_c[0], slot_c[1])):
        packed = jnp.where(at == j + 1, v, packed)
    cols_out[...] = packed.astype(jnp.int32)


def find_routes(lengths, task_ids, expert_table, toks, experts, capacity):
    return call(
        functools.partial(routes_kernel, capacity, experts),
        "routes",
        K["routes"],
        [jax.ShapeDtypeStruct((8, toks), jnp.int32), jax.ShapeDtypeStruct((toks, 8), jnp.int32)],
        [vmem()] * 3,
        [vmem()] * 2,
    )(lengths, task_ids, expert_table)


def pack_kernel(me_ref, out_ref, in_ref, down_ref, up_ref, edown_ref, ff_out, own_out, other_out):
    d, f = up_ref.shape[1:]
    x = me_ref[AXES.index("x")]
    for out, e in ((other_out, 1 - x), (own_out, x)):
        out[0:d, :] = up_ref[e].astype(BF16)
        for b in range(d // f):
            out[d + b * f : d + (b + 1) * f, :] = edown_ref[e, :, b * f : (b + 1) * f].astype(BF16)
        out.send()
    rows, at = out_ref.shape[0], 0
    for ref in (out_ref, in_ref):
        ff_out[:, at : at + ref.shape[1]] = ref[...].astype(BF16)
        at += ref.shape[1]
    cols = down_ref.shape[1]
    for i in range(down_ref.shape[0] // rows):
        ff_out[:, at + i * cols : at + (i + 1) * cols] = down_ref[i * rows : (i + 1) * rows, :].astype(BF16)


def add_kernel(a_ref, b_ref, out_ref, a_s, b_s, out_s, sems):
    n = a_s.shape[0]
    parts = a_ref.shape[0]
    rows = a_ref.shape[1] // (n // parts)
    at = [(i // (n // parts), pl.ds(i % (n // parts) * rows, rows)) for i in range(n)]
    gets = []
    for i, (p, row) in enumerate(at):
        gets.append([pltpu.make_async_copy(ref.at[p, row, :], s.at[i], sems.at[j, i]) for j, (ref, s) in enumerate(((a_ref, a_s), (b_ref, b_s)))])
        for copy in gets[-1]:
            copy.start()
    puts = []
    for i, (p, row) in enumerate(at):
        for copy in gets[i]:
            copy.wait()
        out_s[i] = (a_s[i].astype(F32) + b_s[i].astype(F32)).astype(out_s.dtype)
        puts.append(pltpu.make_async_copy(out_s.at[i], out_ref.at[p, row, :], sems.at[2, i]))
        puts[-1].start()
    for copy in puts:
        copy.wait()


def sum_cores_kernel(placed, me_ref, *refs):
    n = len(PLANE)
    near, far, outs = refs[:n], refs[n : 2 * n], refs[2 * n :]
    if placed:
        send_ref, send_s, sems = outs
        puts = []
        for i, (dy, dx) in enumerate(PLANE):
            at = lax.bitwise_xor(me_ref[AXES.index("y")], dy) * 2 + lax.bitwise_xor(me_ref[AXES.index("x")], dx)
            send_s[i] = (near[i][...].astype(F32) + far[i][...].astype(F32)).astype(BF16)
            puts.append(pltpu.make_async_copy(send_s.at[i], send_ref.at[at], sems.at[i]))
            puts[-1].start()
        for copy in puts:
            copy.wait()
    else:
        for i in range(1, n):
            outs[i][...] = (near[i][...].astype(F32) + far[i][...].astype(F32)).astype(BF16)
            outs[i].send()
        outs[0][...] = near[0][...].astype(F32) + far[0][...].astype(F32)


def total_of(refs):
    total = refs[0][...]
    for v in refs[1:]:
        total = total + v[...].astype(F32)
    return total


def finish_kernel(n_z, route_cols, n_route, e_ref, *refs):
    gout_ref, gin_ref, gdown_ref, gqkv_ref, grouter_ref, ggain_ref, gbias_ref = refs[2 * n_z :]
    total = total_of(refs[:n_z])
    at = 0
    for ref in (gout_ref, gin_ref):
        ref[...] = total[:, at : at + ref.shape[1]]
        at += ref.shape[1]
    rows, cols = total.shape[0], gdown_ref.shape[1]
    for i in range(gdown_ref.shape[0] // rows):
        gdown_ref[i * rows : (i + 1) * rows, :] = total[:, at : at + cols]
        at += cols
    small = total[:, at:].T
    total = total_of(refs[n_z : 2 * n_z])
    cols = gqkv_ref.shape[1]
    gqkv_ref[...] = total[:, 0:cols]
    first = total[:, cols:].T
    at = lax.broadcasted_iota(jnp.int32, small.shape, 0)
    pick = lambda i: jnp.sum(jnp.where(at == i, small, 0.0), axis=0, keepdims=True)
    for j in range(route_cols):
        grouter_ref[j : j + 1, :] = pick(e_ref[0] * route_cols + j)
    for ref, i in ((ggain_ref, 0), (gbias_ref, 1)):
        ref[0:1, :] = first[i : i + 1]
        ref[1:3, :] = small[n_route + 2 * i : n_route + 2 * i + 2]


def head_blocks(toks):
    n = toks // MAXLEN
    return [(i * MAXLEN, max(i - 1, 0) * MAXLEN, min(i + 2, n) * MAXLEN) for i in range(n)]


def two_heads(block, low_half):
    zero = jnp.zeros_like(block)
    return jnp.concatenate([jnp.where(low_half, block, zero), jnp.where(low_half, zero, block)], axis=0)


def pick_heads(stacked, low_half):
    n = stacked.shape[0] // 2
    return jnp.where(low_half, stacked[:n], stacked[n:])


def probabilities(q2, keys, mask):
    scores = mm(q2, keys, NT) * (1.0 / math.sqrt(HEAD_DIM))
    scores = jnp.where(mask, scores, FILL_SCORE)
    exps = jnp.exp(scores - jnp.max(scores, axis=-1, keepdims=True))
    return exps * (1.0 / jnp.sum(exps, axis=-1, keepdims=True))


def same_sentence(cols_ref, rows_ref, q0, k0, k1):
    seg = cols_ref[q0 : q0 + MAXLEN, 0:1]
    return jnp.concatenate([seg, seg], axis=0) == rows_ref[0:1, k0:k1]


def load_qkv(sizes, me_ref, refs, qkv_w, sem):
    if len(refs) == 1:
        pltpu.make_async_copy(refs[0], qkv_w, sem).start()
        return
    share = sizes["y"] * sizes["c"]
    parts = [(qkv_w, refs[0].shape[1], qkv_w.shape[1] // share, 0, 1)]
    move_pieces(sizes, me_ref, refs, parts, sem, True)


def load_ff(sizes, me_ref, refs, stacked, wholes, sems):
    if stacked:
        for i, part in enumerate(ff_parts(sizes, refs[0].shape[1], *wholes)):
            move_pieces(sizes, me_ref, refs, [part], sems.at[i], True)
    else:
        for i, (ref, whole) in enumerate(zip(refs, wholes)):
            pltpu.make_async_copy(ref, whole, sems.at[i]).start()


def ff_parts(sizes, rows, out_w, in_w, down_w):
    share = sizes["y"] * sizes["c"]
    oc, ic, dc = out_w.shape[1] // share, in_w.shape[1] // share, down_w.shape[1] // share
    folds = down_w.shape[0] // out_w.shape[0]
    return [
        (out_w, rows, oc, 0, 1),
        (in_w, rows, ic, oc, 1),
        (down_w, rows * folds, dc, oc + ic, folds),
    ]


def unpack_small(small_s, route_cols, experts_rows):
    share, d, _ = small_s.shape
    i0 = lax.broadcasted_iota(jnp.int32, (8, LANES), 0)
    i1 = lax.broadcasted_iota(jnp.int32, (8, LANES), 1)
    gb = mm((i1 == i0 + route_cols).astype(BF16), small_s[0], NT)
    route = None
    for e in range(share):
        i0 = lax.broadcasted_iota(jnp.int32, (experts_rows, LANES), 0)
        i1 = lax.broadcasted_iota(jnp.int32, (experts_rows, LANES), 1)
        pick = ((i0 - e * route_cols == i1) & (i1 < route_cols)).astype(BF16)
        part = mm(pick, small_s[e], NT)
        route = part if route is None else route + part
    return gb, route.astype(BF16)


def attend_kernel(sizes, stacked, route_cols, me_ref, tok_ref, cols_ref, rows_ref, *rest):
    if not stacked:
        gb_in, rest = rest[0], rest[1:]
    n_w = len(OFFSETS) if stacked else 1
    w_refs = rest[:n_w]
    rest = rest[n_w:]
    qkv_ref, att_ref = rest[:2]
    d = tok_ref.shape[1]
    if stacked:
        gb_ref, route_ref, qkv_w, small_s, sems = rest[2:]
        first = qkv_w.shape[1] // (sizes["y"] * sizes["c"])
        move_pieces(sizes, me_ref, w_refs, [(small_s, w_refs[0].shape[1], LANES, first, 1)], sems.at[1], True)
        load_qkv(sizes, me_ref, w_refs, qkv_w, sems.at[0])
        wait_all(small_s, sems.at[1])
        gb, route = unpack_small(small_s, route_cols, route_ref.shape[0])
        gb_ref[...] = gb
        route_ref[...] = route
    else:
        qkv_w, sems = rest[2:]
        load_qkv(sizes, me_ref, w_refs, qkv_w, sems.at[0])
        gb = gb_in[...]
    xhat, _ = norm_parts(tok_ref[...].astype(F32))
    n1 = (xhat * gb[0:1, :] + gb[3:4, :]).astype(BF16)
    wait_all(qkv_w, sems.at[0])
    for j in range(3):
        qkv_ref[:, j * d : (j + 1) * d] = mm(n1, qkv_w[:, j * d : (j + 1) * d]).astype(BF16)
    qkv_ref.send()
    qkv_ref = qkv_ref.buffer
    low_half = lax.broadcasted_iota(jnp.int32, (MAXLEN, LANES), 1) < HEAD_DIM
    for q0, k0, k1 in head_blocks(tok_ref.shape[0]):
        mask = same_sentence(cols_ref, rows_ref, q0, k0, k1)
        for p in range(d // LANES):
            at = lambda j: slice(j * d + p * LANES, j * d + (p + 1) * LANES)
            q2 = two_heads(qkv_ref[q0 : q0 + MAXLEN, at(0)], low_half)
            prob = probabilities(q2, qkv_ref[k0:k1, at(1)], mask).astype(BF16)
            out = mm(prob, qkv_ref[k0:k1, at(2)])
            att_ref[q0 : q0 + MAXLEN, at(0)] = pick_heads(out, low_half).astype(BF16)


def probs_kernel(cols_ref, rows_ref, qkv_ref, *prob_refs):
    d = qkv_ref.shape[1] // 3
    low_half = lax.broadcasted_iota(jnp.int32, (MAXLEN, LANES), 1) < HEAD_DIM
    n = len(prob_refs) // 2
    for prob_ref, (q0, k0, k1) in zip(zip(prob_refs[:n], prob_refs[n:]), head_blocks(qkv_ref.shape[0])):
        mask = same_sentence(cols_ref, rows_ref, q0, k0, k1)
        pairs = d // LANES
        for p in range(pairs):
            lanes = slice(p * LANES, (p + 1) * LANES)
            q2 = two_heads(qkv_ref[q0 : q0 + MAXLEN, lanes], low_half)
            prob = probabilities(q2, qkv_ref[k0:k1, d + p * LANES : d + (p + 1) * LANES], mask)
            prob_ref[2 * p // pairs][2 * p % pairs // 2] = prob
        for ref in prob_ref:
            ref.send()


def attend_back_blocks(pairs, prob_refs, qkv_ref, atg_ref, dq_s, dk_s, dv_s):
    toks, d = atg_ref.shape
    scale = 1.0 / math.sqrt(HEAD_DIM)
    dk_s[...] = jnp.zeros_like(dk_s)
    dv_s[...] = jnp.zeros_like(dv_s)
    low_half = lax.broadcasted_iota(jnp.int32, (MAXLEN, LANES), 1) < HEAD_DIM
    for prob_ref, (q0, k0, k1) in zip(prob_refs, head_blocks(toks)):
        for i, p in enumerate(pairs):
            at = lambda j: slice(j * d + p * LANES, j * d + (p + 1) * LANES)
            lanes = slice(i * LANES, (i + 1) * LANES)
            q2 = two_heads(qkv_ref[q0 : q0 + MAXLEN, at(0)], low_half)
            keys, values = qkv_ref[k0:k1, at(1)], qkv_ref[k0:k1, at(2)]
            prob = prob_ref[i]
            a2 = two_heads(atg_ref[q0 : q0 + MAXLEN, at(0)], low_half)
            prob_grad = mm(a2, values, NT)
            dv_s[k0:k1, lanes] += mm(prob.astype(BF16), a2, TN)
            inner = jnp.sum(prob_grad * prob, axis=-1, keepdims=True)
            score_grad = (prob * (prob_grad - inner)).astype(BF16)
            dq_s[q0 : q0 + MAXLEN, lanes] = pick_heads(mm(score_grad, keys), low_half)
            dk_s[k0:k1, lanes] += mm(score_grad, q2, TN)
    return [
        (dq_s[...] * scale).astype(BF16),
        (dk_s[...] * scale).astype(BF16),
        dv_s[...].astype(BF16),
    ]


def attend_back_first_kernel(n_prob, *refs):
    prob_refs = refs[:n_prob]
    qkv_ref, atg_ref, out_ref, dq_s, dk_s, dv_s = refs[n_prob:]
    pairs = range(out_ref.shape[2] // LANES)
    grads = attend_back_blocks(pairs, prob_refs, qkv_ref, atg_ref, dq_s, dk_s, dv_s)
    for j in range(3):
        out_ref[j] = grads[j]


def attend_back_kernel(sizes, stacked, n_prob, me_ref, tok_ref, gb_ref, *rest):
    prob_refs = rest[:n_prob]
    qkv_ref, atg_ref, ag_ref, first_ref = rest[n_prob : n_prob + 4]
    rest = rest[n_prob + 4 :]
    n_w = len(OFFSETS) if stacked else 1
    w_refs = rest[:n_w]
    gtok_ref = rest[n_w]
    g_refs = rest[n_w + 1 : -7]
    qkv_w, dq_s, dk_s, dv_s, gqkv_s, small_s, sems = rest[-7:]
    load_qkv(sizes, me_ref, w_refs, qkv_w, sems.at[0])
    d = tok_ref.shape[1]
    pairs = range(first_ref.shape[2] // LANES, d // LANES)
    grads = attend_back_blocks(pairs, prob_refs, qkv_ref, atg_ref, dq_s, dk_s, dv_s)
    grads = [jnp.concatenate([first_ref[j], grads[j]], axis=1) for j in range(3)]
    xhat, r = norm_parts(tok_ref[...].astype(F32))
    n1 = (xhat * gb_ref[0:1, :] + gb_ref[3:4, :]).astype(BF16)
    rows, cols = g_refs[0].shape[1], 3 * d // (sizes["y"] * sizes["c"])
    for j in range(3):
        gqkv_s[:, j * d : (j + 1) * d] = mm(n1, grads[j], TN).astype(BF16)
    if stacked:
        move_pieces(sizes, me_ref, g_refs, [(gqkv_s, rows, cols, 0, 1)], sems.at[1], False)
    else:
        pltpu.make_async_copy(gqkv_s, g_refs[0], sems.at[1]).start()
    wait_all(qkv_w, sems.at[0])
    n1_grad = sum(mm(grads[j], qkv_w[:, j * d : (j + 1) * d], NT) for j in range(3))
    dv, gain, bias = norm_back(xhat, r, gb_ref[0:1, :], n1_grad)
    small_s[...] = as_columns([gain, bias]).astype(BF16)
    if stacked:
        move_pieces(sizes, me_ref, g_refs, [(small_s, rows, LANES, cols, 1)], sems.at[1], False)
    else:
        pltpu.make_async_copy(small_s, g_refs[1], sems.at[1]).start()
    gtok_ref[...] = ag_ref[...] + dv
    for ref in g_refs:
        wait_all(ref, sems.at[1])


def as_columns(rows):
    n = len(rows)
    block = jnp.concatenate(rows + [jnp.zeros((16 - n, rows[0].shape[1]), F32)], axis=0).astype(BF16)
    i0 = lax.broadcasted_iota(jnp.int32, (16, LANES), 0)
    i1 = lax.broadcasted_iota(jnp.int32, (16, LANES), 1)
    return mm(block, (i0 == i1).astype(BF16), TN)


def feed_kernel(sizes, stacked, me_ref, tok_ref, att_ref, gb_ref, cols_ref, rows_ref, route_ref, cot_ref, *rest):
    n_w = len(OFFSETS) if stacked else 3
    w_refs = rest[:n_w]
    rest = rest[n_w:]
    after_ref, two_ref, gate_ref, send_ref = rest[:4]
    x_s, g_s, send_sems = rest[-3:]
    rest = rest[:-3]
    out_w, in_w, down_w, sems = rest[-4:]
    load_ff(sizes, me_ref, w_refs, stacked, (out_w, in_w, down_w), sems)
    ff = in_w.shape[1]
    toks, d = tok_ref.shape
    wait_all(out_w, sems.at[0])
    after = tok_ref[...].astype(F32) + mm(att_ref[...], out_w[...])
    after_ref[...] = after
    after_ref.send()
    xhat, _ = norm_parts(after)
    n2 = (xhat * gb_ref[1:2, :] + gb_ref[4:5, :]).astype(BF16)
    wait_all(in_w, sems.at[1])
    step = 512
    total = None
    for j in range(ff // step):
        hidden = gelu(mm(n2, in_w[:, j * step : (j + 1) * step])).astype(BF16)
        if j == 0:
            wait_all(down_w, sems.at[2])
        part = mm(hidden, down_w[j * step : (j + 1) * step, :])
        total = part if total is None else total + part
    layer_two = after + total
    two_ref[...] = layer_two
    two_ref.send()
    xhat, _ = norm_parts(layer_two)
    n3 = (xhat * gb_ref[2:3, :] + gb_ref[5:6, :]).astype(BF16)
    logits = mm(n3, route_ref[...], NT)
    lane = lax.broadcasted_iota(jnp.int32, logits.shape, 1)
    chosen = [
        jnp.sum(jnp.where(lane == cols_ref[:, c + 1 : c + 2], logits, 0.0), axis=1, keepdims=True)
        for c in range(2)
    ]
    peak = jnp.maximum(chosen[0], chosen[1])
    exps = [jnp.exp(v - peak) for v in chosen]
    gates = [v / (exps[0] + exps[1]) for v in exps]
    lane = lax.broadcasted_iota(jnp.int32, gate_ref.shape, 1)
    gate_ref[...] = jnp.where(lane == 0, gates[0], jnp.where(lane == 1, gates[1], 0.0))
    upstream = cot_ref[...].astype(F32)
    row_grads = [(gates[c] * upstream).astype(BF16) for c in range(2)]
    experts, cap, _ = x_s.shape
    chunk = min(512, experts * cap)
    per = chunk // cap
    sends = [pltpu.make_async_copy(v, send_ref.at[:, i], send_sems.at[i]) for i, v in enumerate((x_s, g_s))]
    hots = []
    for j in range(experts * cap // chunk):
        slot = lax.broadcasted_iota(jnp.int32, (chunk, toks), 0) + j * chunk
        hots.append([(slot == rows_ref[c + 1 : c + 2, :]).astype(BF16) for c in range(2)])
        x_s[j * per : (j + 1) * per] = mm(hots[-1][0] + hots[-1][1], n3).astype(BF16).reshape(per, cap, x_s.shape[2])
    sends[0].start()
    for j, hot in enumerate(hots):
        rows = (mm(hot[0], row_grads[0]) + mm(hot[1], row_grads[1])).astype(BF16)
        g_s[j * per : (j + 1) * per] = rows.reshape(per, cap, g_s.shape[2])
    sends[1].start()
    for copy in sends:
        copy.wait()


def hidden_kernel(sizes, stacked, me_ref, after_ref, gb_ref, *rest):
    n_w = len(OFFSETS) if stacked else 1
    w_refs = rest[:n_w]
    hid_ref, slope_ref, in_w, sems = rest[n_w:]
    d, ff = in_w.shape
    if stacked:
        oc = d // (sizes["y"] * sizes["c"])
        parts = [(in_w, w_refs[0].shape[1], ff // (sizes["y"] * sizes["c"]), oc, 1)]
        move_pieces(sizes, me_ref, w_refs, parts, sems.at[0], True)
    else:
        pltpu.make_async_copy(w_refs[0], in_w, sems.at[0]).start()
    xhat, _ = norm_parts(after_ref[...])
    n2 = (xhat * gb_ref[1:2, :] + gb_ref[4:5, :]).astype(BF16)
    wait_all(in_w, sems.at[0])
    step = 512

    @pl.loop(0, ff // step)
    def _(j):
        hidden, slope = gelu_both(mm(n2, in_w[:, pl.ds(pl.multiple_of(j * step, step), step)]))
        hid_ref.buffer[j] = hidden.astype(BF16)
        hid_ref.part(j)
        slope_ref.buffer[j] = slope
        slope_ref.part(j)


def feed_back_kernel(sizes, stacked, me_ref, cols_ref, cot_ref, gate_ref, two_ref, gb_ref, route_ref, after_ref, hid_ref, slope_ref, att_ref, back_ref, *rest):
    n_w = len(OFFSETS) if stacked else 3
    w_refs = rest[:n_w]
    rest = rest[n_w:]
    lout_ref, ag_ref, atg_ref = rest[:3]
    g_refs = rest[3:-12]
    out_w, in_w, down_w, gout_s, gin_s, gdown_s, small_s, res_s, ing_s, back_sems, wait_sem, sems = rest[-12:]
    gets = [pltpu.make_async_copy(back_ref.at[:, i], v, back_sems.at[i]) for i, v in enumerate((res_s, ing_s))]
    for copy in gets:
        copy.start()
    load_ff(sizes, me_ref, w_refs, stacked, (out_w, in_w, down_w), wait_sem)
    toks, d = after_ref.shape
    ff = in_w.shape[1]
    experts, cap, _ = res_s.shape
    slots = experts * cap
    slot = lax.broadcasted_iota(jnp.int32, (toks, slots), 1)
    hot = [(slot == cols_ref[:, c + 3 : c + 4]).astype(BF16) for c in range(2)]
    gates = [gate_ref[:, c : c + 1] for c in range(2)]
    upstream = cot_ref[...].astype(F32)
    layer_two = two_ref[...]
    xhat3, r3 = norm_parts(layer_two)
    n3 = (xhat3 * gb_ref[2:3, :] + gb_ref[5:6, :]).astype(BF16)
    gets[0].wait()
    results = res_s[...].reshape(slots, d)
    picked = [mm(hot[c], results) for c in range(2)]
    lout_ref[...] = (layer_two + gates[0] * picked[0] + gates[1] * picked[1]).astype(BF16)
    lout_ref.send()
    gate_grad = [jnp.sum(upstream * v, axis=1, keepdims=True) for v in picked]
    mean = gates[0] * gate_grad[0] + gates[1] * gate_grad[1]
    lane = lax.broadcasted_iota(jnp.int32, (toks, LANES), 1)
    logit_grad = sum(
        jnp.where(lane == cols_ref[:, c + 1 : c + 2], gates[c] * (gate_grad[c] - mean), 0.0) for c in range(2)
    ).astype(BF16)
    grad_route = mm(n3, logit_grad, TN)
    gets[1].wait()
    three_grad = mm(hot[0] + hot[1], ing_s[...].reshape(slots, d)) + mm(logit_grad, route_ref[...])
    dv, gain3, bias3 = norm_back(xhat3, r3, gb_ref[2:3, :], three_grad)
    two_grad = upstream + dv
    ffn_grad = two_grad.astype(BF16)
    xhat, r = norm_parts(after_ref[...])
    n2 = (xhat * gb_ref[1:2, :] + gb_ref[4:5, :]).astype(BF16)
    wait_all(down_w, wait_sem.at[2])
    wait_all(in_w, wait_sem.at[1])
    step = 512
    hid_s, slope_s, n2_grad = hid_ref.ready(), slope_ref.ready(), ag_ref.buffer
    n2_grad[...] = jnp.zeros_like(n2_grad)

    @pl.loop(0, ff // step)
    def _(j):
        at = pl.ds(pl.multiple_of(j * step, step), step)
        gdown_s[at, :] = mm(hid_s[j], ffn_grad, TN).astype(BF16)
        pre_grad = (mm(ffn_grad, down_w[at, :], NT) * slope_s[j]).astype(BF16)
        gin_s[:, at] = mm(n2, pre_grad, TN).astype(BF16)
        n2_grad[...] += mm(pre_grad, in_w[:, at], NT)

    if stacked:
        _, rows, width = g_refs[0].shape
        parts = ff_parts(sizes, rows, gout_s, gin_s, gdown_s)
        move_pieces(sizes, me_ref, g_refs, parts[1:], sems.at[0], False)
    else:
        for src, dst in zip((gin_s, gdown_s), g_refs[1:3]):
            pltpu.make_async_copy(src, dst, sems.at[0]).start()
    dv, gain2, bias2 = norm_back(xhat, r, gb_ref[1:2, :], n2_grad[...])
    after_grad = two_grad + dv
    ag_ref[...] = after_grad
    ag_ref.send()
    attn_grad = after_grad.astype(BF16)
    gout_s[...] = mm(att_ref[...], attn_grad, TN).astype(BF16)
    lanes = lax.broadcasted_iota(jnp.int32, (16, LANES), 1)
    lanes = lanes - lax.broadcasted_iota(jnp.int32, (16, LANES), 0)
    norms = jnp.concatenate([gain2, gain3, bias2, bias3, jnp.zeros((12, d), F32)], axis=0).astype(BF16)
    n_route = route_columns(sizes)
    small_s[...] = (grad_route + mm(norms, (lanes == n_route).astype(BF16), TN)).astype(BF16)
    if stacked:
        parts = [parts[0], (small_s, rows, LANES, width - LANES, 1)]
        move_pieces(sizes, me_ref, g_refs, parts, sems.at[0], False)
    else:
        for src, dst in zip((gout_s, small_s), (g_refs[0], g_refs[3])):
            pltpu.make_async_copy(src, dst, sems.at[0]).start()
    wait_all(out_w, wait_sem.at[0])
    atg_ref[...] = mm(attn_grad, out_w[...], NT).astype(BF16)
    for ref in g_refs:
        wait_all(ref, sems.at[0])


def route_columns(sizes):
    return sizes["y"] * sizes["c"] * sizes["x"]


def expert_kernel(n_ring, recv_ref, *rest):
    w_refs = rest[:n_ring]
    ret_ref = rest[n_ring]
    hid_ref, pg_ref, x_s, g_s, up_s, down_s, acc_s, gacc_s, sems, w_sems = rest[n_ring + 1 :]
    gets = [pltpu.make_async_copy(recv_ref.at[:, i], v, sems.at[i]) for i, v in enumerate((x_s, g_s))]
    gets[0].start()
    per, _, f = w_refs[0].shape
    n_src, cap, d = x_s.shape
    for s in range(n_ring):
        for k in range(per):
            piece = w_refs[s].at[k]
            cols = pl.ds(k * f, f)
            pltpu.make_async_copy(piece.at[pl.ds(0, d), :], up_s.at[s, :, cols], w_sems.at[s]).start()
            for b in range(d // f):
                part = piece.at[pl.ds(d + b * f, f), :]
                pltpu.make_async_copy(part, down_s.at[s, cols, pl.ds(b * f, f)], w_sems.at[s]).start()
        if s == 0:
            gets[1].start()
    rows = n_src * cap
    step = min(512, rows)
    blocks = [(slice(j, j + step), slice(j // cap, (j + step) // cap)) for j in range(0, rows, step)]
    for copy in gets:
        copy.wait()
    acc_s[...] = jnp.zeros_like(acc_s)
    gacc_s[...] = jnp.zeros_like(gacc_s)
    hid_s, pg_s = hid_ref.buffer, pg_ref.buffer

    @pl.loop(0, n_ring)
    def _(s):
        wait_all(up_s.at[s], w_sems.at[s])
        wait_all(down_s.at[s], w_sems.at[s])
        for at, src in blocks:
            x = x_s[src].reshape(step, d)
            hidden, slope = gelu_both(mm(x, up_s[s]))
            hidden = hidden.astype(BF16)
            hid_s[s, at, :] = hidden
            acc_s[at, :] += mm(hidden, down_s[s])
            pre_grad = (mm(g_s[src].reshape(step, d), down_s[s], NT) * slope).astype(BF16)
            pg_s[s, at, :] = pre_grad
            gacc_s[at, :] += mm(pre_grad, up_s[s], NT)
        hid_ref.part(s)
        pg_ref.part(s)

    x_s[...] = acc_s[...].astype(BF16).reshape(x_s.shape)
    g_s[...] = gacc_s[...].astype(BF16).reshape(g_s.shape)
    puts = [pltpu.make_async_copy(v, ret_ref.at[:, i], sems.at[i]) for i, v in enumerate((x_s, g_s))]
    for copy in puts:
        copy.start()
    for copy in puts:
        copy.wait()


def expert_grad_kernel(places, recv_ref, hid_ref, pg_ref, *refs):
    n = len(places)
    out_refs = refs[:n]
    x_s, g_s, hid_s, pg_s, out_s, sems, block_sems, out_sem = refs[n:]
    gets = [pltpu.make_async_copy(recv_ref.at[:, i], v, sems.at[i]) for i, v in enumerate((x_s, g_s))]
    for copy in gets:
        copy.start()
    for s, place in enumerate(places):
        for ref, v in ((pg_ref, pg_s), (hid_ref, hid_s)):
            pltpu.make_async_copy(ref.at[place], v.at[s], block_sems.at[s]).start()
    n_src, cap, d = x_s.shape
    rows = n_src * cap
    _, per, _, f = out_s.shape
    for copy in gets:
        copy.wait()

    @pl.loop(0, n)
    def _(s):
        wait_all(pg_s.at[s], block_sems.at[s])
        wait_all(hid_s.at[s], block_sems.at[s])
        up = mm(x_s[...].reshape(rows, d), pg_s[s], TN).astype(BF16)
        down = mm(hid_s[s], g_s[...].reshape(rows, d), TN).astype(BF16)
        for k in range(per):
            cols = slice(k * f, (k + 1) * f)
            out_s[s, k, 0:d, :] = up[:, cols]
            for b in range(d // f):
                out_s[s, k, d + b * f : d + (b + 1) * f, :] = down[cols, b * f : (b + 1) * f]

    puts = [pltpu.make_async_copy(out_s.at[s], ref, out_sem.at[s]) for s, ref in enumerate(out_refs)]
    for copy in puts:
        copy.start()
    for copy in puts:
        copy.wait()


def local(sizes, tokens, lengths, task_ids, expert_table, norm_gain, norm_bias, w_qkv, w_out, w_in, w_down, w_router, expert_up, expert_down, cotangent):
    toks, d = tokens.shape
    local_experts, _, f = expert_up.shape
    assert local_experts == sizes["x"] == 2
    share = sizes["y"] * sizes["c"]
    n_hid = sizes["z"] * sizes["x"]
    experts = share * local_experts
    capacity = 2 * toks // experts
    slots = experts * capacity
    ff = w_in.shape[1] * share
    rc = w_router.shape[1]
    rows_dev = d // n_hid
    n_ring = sizes["z"]
    ring = [(i, (i + 1) % n_ring) for i in range(n_ring)]
    stacked = sizes["y"] == sizes["c"] == 2 and all(
        w.shape[1] % LANES == 0 for w in (w_qkv, w_out, w_in, w_down)
    )

    def after(v, *others):
        return lax.optimization_barrier((v,) + others)[0]

    def swap(v, axis, by=1):
        n = math.prod(sizes[a] for a in axis)
        return lax.ppermute(v, axis, [(i, i ^ by) for i in range(n)])

    def gather_z(piece):
        return [piece] + [swap(piece, ("z",), by) for by in range(1, n_ring)]

    def plane_swaps(stacks):
        return [swap(stacks[by], ("y", "x"), by) for by in range(1, len(PLANE))]

    def other_core(stacks):
        return [swap(t, ("c",)) for t in stacks]

    def add_core(near, far, name, placed=False):
        n, shape = len(PLANE), near[0].shape
        outs = [sds((n,) + shape, BF16)] if placed else [sds(shape, F32)] + [sds(shape, BF16)] * (n - 1)
        return call(
            functools.partial(sum_cores_kernel, placed),
            name,
            K[name],
            outs,
            [smem()] + ["late"] * (2 * n),
            [anywhere()] if placed else ["early"] * n,
            [pltpu.VMEM((n,) + shape, BF16), dma((n,))] if placed else [],
        )(me, *[v for v in near[:n]], *far)

    def add_plane(mine, got):
        total = sum((v.astype(F32) for v in got), mine)
        return total[0], total[1:].astype(BF16)

    def z_swaps(parts):
        return [swap(parts[by - 1], ("z",), by) for by in range(1, n_ring)]

    def add_z(mine, got):
        return sum((v.astype(F32) for v in got), mine)

    def exchange(v):
        return lax.all_to_all(v, ("y", "c", "x"), split_axis=0, concat_axis=0, tiled=True)

    def gather_whole(w):
        w = lax.all_gather(w.astype(BF16), ("y", "c"), axis=1, tiled=True)
        return lax.all_gather(w, ("z", "x"), axis=0, tiled=True)

    def reduce_whole(g):
        g = lax.psum_scatter(g.astype(F32), ("z", "x"), scatter_dimension=0, tiled=True)
        return lax.psum_scatter(g, ("y", "c"), scatter_dimension=1, tiled=True)

    def sds(shape, dtype):
        return jax.ShapeDtypeStruct(shape, dtype)

    dma = pltpu.SemaphoreType.DMA
    me = jnp.stack([lax.axis_index(a) for a in AXES]).astype(jnp.int32)
    x_at = lax.axis_index("x")

    def piece_of(at):
        up = lax.dynamic_index_in_dim(expert_up, at, 0, keepdims=False)
        down = lax.dynamic_index_in_dim(expert_down, at, 0, keepdims=False)
        return jnp.concatenate(
            [up] + [down[:, b * f : (b + 1) * f] for b in range(d // f)], axis=0
        ).astype(BF16)

    def routes(lengths):
        return find_routes(lengths, task_ids, expert_table, toks, experts, capacity)

    if stacked:
        folds = w_down.shape[0] // rows_dev
        width = w_out.shape[1] + w_in.shape[1] + folds * w_down.shape[1]
        small = jnp.concatenate([w_router, norm_gain, norm_bias], axis=1)
        small = jnp.pad(small, ((0, 0), (0, LANES - small.shape[1])))
        qkv_piece = jnp.concatenate([w_qkv, small], axis=1).astype(BF16)
        ff_piece, own, other = call(
            pack_kernel,
            "pack",
            K["pack"],
            [sds((rows_dev, width), BF16)] + [sds((2 * d, f), BF16)] * 2,
            [smem()] + ["late"] * 5,
            ["early"] * 3,
        )(me, w_out, w_in, w_down, expert_up, expert_down)
        expert_x = swap(other, ("x",))
        qkv_z = gather_z(qkv_piece)
        mine = jnp.stack(qkv_z)
        qkv_w = [mine] + plane_swaps([mine] * len(PLANE))
        ff_z = gather_z(after(ff_piece, *qkv_z[1:]))
        rows, cols = routes(after(lengths, *qkv_z[1:], *([expert_x] if K["x_first"] else [])))
        if K["tie_near"]:
            qkv_w = [mine] + [after(t, rows) for t in qkv_w[1:]]
        qkv_w = qkv_w + other_core(qkv_w)
        blocks = [jnp.stack([own, expert_x])]
        if K["ring1"]:
            blocks[0] = after(blocks[0], *ff_z[1:])
        blocks.append(lax.ppermute(blocks[0], "z", ring))
        if K["tie_ffz"]:
            ff_z = [ff_z[0]] + [after(t, rows) for t in ff_z[1:]]
        mine = jnp.stack(ff_z)
        ffw = [mine] + plane_swaps([mine] * len(PLANE))
        tokens_in = after(tokens, rows)
        gb_in = []
    else:
        qkv_w = [gather_whole(w_qkv)]
        ffw = [gather_whole(w_out), gather_whole(w_in), gather_whole(w_down)]
        small = jnp.concatenate([w_router, norm_gain, norm_bias], axis=1)
        small = lax.all_gather(small.astype(BF16), AXES)
        route = small[:, :, :rc].reshape(share, d, rc).transpose(0, 2, 1).reshape(experts, d)
        route = jnp.pad(route, ((0, LANES - experts), (0, 0)))
        gb = small[:n_hid, :, rc:].reshape(d, 6).T.astype(F32)
        gb = jnp.pad(gb, ((0, 2), (0, 0)))
        gb_in = [gb]
        tokens_in = tokens
        rows, cols = routes(lengths)
        blocks = [jnp.stack([piece_of(x_at), swap(piece_of(1 - x_at), ("x",))])]
        blocks.append(lax.ppermute(blocks[0], "z", ring))

    out_shape = [sds((toks, 3 * d), BF16), sds((toks, d), BF16)]
    scratch = [pltpu.VMEM((d, 3 * d), BF16)]
    if stacked:
        out_shape += [sds((8, d), F32), sds((LANES, d), BF16)]
        scratch += [pltpu.VMEM((share, d, LANES), BF16)]
    out = call(
        functools.partial(attend_kernel, sizes, stacked, rc),
        "attend",
        K["attend"],
        out_shape,
        [smem()] + ["late"] * 3 + [vmem()] * len(gb_in) + [anywhere()] * len(qkv_w),
        ["early"] * 2 + [vmem()] * (len(out_shape) - 2),
        scratch + [dma((2,))],
    )(me, tokens_in, cols, rows, *gb_in, *qkv_w)
    qkv, attended = out[:2]
    if stacked:
        gb, route = out[2:]
        ffw = [ffw[0]] + [after(t, attended, *(blocks[-1:] if K["ringff"] else [])) for t in ffw[1:]]
        ffw = ffw + other_core(ffw)
    if n_ring > 2:
        blocks.append(lax.ppermute(after(blocks[-1], attended), "z", ring))

    f_scratch = [pltpu.VMEM((d, d), BF16), pltpu.VMEM((d, ff), BF16), pltpu.VMEM((ff, d), BF16)]
    pair = [pltpu.VMEM((experts, capacity, d), BF16)] * 2
    after_attn, layer_two, gates, send = call(
        functools.partial(feed_kernel, sizes, stacked),
        "feed",
        K["feed"],
        [sds((toks, d), F32), sds((toks, d), F32), sds((toks, LANES), F32)]
        + [sds((experts, 2, capacity, d), BF16)],
        [smem()] + ["late"] * 2 + [vmem()] + ["late"] * 4 + [anywhere()] * len(ffw),
        ["early"] * 3 + [anywhere()],
        f_scratch + [dma((3,))] + pair + [dma((2,))],
    )(me, tokens, attended, gb, cols, rows, route, cotangent, *ffw)
    while len(blocks) < n_ring:
        blocks.append(lax.ppermute(after(blocks[-1], after_attn), "z", ring))

    recv = exchange(send)
    block = [sds((n_ring, slots, 2 * f), BF16)]
    out = call(
        functools.partial(expert_kernel, n_ring),
        "experts",
        K["experts"],
        [sds(recv.shape, BF16)] + block * 2,
        [anywhere()] * (1 + n_ring),
        [anywhere()] + ["early"] * 2,
        pair
        + [pltpu.VMEM((n_ring, d, 2 * f), BF16), pltpu.VMEM((n_ring, 2 * f, d), BF16)]
        + [pltpu.VMEM((slots, d), F32)] * 2
        + [dma((2,)), dma((n_ring,))],
    )(recv, *blocks)
    hids, pre_grads = out[1:]
    back = exchange(out[0])

    def expert_grads(places, recv):
        n = len(places)
        blocks = [pltpu.VMEM((n, slots, 2 * f), BF16)] * 2 + [pltpu.VMEM((n, 2, 2 * d, f), BF16)]
        return call(
            functools.partial(expert_grad_kernel, places),
            "expert_grads",
            K["expert_grads"] * n,
            [sds((2, 2 * d, f), BF16)] * n,
            [anywhere()] * 3,
            [anywhere()] * n,
            pair + blocks + [dma((2,)), dma((n,)), dma((n,))],
        )(recv, hids, pre_grads)

    far_grads = expert_grads([1], recv)
    moving = lax.ppermute(far_grads[0], "z", ring)
    rest = expert_grads([s % n_ring for s in range(2, n_ring + 1)], after(recv, far_grads[0]))
    prob_shapes = [sds((d // LANES // 2, 2 * MAXLEN, k1 - k0), F32) for _, k0, k1 in head_blocks(toks)] * 2
    probs = call(
        probs_kernel, "probs", K["probs"], prob_shapes, [vmem()] * 3, ["early"] * len(prob_shapes)
    )(cols, rows, after(qkv, rest[0]))
    hidden, slope = call(
        functools.partial(hidden_kernel, sizes, stacked),
        "hidden",
        K["hidden"],
        [sds((ff // 512, toks, 512), BF16), sds((ff // 512, toks, 512), F32)],
        [smem()] + [vmem()] * 2 + [anywhere()] * (len(OFFSETS) if stacked else 1),
        ["early"] * 2,
        [pltpu.VMEM((d, ff), BF16), dma((1,))],
    )(me, after(after_attn, rest[0]), gb, *(ffw if stacked else ffw[1:2]))

    if stacked:
        ff_cols, qkv_cols = ffw[0].shape[-1] + LANES, qkv_w[0].shape[-1]
        ff_out = [sds((n_ring, rows_dev, ff_cols), BF16)] * len(OFFSETS)
        qkv_out = [sds((n_ring, rows_dev, qkv_cols), BF16)] * len(OFFSETS)
    else:
        ff_out = [sds((d, d), BF16), sds((d, ff), BF16), sds((ff, d), BF16), sds((d, LANES), BF16)]
        qkv_out = [sds((d, 3 * d), BF16), sds((d, LANES), BF16)]
    out = call(
        functools.partial(feed_back_kernel, sizes, stacked),
        "feed_back",
        K["feed_back"],
        [sds((toks, d), BF16), sds((toks, d), F32), sds((toks, d), BF16)] + ff_out,
        [smem()] + ["late"] * 4 + [vmem()] + ["late"] * 5 + [anywhere()] * (1 + len(ffw)),
        ["early"] * 3 + [anywhere()] * len(ff_out),
        f_scratch + f_scratch + [pltpu.VMEM((d, LANES), BF16)] + pair + [dma((2,)), dma((3,)), dma((1,))],
    )(me, cols, cotangent, gates, layer_two, gb, route, after_attn, hidden, slope, attended, after(back, probs[0]), *ffw)
    layer_out, after_grad, att_grad = out[:3]
    ff_grads = out[3:]
    step = n_ring - 2

    def add_on(moving, mine, weight):
        n, shape = 4, (4, mine.shape[0] * mine.shape[1] // 4, mine.shape[2])
        scratch = [pltpu.VMEM(shape, BF16)] * 3 + [dma((3, n))]
        return call(add_kernel, "add", weight, sds(mine.shape, BF16), [anywhere()] * 2, anywhere(), scratch)(moving, mine)

    for t in range(step - 1):
        if K["tie_ring1"]:
            moving = after(moving, after_grad)
        moving = lax.ppermute(add_on(moving, rest[t], K["add1"]), "z", ring)
    if stacked:
        ff_far = other_core(ff_grads[len(PLANE) :])
    half = d // 2
    n_prob = len(probs) // 2
    acc = [pltpu.VMEM((toks, half), F32)] * 3
    first_half = call(
        functools.partial(attend_back_first_kernel, n_prob),
        "attend_back_first",
        K["first"],
        [sds((3, toks, half), BF16)],
        ["late"] * (2 + n_prob),
        [vmem()],
        acc,
    )(*probs[:n_prob], qkv, att_grad)[0]
    if stacked:
        if K["tie_ffc"]:
            ff_far = [after(v, first_half) for v in ff_far]
        ff_sums = add_core(ff_grads, ff_far, "sum_ff", K["ff_a2a"])
        if K["ff_a2a"]:
            ff_got = [lax.all_to_all(ff_sums[0], ("y", "x"), split_axis=0, concat_axis=0, tiled=True)]
        else:
            ff_got = plane_swaps(ff_sums)
        att_grad = after(att_grad, ff_sums[0])
    else:
        att_grad = after(att_grad, first_half)
    out = call(
        functools.partial(attend_back_kernel, sizes, stacked, n_prob),
        "attend_back",
        K["attend_back"],
        [sds((toks, d), F32)] + qkv_out,
        [smem(), "late", vmem()] + ["late"] * (4 + n_prob) + [anywhere()] * len(qkv_w),
        ["early"] + [anywhere()] * len(qkv_out),
        [pltpu.VMEM((d, 3 * d), BF16)]
        + acc
        + [pltpu.VMEM((d, 3 * d), BF16), pltpu.VMEM((d, LANES), BF16), dma((2,))],
    )(me, tokens, gb, *probs[n_prob:], qkv, att_grad, after_grad, first_half, *qkv_w)
    grad_tokens = out[0]
    qkv_grads = out[1:]

    e_at = lax.axis_index("y") * sizes["c"] + lax.axis_index("c")
    if step:
        if K["tie_ring2"]:
            moving = after(moving, grad_tokens)
        moving = lax.ppermute(add_on(moving, rest[step - 1], K["add2"]), "z", ring)
    if stacked:
        qkv_sums = add_core(qkv_grads, other_core(qkv_grads[len(PLANE) :]), "sum_qkv")
        qkv_got = plane_swaps(qkv_sums)
        if K["tie_qkv"]:
            qkv_got = [after(v, *ff_got) for v in qkv_got]
        if K["tie_ring3"] == 1:
            moving = after(moving, *qkv_got)
        if K["ff_a2a"]:
            ff_mine, ff_parts_z = add_plane(0.0, [ff_got[0][i] for i in range(len(PLANE))])
        else:
            ff_mine, ff_parts_z = add_plane(ff_sums[0], ff_got)
        ff_got = z_swaps(ff_parts_z)
        qkv_mine, qkv_parts_z = add_plane(qkv_sums[0], qkv_got)
        qkv_got = z_swaps(qkv_parts_z)
    summed = moving.astype(F32) + rest[-1].astype(F32)
    other = swap(summed[1].astype(BF16), ("x",))
    if stacked and K["tie_x"] == 1:
        qkv_got = [after(v, other) for v in qkv_got]
    if stacked and K["tie_x"] == 2:
        other = after(other, *qkv_got)
    other = other.astype(F32)
    mine = summed[0]

    def unpiece(p):
        return p[:d], jnp.concatenate([p[d + b * f : d + (b + 1) * f] for b in range(d // f)], axis=1)

    own_up, own_down = unpiece(mine)
    oth_up, oth_down = unpiece(other)
    first = x_at == 0
    grad_up = jnp.where(first, jnp.stack([own_up, oth_up]), jnp.stack([oth_up, own_up]))
    grad_edown = jnp.where(first, jnp.stack([own_down, oth_down]), jnp.stack([oth_down, own_down]))

    if stacked:
        shapes = [v.shape for v in (w_out, w_in, w_down, w_qkv)]
        shapes += [v.shape[::-1] for v in (w_router, norm_gain, norm_bias)]
        grad_out, grad_in, grad_down, grad_qkv, grad_router, grad_gain, grad_bias = call(
            functools.partial(finish_kernel, n_ring, rc, route_columns(sizes)),
            "finish",
            K["finish"],
            [sds(v, F32) for v in shapes],
            [smem()] + [vmem()] * (2 * n_ring),
            [vmem()] * len(shapes),
        )(e_at.reshape(1).astype(jnp.int32), ff_mine, *ff_got, qkv_mine, *qkv_got)
        grad_router, grad_gain, grad_bias = grad_router.T, grad_gain.T, grad_bias.T
    else:
        grad_out, grad_in, grad_down = (reduce_whole(g) for g in ff_grads[:3])
        grad_qkv = reduce_whole(qkv_grads[0])
        small_ff, small_qkv = (
            lax.psum(lax.psum_scatter(g.astype(F32), ("z", "x"), scatter_dimension=0, tiled=True), ("y", "c"))
            for g in (ff_grads[3], qkv_grads[1])
        )
        grad_router = lax.dynamic_slice_in_dim(small_ff, e_at * rc, rc, axis=1)
        n_route = route_columns(sizes)
        gains, biases = small_ff[:, n_route : n_route + 2], small_ff[:, n_route + 2 : n_route + 4]
        grad_gain = jnp.concatenate([small_qkv[:, 0:1], gains], axis=1)
        grad_bias = jnp.concatenate([small_qkv[:, 1:2], biases], axis=1)
    return (
        layer_out,
        grad_tokens,
        grad_gain,
        grad_bias,
        grad_qkv,
        grad_out,
        grad_in,
        grad_down,
        grad_router,
        grad_up,
        grad_edown,
    )


def solution(mesh):
    n_exp, n_hid = mesh.shape["expert"], mesh.shape["hidden"]
    sizes = {"y": n_exp // 2, "c": 2, "z": n_hid // 2, "x": 2}
    fine = Mesh(mesh.devices.reshape(tuple(sizes[a] for a in AXES)), AXES)
    both, exp, hid = AXES, ("y", "c"), ("z", "x")
    return jax.shard_map(
        functools.partial(local, sizes),
        mesh=fine,
        in_specs=(
            P(both, None),
            P(both, None),
            P(both, None),
            P(),
            P(hid, None),
            P(hid, None),
            P(hid, exp),
            P(hid, exp),
            P(hid, exp),
            P(hid, exp),
            P(hid, exp),
            P(exp, None, hid),
            P(exp, hid, None),
            P(both, None),
        ),
        out_specs=(
            P(both, None),
            P(both, None),
            P(hid, None),
            P(hid, None),
            P(hid, exp),
            P(hid, exp),
            P(hid, exp),
            P(hid, exp),
            P(hid, exp),
            P(exp, None, hid),
            P(exp, hid, None),
        ),
        check_vma=False,
    )
```

```python
import functools
import math

import jax
import jax.numpy as jnp
from jax import lax
from jax.experimental import pallas as pl
from jax.experimental.pallas import tpu as pltpu
from jax.sharding import Mesh, PartitionSpec as P

HEAD_DIM = 64
MAXLEN = 128
LANES = 128
EPSILON = 1e-05
FILL_SCORE = -1000000000.0
AXES = ("y", "c", "z", "x")
VMEM_BYTES = 56 * 1024 * 1024
GELU_A = math.sqrt(2.0 / math.pi)
GELU_B = 0.044715

F32 = jnp.float32
BF16 = jnp.bfloat16

NN = (((1,), (0,)), ((), ()))
NT = (((1,), (1,)), ((), ()))
TN = (((0,), (0,)), ((), ()))


def mm(a, b, dims=NN):
    return lax.dot_general(a, b, dims, preferred_element_type=F32)


def gelu(v):
    t = jnp.tanh(GELU_A * (v + GELU_B * (v * v * v)))
    return 0.5 * v * (1.0 + t)


def gelu_both(v):
    v2 = v * v
    t = jnp.tanh(GELU_A * (v + GELU_B * (v2 * v)))
    half = 0.5 * (1.0 + t)
    slope = half + 0.5 * v * (1.0 - t * t) * (GELU_A + (3.0 * GELU_A * GELU_B) * v2)
    return v * half, slope


def norm_parts(v):
    center = v - jnp.mean(v, axis=-1, keepdims=True)
    r = lax.rsqrt(jnp.mean(center * center, axis=-1, keepdims=True) + EPSILON)
    return center * r, r


def norm_back(xhat, r, gain, h):
    hg = h * gain
    inner = jnp.mean(hg * xhat, axis=-1, keepdims=True)
    dv = r * (hg - jnp.mean(hg, axis=-1, keepdims=True) - xhat * inner)
    return dv, jnp.sum(h * xhat, axis=0, keepdims=True), jnp.sum(h, axis=0, keepdims=True)


K = dict(scale=0.35, routes=60, attend=0.3, feed=3, probs=3, hidden=6, experts=18, expert_grads=3, feed_back=20, first=4, attend_back=9, add1=2, add2=14, sum_ff=2, sum_qkv=3, sum_plane=0.3, finish=0.3, pack=3, gate=60, ring1=1, ringff=0, tie_near=1, tie_ffz=1, x_first=0, ff_a2a=1, tie_qkv=1, tie_ring3=1, tie_ring2=1, tie_ring1=1, tie_x=1, tie_ffc=1)


def cost(us):
    return pl.CostEstimate(flops=int(K["scale"] * us * 1.15e9), bytes_accessed=0, transcendentals=0)


def vmem():
    return pl.BlockSpec(memory_space=pltpu.VMEM)


class Late:
    def __init__(self, ref, buffer, sem):
        self.buffer, self.shape, self.dtype = buffer, buffer.shape, buffer.dtype
        self.copy = pltpu.make_async_copy(ref, buffer, sem)
        self.copy.start()
        self.waited = False

    def ready(self):
        if not self.waited:
            self.copy.wait()
            self.waited = True
        return self.buffer

    finish = ready

    def __getitem__(self, at):
        return self.ready()[at]


class Early:
    def __init__(self, ref, buffer, sem):
        self.buffer, self.shape, self.dtype = buffer, buffer.shape, buffer.dtype
        self.ref, self.sem = ref, sem
        self.copy = pltpu.make_async_copy(buffer, ref, sem)
        self.sent = False

    def send(self):
        self.copy.start()
        self.sent = True

    def part(self, i):
        pltpu.make_async_copy(self.buffer.at[i], self.ref.at[i], self.sem).start()
        self.sent = True

    def finish(self):
        if not self.sent:
            self.send()
        self.copy.wait()

    def __setitem__(self, at, value):
        self.buffer[at] = value


def call(kernel, name, us, out_shape, in_specs, out_specs, scratch=()):
    single = not isinstance(out_shape, list)
    outs, out_specs = ([out_shape], [out_specs]) if single else (out_shape, out_specs)
    specs = list(in_specs) + list(out_specs)

    def run(*args):
        arrays = list(args) + outs
        moving = [i for i, spec in enumerate(specs) if spec in ("late", "early")]

        def body(*refs):
            refs = list(refs)
            buffers, sems = refs[len(specs) + len(scratch) : -1], refs[-1]
            for j, i in enumerate(moving):
                kind = Late if specs[i] == "late" else Early
                refs[i] = kind(refs[i], buffers[j], sems.at[j])
            kernel(*refs[: len(specs) + len(scratch)])
            for i in moving:
                refs[i].finish()

        buffers = [pltpu.VMEM(arrays[i].shape, arrays[i].dtype) for i in moving]
        places = [anywhere() if spec in ("late", "early") else spec for spec in specs]
        results = pl.pallas_call(
            body,
            out_shape=outs,
            in_specs=places[: len(in_specs)],
            out_specs=places[len(in_specs) :],
            scratch_shapes=list(scratch) + buffers + [pltpu.SemaphoreType.DMA((max(len(moving), 1),))],
            compiler_params=pltpu.CompilerParams(vmem_limit_bytes=VMEM_BYTES),
            cost_estimate=cost(us),
            name=name,
        )(*args)
        return results[0] if single else results

    return run


def smem():
    return pl.BlockSpec(memory_space=pltpu.SMEM)


def anywhere():
    return pl.BlockSpec(memory_space=pl.ANY)


PLANE = ((0, 0), (0, 1), (1, 0), (1, 1))
OFFSETS = tuple((c, y, x) for c in (0, 1) for y, x in PLANE)


def move_pieces(sizes, me_ref, stacks, parts, sem, inward, placed=False):
    at = {axis: me_ref[i] for i, axis in enumerate(AXES)}
    for (dc, dy, dx), stack in zip(OFFSETS, stacks):
        y = dy if placed else lax.bitwise_xor(at["y"], dy)
        x = dx if placed else lax.bitwise_xor(at["x"], dx)
        e = y * sizes["c"] + lax.bitwise_xor(at["c"], dc)

        @pl.loop(0, sizes["z"])
        def _(dz):
            h = lax.bitwise_xor(at["z"], dz) * sizes["x"] + x
            for whole, rows, cols, first, folds in parts:
                step = rows // folds
                for i in range(folds):
                    piece = stack.at[dz, :, pl.ds(first + i * cols, cols)]
                    top = pl.multiple_of(h * rows + i * step, step)
                    if len(whole.shape) == 3:
                        block = whole.at[e, pl.ds(top, step), :]
                    elif whole.shape[1] == cols:
                        block = whole.at[pl.ds(top, step), :]
                    else:
                        block = whole.at[pl.ds(top, step), pl.ds(pl.multiple_of(e * cols, cols), cols)]
                    src, dst = (piece, block) if inward else (block, piece)
                    pltpu.make_async_copy(src, dst, sem).start()


def wait_all(ref, sem):
    pltpu.make_async_copy(ref, ref, sem).wait()


def routes_kernel(capacity, experts, len_row, task_row, table, rows_out, cols_out):
    sents = len_row.shape[1]
    tasks = table.shape[0]
    toks = rows_out.shape[1]
    f = lambda v: v.astype(F32)
    i0 = lax.broadcasted_iota(jnp.int32, (sents, sents), 0)
    i1 = lax.broadcasted_iota(jnp.int32, (sents, sents), 1)
    turn = lambda row: jnp.sum(jnp.where(i0 == i1, row, 0.0), axis=1, keepdims=True)
    len_r, task_r = f(len_row[...]), f(task_row[...])
    len_c, task_c = turn(len_r), turn(task_r)
    ends_row = jnp.sum(jnp.where(i0 <= i1, len_c, 0.0), axis=0, keepdims=True)
    ends_col = jnp.sum(jnp.where(i1 <= i0, len_r, 0.0), axis=1, keepdims=True)
    starts_row = ends_row - len_r
    starts_col = ends_col - len_c
    t0 = lax.broadcasted_iota(jnp.int32, (tasks, tasks), 0)
    t1 = lax.broadcasted_iota(jnp.int32, (tasks, tasks), 1)
    table_c = [f(table[:, c : c + 1]) for c in range(2)]
    table_r = [jnp.sum(jnp.where(t0 == t1, v, 0.0), axis=0, keepdims=True) for v in table_c]
    tok = f(lax.broadcasted_iota(jnp.int32, (toks, sents), 0))
    sent = lax.broadcasted_iota(jnp.int32, (toks, sents), 1)
    hot = (tok >= starts_row) & (tok < ends_row)
    seg_c = jnp.sum(jnp.where(hot, f(sent), 0.0), axis=1, keepdims=True)
    own = jnp.sum(jnp.where(hot, task_r, 0.0), axis=1, keepdims=True)
    thot = f(lax.broadcasted_iota(jnp.int32, (toks, tasks), 1)) == own
    pair_c = [
        jnp.sum(jnp.where(thot, table_r[c], 0.0), axis=1, keepdims=True)
        for c in range(2)
    ]
    tok = f(lax.broadcasted_iota(jnp.int32, (sents, toks), 1))
    sent = lax.broadcasted_iota(jnp.int32, (sents, toks), 0)
    hot = (tok >= starts_col) & (tok < ends_col)
    seg_r = jnp.sum(jnp.where(hot, f(sent), 0.0), axis=0, keepdims=True)
    own = jnp.sum(jnp.where(hot, task_c, 0.0), axis=0, keepdims=True)
    thot = f(lax.broadcasted_iota(jnp.int32, (tasks, toks), 0)) == own
    pair_r = [
        jnp.sum(jnp.where(thot, table_c[c], 0.0), axis=0, keepdims=True)
        for c in range(2)
    ]
    a0 = lax.broadcasted_iota(jnp.int32, (toks, toks), 0)
    a1 = lax.broadcasted_iota(jnp.int32, (toks, toks), 1)
    upper = (a0 < a1).astype(BF16)
    lower = (a1 < a0).astype(BF16)
    er = f(lax.broadcasted_iota(jnp.int32, (experts, toks), 0))
    ec = f(lax.broadcasted_iota(jnp.int32, (toks, experts), 1))
    hot_r = [(er == pair_r[c]).astype(F32) for c in range(2)]
    hot_c = [(ec == pair_c[c]).astype(F32) for c in range(2)]
    before_r = [mm(hot_r[c].astype(BF16), upper) for c in range(2)]
    before_c = [mm(lower, hot_c[c].astype(BF16)) for c in range(2)]
    before_r[1] = before_r[1] + jnp.sum(hot_r[0], axis=1, keepdims=True)
    before_c[1] = before_c[1] + jnp.sum(hot_c[0], axis=0, keepdims=True)
    place = lambda pair, rank: jnp.where(rank < capacity, pair * capacity + rank, -1.0)
    slot_r = [place(pair_r[c], jnp.sum(hot_r[c] * before_r[c], axis=0, keepdims=True)) for c in range(2)]
    slot_c = [place(pair_c[c], jnp.sum(hot_c[c] * before_c[c], axis=1, keepdims=True)) for c in range(2)]
    at = lax.broadcasted_iota(jnp.int32, rows_out.shape, 0)
    rows_out[...] = jnp.where(
        at == 0, seg_r, jnp.where(at == 1, slot_r[0], slot_r[1])
    ).astype(jnp.int32)
    at = lax.broadcasted_iota(jnp.int32, cols_out.shape, 1)
    packed = jnp.where(at == 0, seg_c, 0.0)
    for j, v in enumerate((pair_c[0], pair_c[1], slot_c[0], slot_c[1])):
        packed = jnp.where(at == j + 1, v, packed)
    cols_out[...] = packed.astype(jnp.int32)


def find_routes(lengths, task_ids, expert_table, toks, experts, capacity):
    return call(
        functools.partial(routes_kernel, capacity, experts),
        "routes",
        K["routes"],
        [jax.ShapeDtypeStruct((8, toks), jnp.int32), jax.ShapeDtypeStruct((toks, 8), jnp.int32)],
        [vmem()] * 3,
        [vmem()] * 2,
    )(lengths, task_ids, expert_table)


def pack_kernel(me_ref, out_ref, in_ref, down_ref, up_ref, edown_ref, ff_out, own_out, other_out):
    d, f = up_ref.shape[1:]
    x = me_ref[AXES.index("x")]
    for out, e in ((other_out, 1 - x), (own_out, x)):
        out[0:d, :] = up_ref[e].astype(BF16)
        for b in range(d // f):
            out[d + b * f : d + (b + 1) * f, :] = edown_ref[e, :, b * f : (b + 1) * f].astype(BF16)
        out.send()
    rows, at = out_ref.shape[0], 0
    for ref in (out_ref, in_ref):
        ff_out[:, at : at + ref.shape[1]] = ref[...].astype(BF16)
        at += ref.shape[1]
    cols = down_ref.shape[1]
    for i in range(down_ref.shape[0] // rows):
        ff_out[:, at + i * cols : at + (i + 1) * cols] = down_ref[i * rows : (i + 1) * rows, :].astype(BF16)


def add_kernel(a_ref, b_ref, out_ref, a_s, b_s, out_s, sems):
    n = a_s.shape[0]
    parts = a_ref.shape[0]
    rows = a_ref.shape[1] // (n // parts)
    at = [(i // (n // parts), pl.ds(i % (n // parts) * rows, rows)) for i in range(n)]
    gets = []
    for i, (p, row) in enumerate(at):
        gets.append([pltpu.make_async_copy(ref.at[p, row, :], s.at[i], sems.at[j, i]) for j, (ref, s) in enumerate(((a_ref, a_s), (b_ref, b_s)))])
        for copy in gets[-1]:
            copy.start()
    puts = []
    for i, (p, row) in enumerate(at):
        for copy in gets[i]:
            copy.wait()
        out_s[i] = (a_s[i].astype(F32) + b_s[i].astype(F32)).astype(out_s.dtype)
        puts.append(pltpu.make_async_copy(out_s.at[i], out_ref.at[p, row, :], sems.at[2, i]))
        puts[-1].start()
    for copy in puts:
        copy.wait()


def sum_cores_kernel(placed, me_ref, *refs):
    n = len(PLANE)
    near, far, outs = refs[:n], refs[n : 2 * n], refs[2 * n :]
    if placed:
        send_ref, send_s, sems = outs
        puts = []
        for i, (dy, dx) in enumerate(PLANE):
            at = lax.bitwise_xor(me_ref[AXES.index("y")], dy) * 2 + lax.bitwise_xor(me_ref[AXES.index("x")], dx)
            send_s[i] = (near[i][...].astype(F32) + far[i][...].astype(F32)).astype(BF16)
            puts.append(pltpu.make_async_copy(send_s.at[i], send_ref.at[at], sems.at[i]))
            puts[-1].start()
        for copy in puts:
            copy.wait()
    else:
        for i in range(1, n):
            outs[i][...] = (near[i][...].astype(F32) + far[i][...].astype(F32)).astype(BF16)
            outs[i].send()
        outs[0][...] = near[0][...].astype(F32) + far[0][...].astype(F32)


def sum_plane_kernel(me_ref, got_ref, send_ref, send_s, sems):
    n = got_ref.shape[1]
    puts = []
    for k in range(n):
        total = got_ref[0, k].astype(F32)
        for i in range(1, got_ref.shape[0]):
            total = total + got_ref[i, k].astype(F32)
        send_s[k] = total.astype(BF16)
        at = lax.bitwise_xor(me_ref[AXES.index("z")], k)
        puts.append(pltpu.make_async_copy(send_s.at[k], send_ref.at[at], sems.at[k]))
        puts[-1].start()
    for copy in puts:
        copy.wait()


def finish_experts_kernel(me_ref, moving_ref, mine_ref, other_ref, gup_ref, gdown_ref, a_s, b_s, sems):
    gets = [pltpu.make_async_copy(ref.at[0], v, sems.at[i]) for i, (ref, v) in enumerate(((moving_ref, a_s), (mine_ref, b_s)))]
    for copy in gets:
        copy.start()
    d, f = gup_ref.shape[1:]
    x = me_ref[AXES.index("x")]

    def put(value, e):
        gup_ref.buffer[e] = value[:d]
        gup_ref.part(e)
        for b in range(d // f):
            gdown_ref.buffer[e, :, b * f : (b + 1) * f] = value[d + b * f : d + (b + 1) * f]
        gdown_ref.part(e)

    for copy in gets:
        copy.wait()
    put(a_s[...].astype(F32) + b_s[...].astype(F32), x)
    put(other_ref[...].astype(F32), 1 - x)


def total_of(refs):
    total = refs[0][...].astype(F32)
    for v in refs[1:]:
        total = total + v[...].astype(F32)
    return total


def finish_kernel(n_z, route_cols, n_route, e_ref, *refs):
    gout_ref, gin_ref, gdown_ref, gqkv_ref, grouter_ref, ggain_ref, gbias_ref = refs[1 + n_z :]
    total = total_of([refs[0].at[k] for k in range(n_z)])
    at = 0
    for ref in (gout_ref, gin_ref):
        ref[...] = total[:, at : at + ref.shape[1]]
        at += ref.shape[1]
    rows, cols = total.shape[0], gdown_ref.shape[1]
    for i in range(gdown_ref.shape[0] // rows):
        gdown_ref[i * rows : (i + 1) * rows, :] = total[:, at : at + cols]
        at += cols
    small = total[:, at:].T
    total = total_of(refs[1 : 1 + n_z])
    cols = gqkv_ref.shape[1]
    gqkv_ref[...] = total[:, 0:cols]
    first = total[:, cols:].T
    at = lax.broadcasted_iota(jnp.int32, small.shape, 0)
    pick = lambda i: jnp.sum(jnp.where(at == i, small, 0.0), axis=0, keepdims=True)
    for j in range(route_cols):
        grouter_ref[j : j + 1, :] = pick(e_ref[0] * route_cols + j)
    for ref, i in ((ggain_ref, 0), (gbias_ref, 1)):
        ref[0:1, :] = first[i : i + 1]
        ref[1:3, :] = small[n_route + 2 * i : n_route + 2 * i + 2]


def head_blocks(toks):
    n = toks // MAXLEN
    return [(i * MAXLEN, max(i - 1, 0) * MAXLEN, min(i + 2, n) * MAXLEN) for i in range(n)]


def two_heads(block, low_half):
    zero = jnp.zeros_like(block)
    return jnp.concatenate([jnp.where(low_half, block, zero), jnp.where(low_half, zero, block)], axis=0)


def pick_heads(stacked, low_half):
    n = stacked.shape[0] // 2
    return jnp.where(low_half, stacked[:n], stacked[n:])


def probabilities(q2, keys, mask):
    scores = mm(q2, keys, NT) * (1.0 / math.sqrt(HEAD_DIM))
    scores = jnp.where(mask, scores, FILL_SCORE)
    exps = jnp.exp(scores - jnp.max(scores, axis=-1, keepdims=True))
    return exps * (1.0 / jnp.sum(exps, axis=-1, keepdims=True))


def same_sentence(cols_ref, rows_ref, q0, k0, k1):
    seg = cols_ref[q0 : q0 + MAXLEN, 0:1]
    return jnp.concatenate([seg, seg], axis=0) == rows_ref[0:1, k0:k1]


def load_qkv(sizes, me_ref, refs, qkv_w, sem):
    if len(refs) == 1:
        pltpu.make_async_copy(refs[0], qkv_w, sem).start()
        return
    share = sizes["y"] * sizes["c"]
    stacks = [ref.at[i] for ref in refs for i in range(ref.shape[0])]
    parts = [(qkv_w, refs[0].shape[2], qkv_w.shape[1] // share, 0, 1)]
    move_pieces(sizes, me_ref, stacks, parts, sem, True, placed=True)


def load_ff(sizes, me_ref, refs, stacked, wholes, sems):
    if stacked:
        for i, part in enumerate(ff_parts(sizes, refs[0].shape[1], *wholes)):
            move_pieces(sizes, me_ref, refs, [part], sems.at[i], True)
    else:
        for i, (ref, whole) in enumerate(zip(refs, wholes)):
            pltpu.make_async_copy(ref, whole, sems.at[i]).start()


def ff_parts(sizes, rows, out_w, in_w, down_w):
    share = sizes["y"] * sizes["c"]
    oc, ic, dc = out_w.shape[1] // share, in_w.shape[1] // share, down_w.shape[1] // share
    folds = down_w.shape[0] // out_w.shape[0]
    return [
        (out_w, rows, oc, 0, 1),
        (in_w, rows, ic, oc, 1),
        (down_w, rows * folds, dc, oc + ic, folds),
    ]


def unpack_small(small_s, route_cols, experts_rows):
    share, d, _ = small_s.shape
    i0 = lax.broadcasted_iota(jnp.int32, (8, LANES), 0)
    i1 = lax.broadcasted_iota(jnp.int32, (8, LANES), 1)
    gb = mm((i1 == i0 + route_cols).astype(BF16), small_s[0], NT)
    route = None
    for e in range(share):
        i0 = lax.broadcasted_iota(jnp.int32, (experts_rows, LANES), 0)
        i1 = lax.broadcasted_iota(jnp.int32, (experts_rows, LANES), 1)
        pick = ((i0 - e * route_cols == i1) & (i1 < route_cols)).astype(BF16)
        part = mm(pick, small_s[e], NT)
        route = part if route is None else route + part
    return gb, route.astype(BF16)


def attend_kernel(sizes, stacked, route_cols, me_ref, tok_ref, cols_ref, rows_ref, *rest):
    if not stacked:
        gb_in, rest = rest[0], rest[1:]
    n_w = 3 if stacked else 1
    w_refs = rest[:n_w]
    rest = rest[n_w:]
    qkv_ref, att_ref = rest[:2]
    d = tok_ref.shape[1]
    if stacked:
        gb_ref, route_ref, qkv_w, small_s, sems = rest[2:]
        first = qkv_w.shape[1] // (sizes["y"] * sizes["c"])
        stacks = [ref.at[i] for ref in w_refs for i in range(ref.shape[0])]
        move_pieces(sizes, me_ref, stacks, [(small_s, w_refs[0].shape[2], LANES, first, 1)], sems.at[1], True, placed=True)
        load_qkv(sizes, me_ref, w_refs, qkv_w, sems.at[0])
        wait_all(small_s, sems.at[1])
        gb, route = unpack_small(small_s, route_cols, route_ref.shape[0])
        gb_ref[...] = gb
        route_ref[...] = route
    else:
        qkv_w, sems = rest[2:]
        load_qkv(sizes, me_ref, w_refs, qkv_w, sems.at[0])
        gb = gb_in[...]
    xhat, _ = norm_parts(tok_ref[...].astype(F32))
    n1 = (xhat * gb[0:1, :] + gb[3:4, :]).astype(BF16)
    wait_all(qkv_w, sems.at[0])
    for j in range(3):
        qkv_ref[:, j * d : (j + 1) * d] = mm(n1, qkv_w[:, j * d : (j + 1) * d]).astype(BF16)
    qkv_ref.send()
    qkv_ref = qkv_ref.buffer
    low_half = lax.broadcasted_iota(jnp.int32, (MAXLEN, LANES), 1) < HEAD_DIM
    for q0, k0, k1 in head_blocks(tok_ref.shape[0]):
        mask = same_sentence(cols_ref, rows_ref, q0, k0, k1)
        for p in range(d // LANES):
            at = lambda j: slice(j * d + p * LANES, j * d + (p + 1) * LANES)
            q2 = two_heads(qkv_ref[q0 : q0 + MAXLEN, at(0)], low_half)
            prob = probabilities(q2, qkv_ref[k0:k1, at(1)], mask).astype(BF16)
            out = mm(prob, qkv_ref[k0:k1, at(2)])
            att_ref[q0 : q0 + MAXLEN, at(0)] = pick_heads(out, low_half).astype(BF16)


def probs_kernel(cols_ref, rows_ref, qkv_ref, *prob_refs):
    d = qkv_ref.shape[1] // 3
    low_half = lax.broadcasted_iota(jnp.int32, (MAXLEN, LANES), 1) < HEAD_DIM
    n = len(prob_refs) // 2
    for prob_ref, (q0, k0, k1) in zip(zip(prob_refs[:n], prob_refs[n:]), head_blocks(qkv_ref.shape[0])):
        mask = same_sentence(cols_ref, rows_ref, q0, k0, k1)
        pairs = d // LANES
        for p in range(pairs):
            lanes = slice(p * LANES, (p + 1) * LANES)
            q2 = two_heads(qkv_ref[q0 : q0 + MAXLEN, lanes], low_half)
            prob = probabilities(q2, qkv_ref[k0:k1, d + p * LANES : d + (p + 1) * LANES], mask)
            prob_ref[2 * p // pairs][2 * p % pairs // 2] = prob
        for ref in prob_ref:
            ref.send()


def attend_back_blocks(pairs, prob_refs, qkv_ref, atg_ref, dq_s, dk_s, dv_s):
    toks, d = atg_ref.shape
    scale = 1.0 / math.sqrt(HEAD_DIM)
    dk_s[...] = jnp.zeros_like(dk_s)
    dv_s[...] = jnp.zeros_like(dv_s)
    low_half = lax.broadcasted_iota(jnp.int32, (MAXLEN, LANES), 1) < HEAD_DIM
    for prob_ref, (q0, k0, k1) in zip(prob_refs, head_blocks(toks)):
        for i, p in enumerate(pairs):
            at = lambda j: slice(j * d + p * LANES, j * d + (p + 1) * LANES)
            lanes = slice(i * LANES, (i + 1) * LANES)
            q2 = two_heads(qkv_ref[q0 : q0 + MAXLEN, at(0)], low_half)
            keys, values = qkv_ref[k0:k1, at(1)], qkv_ref[k0:k1, at(2)]
            prob = prob_ref[i]
            a2 = two_heads(atg_ref[q0 : q0 + MAXLEN, at(0)], low_half)
            prob_grad = mm(a2, values, NT)
            dv_s[k0:k1, lanes] += mm(prob.astype(BF16), a2, TN)
            inner = jnp.sum(prob_grad * prob, axis=-1, keepdims=True)
            score_grad = (prob * (prob_grad - inner)).astype(BF16)
            dq_s[q0 : q0 + MAXLEN, lanes] = pick_heads(mm(score_grad, keys), low_half)
            dk_s[k0:k1, lanes] += mm(score_grad, q2, TN)
    return [
        (dq_s[...] * scale).astype(BF16),
        (dk_s[...] * scale).astype(BF16),
        dv_s[...].astype(BF16),
    ]


def attend_back_first_kernel(n_prob, *refs):
    prob_refs = refs[:n_prob]
    qkv_ref, atg_ref, out_ref, dq_s, dk_s, dv_s = refs[n_prob:]
    pairs = range(out_ref.shape[2] // LANES)
    grads = attend_back_blocks(pairs, prob_refs, qkv_ref, atg_ref, dq_s, dk_s, dv_s)
    for j in range(3):
        out_ref[j] = grads[j]


def attend_back_kernel(sizes, stacked, n_prob, me_ref, tok_ref, gb_ref, *rest):
    prob_refs = rest[:n_prob]
    qkv_ref, atg_ref, ag_ref, first_ref = rest[n_prob : n_prob + 4]
    rest = rest[n_prob + 4 :]
    n_w = 3 if stacked else 1
    w_refs = rest[:n_w]
    gtok_ref = rest[n_w]
    g_refs = rest[n_w + 1 : -7]
    qkv_w, dq_s, dk_s, dv_s, gqkv_s, small_s, sems = rest[-7:]
    load_qkv(sizes, me_ref, w_refs, qkv_w, sems.at[0])
    d = tok_ref.shape[1]
    pairs = range(first_ref.shape[2] // LANES, d // LANES)
    grads = attend_back_blocks(pairs, prob_refs, qkv_ref, atg_ref, dq_s, dk_s, dv_s)
    grads = [jnp.concatenate([first_ref[j], grads[j]], axis=1) for j in range(3)]
    xhat, r = norm_parts(tok_ref[...].astype(F32))
    n1 = (xhat * gb_ref[0:1, :] + gb_ref[3:4, :]).astype(BF16)
    rows, cols = g_refs[0].shape[1], 3 * d // (sizes["y"] * sizes["c"])
    for j in range(3):
        gqkv_s[:, j * d : (j + 1) * d] = mm(n1, grads[j], TN).astype(BF16)
    if stacked:
        move_pieces(sizes, me_ref, g_refs, [(gqkv_s, rows, cols, 0, 1)], sems.at[1], False)
    else:
        pltpu.make_async_copy(gqkv_s, g_refs[0], sems.at[1]).start()
    wait_all(qkv_w, sems.at[0])
    n1_grad = sum(mm(grads[j], qkv_w[:, j * d : (j + 1) * d], NT) for j in range(3))
    dv, gain, bias = norm_back(xhat, r, gb_ref[0:1, :], n1_grad)
    small_s[...] = as_columns([gain, bias]).astype(BF16)
    if stacked:
        move_pieces(sizes, me_ref, g_refs, [(small_s, rows, LANES, cols, 1)], sems.at[1], False)
    else:
        pltpu.make_async_copy(small_s, g_refs[1], sems.at[1]).start()
    gtok_ref[...] = ag_ref[...] + dv
    for ref in g_refs:
        wait_all(ref, sems.at[1])


def as_columns(rows):
    n = len(rows)
    block = jnp.concatenate(rows + [jnp.zeros((16 - n, rows[0].shape[1]), F32)], axis=0).astype(BF16)
    i0 = lax.broadcasted_iota(jnp.int32, (16, LANES), 0)
    i1 = lax.broadcasted_iota(jnp.int32, (16, LANES), 1)
    return mm(block, (i0 == i1).astype(BF16), TN)


def feed_kernel(sizes, stacked, me_ref, tok_ref, att_ref, gb_ref, cols_ref, rows_ref, route_ref, cot_ref, *rest):
    n_w = len(OFFSETS) if stacked else 3
    w_refs = rest[:n_w]
    rest = rest[n_w:]
    after_ref, two_ref, gate_ref, send_ref = rest[:4]
    x_s, g_s, send_sems = rest[-3:]
    rest = rest[:-3]
    out_w, in_w, down_w, sems = rest[-4:]
    load_ff(sizes, me_ref, w_refs, stacked, (out_w, in_w, down_w), sems)
    ff = in_w.shape[1]
    toks, d = tok_ref.shape
    wait_all(out_w, sems.at[0])
    after = tok_ref[...].astype(F32) + mm(att_ref[...], out_w[...])
    after_ref[...] = after
    after_ref.send()
    xhat, _ = norm_parts(after)
    n2 = (xhat * gb_ref[1:2, :] + gb_ref[4:5, :]).astype(BF16)
    wait_all(in_w, sems.at[1])
    step = 512
    total = None
    for j in range(ff // step):
        hidden = gelu(mm(n2, in_w[:, j * step : (j + 1) * step])).astype(BF16)
        if j == 0:
            wait_all(down_w, sems.at[2])
        part = mm(hidden, down_w[j * step : (j + 1) * step, :])
        total = part if total is None else total + part
    layer_two = after + total
    two_ref[...] = layer_two
    two_ref.send()
    xhat, _ = norm_parts(layer_two)
    n3 = (xhat * gb_ref[2:3, :] + gb_ref[5:6, :]).astype(BF16)
    logits = mm(n3, route_ref[...], NT)
    lane = lax.broadcasted_iota(jnp.int32, logits.shape, 1)
    chosen = [
        jnp.sum(jnp.where(lane == cols_ref[:, c + 1 : c + 2], logits, 0.0), axis=1, keepdims=True)
        for c in range(2)
    ]
    peak = jnp.maximum(chosen[0], chosen[1])
    exps = [jnp.exp(v - peak) for v in chosen]
    gates = [v / (exps[0] + exps[1]) for v in exps]
    lane = lax.broadcasted_iota(jnp.int32, gate_ref.shape, 1)
    gate_ref[...] = jnp.where(lane == 0, gates[0], jnp.where(lane == 1, gates[1], 0.0))
    upstream = cot_ref[...].astype(F32)
    row_grads = [(gates[c] * upstream).astype(BF16) for c in range(2)]
    experts, cap, _ = x_s.shape
    chunk = min(512, experts * cap)
    per = chunk // cap
    sends = [pltpu.make_async_copy(v, send_ref.at[:, i], send_sems.at[i]) for i, v in enumerate((x_s, g_s))]
    hots = []
    for j in range(experts * cap // chunk):
        slot = lax.broadcasted_iota(jnp.int32, (chunk, toks), 0) + j * chunk
        hots.append([(slot == rows_ref[c + 1 : c + 2, :]).astype(BF16) for c in range(2)])
        x_s[j * per : (j + 1) * per] = mm(hots[-1][0] + hots[-1][1], n3).astype(BF16).reshape(per, cap, x_s.shape[2])
    sends[0].start()
    for j, hot in enumerate(hots):
        rows = (mm(hot[0], row_grads[0]) + mm(hot[1], row_grads[1])).astype(BF16)
        g_s[j * per : (j + 1) * per] = rows.reshape(per, cap, g_s.shape[2])
    sends[1].start()
    for copy in sends:
        copy.wait()


def hidden_kernel(sizes, stacked, me_ref, after_ref, gb_ref, *rest):
    n_w = len(OFFSETS) if stacked else 1
    w_refs = rest[:n_w]
    hid_ref, slope_ref, in_w, sems = rest[n_w:]
    d, ff = in_w.shape
    if stacked:
        oc = d // (sizes["y"] * sizes["c"])
        parts = [(in_w, w_refs[0].shape[1], ff // (sizes["y"] * sizes["c"]), oc, 1)]
        move_pieces(sizes, me_ref, w_refs, parts, sems.at[0], True)
    else:
        pltpu.make_async_copy(w_refs[0], in_w, sems.at[0]).start()
    xhat, _ = norm_parts(after_ref[...])
    n2 = (xhat * gb_ref[1:2, :] + gb_ref[4:5, :]).astype(BF16)
    wait_all(in_w, sems.at[0])
    step = 512

    @pl.loop(0, ff // step)
    def _(j):
        hidden, slope = gelu_both(mm(n2, in_w[:, pl.ds(pl.multiple_of(j * step, step), step)]))
        hid_ref.buffer[j] = hidden.astype(BF16)
        hid_ref.part(j)
        slope_ref.buffer[j] = slope
        slope_ref.part(j)


def feed_back_kernel(sizes, stacked, me_ref, cols_ref, cot_ref, gate_ref, two_ref, gb_ref, route_ref, after_ref, hid_ref, slope_ref, att_ref, back_ref, *rest):
    n_w = len(OFFSETS) if stacked else 3
    w_refs = rest[:n_w]
    rest = rest[n_w:]
    lout_ref, ag_ref, atg_ref = rest[:3]
    g_refs = rest[3:-12]
    out_w, in_w, down_w, gout_s, gin_s, gdown_s, small_s, res_s, ing_s, back_sems, wait_sem, sems = rest[-12:]
    gets = [pltpu.make_async_copy(back_ref.at[:, i], v, back_sems.at[i]) for i, v in enumerate((res_s, ing_s))]
    for copy in gets:
        copy.start()
    load_ff(sizes, me_ref, w_refs, stacked, (out_w, in_w, down_w), wait_sem)
    toks, d = after_ref.shape
    ff = in_w.shape[1]
    experts, cap, _ = res_s.shape
    slots = experts * cap
    slot = lax.broadcasted_iota(jnp.int32, (toks, slots), 1)
    hot = [(slot == cols_ref[:, c + 3 : c + 4]).astype(BF16) for c in range(2)]
    gates = [gate_ref[:, c : c + 1] for c in range(2)]
    upstream = cot_ref[...].astype(F32)
    layer_two = two_ref[...]
    xhat3, r3 = norm_parts(layer_two)
    n3 = (xhat3 * gb_ref[2:3, :] + gb_ref[5:6, :]).astype(BF16)
    gets[0].wait()
    results = res_s[...].reshape(slots, d)
    picked = [mm(hot[c], results) for c in range(2)]
    lout_ref[...] = (layer_two + gates[0] * picked[0] + gates[1] * picked[1]).astype(BF16)
    lout_ref.send()
    gate_grad = [jnp.sum(upstream * v, axis=1, keepdims=True) for v in picked]
    mean = gates[0] * gate_grad[0] + gates[1] * gate_grad[1]
    lane = lax.broadcasted_iota(jnp.int32, (toks, LANES), 1)
    logit_grad = sum(
        jnp.where(lane == cols_ref[:, c + 1 : c + 2], gates[c] * (gate_grad[c] - mean), 0.0) for c in range(2)
    ).astype(BF16)
    grad_route = mm(n3, logit_grad, TN)
    gets[1].wait()
    three_grad = mm(hot[0] + hot[1], ing_s[...].reshape(slots, d)) + mm(logit_grad, route_ref[...])
    dv, gain3, bias3 = norm_back(xhat3, r3, gb_ref[2:3, :], three_grad)
    two_grad = upstream + dv
    ffn_grad = two_grad.astype(BF16)
    xhat, r = norm_parts(after_ref[...])
    n2 = (xhat * gb_ref[1:2, :] + gb_ref[4:5, :]).astype(BF16)
    wait_all(down_w, wait_sem.at[2])
    wait_all(in_w, wait_sem.at[1])
    step = 512
    hid_s, slope_s, n2_grad = hid_ref.ready(), slope_ref.ready(), ag_ref.buffer
    n2_grad[...] = jnp.zeros_like(n2_grad)

    @pl.loop(0, ff // step)
    def _(j):
        at = pl.ds(pl.multiple_of(j * step, step), step)
        gdown_s[at, :] = mm(hid_s[j], ffn_grad, TN).astype(BF16)
        pre_grad = (mm(ffn_grad, down_w[at, :], NT) * slope_s[j]).astype(BF16)
        gin_s[:, at] = mm(n2, pre_grad, TN).astype(BF16)
        n2_grad[...] += mm(pre_grad, in_w[:, at], NT)

    if stacked:
        _, rows, width = g_refs[0].shape
        parts = ff_parts(sizes, rows, gout_s, gin_s, gdown_s)
        move_pieces(sizes, me_ref, g_refs, parts[1:], sems.at[0], False)
    else:
        for src, dst in zip((gin_s, gdown_s), g_refs[1:3]):
            pltpu.make_async_copy(src, dst, sems.at[0]).start()
    dv, gain2, bias2 = norm_back(xhat, r, gb_ref[1:2, :], n2_grad[...])
    after_grad = two_grad + dv
    ag_ref[...] = after_grad
    ag_ref.send()
    attn_grad = after_grad.astype(BF16)
    gout_s[...] = mm(att_ref[...], attn_grad, TN).astype(BF16)
    lanes = lax.broadcasted_iota(jnp.int32, (16, LANES), 1)
    lanes = lanes - lax.broadcasted_iota(jnp.int32, (16, LANES), 0)
    norms = jnp.concatenate([gain2, gain3, bias2, bias3, jnp.zeros((12, d), F32)], axis=0).astype(BF16)
    n_route = route_columns(sizes)
    small_s[...] = (grad_route + mm(norms, (lanes == n_route).astype(BF16), TN)).astype(BF16)
    if stacked:
        parts = [parts[0], (small_s, rows, LANES, width - LANES, 1)]
        move_pieces(sizes, me_ref, g_refs, parts, sems.at[0], False)
    else:
        for src, dst in zip((gout_s, small_s), (g_refs[0], g_refs[3])):
            pltpu.make_async_copy(src, dst, sems.at[0]).start()
    wait_all(out_w, wait_sem.at[0])
    atg_ref[...] = mm(attn_grad, out_w[...], NT).astype(BF16)
    for ref in g_refs:
        wait_all(ref, sems.at[0])


def route_columns(sizes):
    return sizes["y"] * sizes["c"] * sizes["x"]


def gate_kernel(*refs):
    refs[-1][...] = jnp.zeros_like(refs[-1])


def expert_kernel(n_ring, gate_ref, recv_ref, *rest):
    w_refs = rest[:n_ring]
    ret_ref = rest[n_ring]
    hid_ref, pg_ref, x_s, g_s, up_s, down_s, acc_s, gacc_s, sems, w_sems = rest[n_ring + 1 :]
    gets = [pltpu.make_async_copy(recv_ref.at[:, i], v, sems.at[i]) for i, v in enumerate((x_s, g_s))]
    gets[0].start()
    per, _, f = w_refs[0].shape
    n_src, cap, d = x_s.shape
    for s in range(n_ring):
        for k in range(per):
            piece = w_refs[s].at[k]
            cols = pl.ds(k * f, f)
            pltpu.make_async_copy(piece.at[pl.ds(0, d), :], up_s.at[s, :, cols], w_sems.at[s]).start()
            for b in range(d // f):
                part = piece.at[pl.ds(d + b * f, f), :]
                pltpu.make_async_copy(part, down_s.at[s, cols, pl.ds(b * f, f)], w_sems.at[s]).start()
        if s == 0:
            gets[1].start()
    rows = n_src * cap
    step = min(512, rows)
    blocks = [(slice(j, j + step), slice(j // cap, (j + step) // cap)) for j in range(0, rows, step)]
    for copy in gets:
        copy.wait()
    acc_s[...] = jnp.zeros_like(acc_s)
    gacc_s[...] = jnp.zeros_like(gacc_s)
    hid_s, pg_s = hid_ref.buffer, pg_ref.buffer

    @pl.loop(0, n_ring)
    def _(s):
        wait_all(up_s.at[s], w_sems.at[s])
        wait_all(down_s.at[s], w_sems.at[s])
        for at, src in blocks:
            x = x_s[src].reshape(step, d)
            hidden, slope = gelu_both(mm(x, up_s[s]))
            hidden = hidden.astype(BF16)
            hid_s[s, at, :] = hidden
            acc_s[at, :] += mm(hidden, down_s[s])
            pre_grad = (mm(g_s[src].reshape(step, d), down_s[s], NT) * slope).astype(BF16)
            pg_s[s, at, :] = pre_grad
            gacc_s[at, :] += mm(pre_grad, up_s[s], NT)
        hid_ref.part(s)
        pg_ref.part(s)

    x_s[...] = acc_s[...].astype(BF16).reshape(x_s.shape)
    g_s[...] = gacc_s[...].astype(BF16).reshape(g_s.shape)
    puts = [pltpu.make_async_copy(v, ret_ref.at[:, i], sems.at[i]) for i, v in enumerate((x_s, g_s))]
    for copy in puts:
        copy.start()
    for copy in puts:
        copy.wait()


def expert_grad_kernel(places, recv_ref, hid_ref, pg_ref, *refs):
    n = len(places)
    out_refs = refs[:n]
    x_s, g_s, hid_s, pg_s, out_s, sems, block_sems, out_sem = refs[n:]
    gets = [pltpu.make_async_copy(recv_ref.at[:, i], v, sems.at[i]) for i, v in enumerate((x_s, g_s))]
    for copy in gets:
        copy.start()
    for s, place in enumerate(places):
        for ref, v in ((pg_ref, pg_s), (hid_ref, hid_s)):
            pltpu.make_async_copy(ref.at[place], v.at[s], block_sems.at[s]).start()
    n_src, cap, d = x_s.shape
    rows = n_src * cap
    _, per, _, f = out_s.shape
    for copy in gets:
        copy.wait()

    @pl.loop(0, n)
    def _(s):
        wait_all(pg_s.at[s], block_sems.at[s])
        wait_all(hid_s.at[s], block_sems.at[s])
        up = mm(x_s[...].reshape(rows, d), pg_s[s], TN).astype(BF16)
        down = mm(hid_s[s], g_s[...].reshape(rows, d), TN).astype(BF16)
        for k in range(per):
            cols = slice(k * f, (k + 1) * f)
            out_s[s, k, 0:d, :] = up[:, cols]
            for b in range(d // f):
                out_s[s, k, d + b * f : d + (b + 1) * f, :] = down[cols, b * f : (b + 1) * f]

    puts = [pltpu.make_async_copy(out_s.at[s], ref, out_sem.at[s]) for s, ref in enumerate(out_refs)]
    for copy in puts:
        copy.start()
    for copy in puts:
        copy.wait()


def local(sizes, tokens, lengths, task_ids, expert_table, norm_gain, norm_bias, w_qkv, w_out, w_in, w_down, w_router, expert_up, expert_down, cotangent):
    toks, d = tokens.shape
    local_experts, _, f = expert_up.shape
    assert local_experts == sizes["x"] == 2
    share = sizes["y"] * sizes["c"]
    n_hid = sizes["z"] * sizes["x"]
    experts = share * local_experts
    capacity = 2 * toks // experts
    slots = experts * capacity
    ff = w_in.shape[1] * share
    rc = w_router.shape[1]
    rows_dev = d // n_hid
    n_ring = sizes["z"]
    ring = [(i, (i + 1) % n_ring) for i in range(n_ring)]
    down = [(j, i) for i, j in ring]
    n_up = n_ring // 2
    n_down = n_ring - 1 - n_up
    stacked = sizes["y"] == sizes["c"] == 2 and all(
        w.shape[1] % LANES == 0 for w in (w_qkv, w_out, w_in, w_down)
    )

    def after(v, *others):
        return lax.optimization_barrier((v,) + others)[0]

    def swap(v, axis, by=1):
        n = math.prod(sizes[a] for a in axis)
        return lax.ppermute(v, axis, [(i, i ^ by) for i in range(n)])

    def gather_z(piece):
        return [piece] + [swap(piece, ("z",), by) for by in range(1, n_ring)]

    def plane_swaps(stacks):
        return [swap(stacks[by], ("y", "x"), by) for by in range(1, len(PLANE))]

    def other_core(stacks):
        return [swap(t, ("c",)) for t in stacks]

    def add_core(near, far, name, placed=False):
        n, shape = len(PLANE), near[0].shape
        outs = [sds((n,) + shape, BF16)] if placed else [sds(shape, F32)] + [sds(shape, BF16)] * (n - 1)
        return call(
            functools.partial(sum_cores_kernel, placed),
            name,
            K[name],
            outs,
            [smem()] + ["late"] * (2 * n),
            [anywhere()] if placed else ["early"] * n,
            [pltpu.VMEM((n,) + shape, BF16), dma((n,))] if placed else [],
        )(me, *[v for v in near[:n]], *far)

    def add_plane(mine, got):
        total = sum((v.astype(F32) for v in got), mine)
        return total[0], total[1:].astype(BF16)

    def z_swaps(parts):
        return [swap(parts[by - 1], ("z",), by) for by in range(1, n_ring)]

    def add_z(mine, got):
        return sum((v.astype(F32) for v in got), mine)

    def exchange(v):
        return lax.all_to_all(v, ("y", "c", "x"), split_axis=0, concat_axis=0, tiled=True)

    def gather_whole(w):
        w = lax.all_gather(w.astype(BF16), ("y", "c"), axis=1, tiled=True)
        return lax.all_gather(w, ("z", "x"), axis=0, tiled=True)

    def reduce_whole(g):
        g = lax.psum_scatter(g.astype(F32), ("z", "x"), scatter_dimension=0, tiled=True)
        return lax.psum_scatter(g, ("y", "c"), scatter_dimension=1, tiled=True)

    def sds(shape, dtype):
        return jax.ShapeDtypeStruct(shape, dtype)

    dma = pltpu.SemaphoreType.DMA
    me = jnp.stack([lax.axis_index(a) for a in AXES]).astype(jnp.int32)
    x_at = lax.axis_index("x")

    def piece_of(at):
        up = lax.dynamic_index_in_dim(expert_up, at, 0, keepdims=False)
        down = lax.dynamic_index_in_dim(expert_down, at, 0, keepdims=False)
        return jnp.concatenate(
            [up] + [down[:, b * f : (b + 1) * f] for b in range(d // f)], axis=0
        ).astype(BF16)

    def routes(lengths):
        return find_routes(lengths, task_ids, expert_table, toks, experts, capacity)

    if stacked:
        folds = w_down.shape[0] // rows_dev
        width = w_out.shape[1] + w_in.shape[1] + folds * w_down.shape[1]
        small = jnp.concatenate([w_router, norm_gain, norm_bias], axis=1)
        small = jnp.pad(small, ((0, 0), (0, LANES - small.shape[1])))
        qkv_piece = jnp.concatenate([w_qkv, small], axis=1).astype(BF16)
        ff_piece, own, other = call(
            pack_kernel,
            "pack",
            K["pack"],
            [sds((rows_dev, width), BF16)] + [sds((2 * d, f), BF16)] * 2,
            [smem()] + ["late"] * 5,
            ["early"] * 3,
        )(me, w_out, w_in, w_down, expert_up, expert_down)
        expert_x = swap(other, ("x",))
        qkv_z = gather_z(qkv_piece)
        mine = jnp.stack(qkv_z)
        qkv_w = lax.all_to_all(jnp.stack([mine] * len(PLANE)), ("y", "x"), split_axis=0, concat_axis=0, tiled=True)
        ff_z = gather_z(after(ff_piece, *qkv_z[1:]))
        rows, cols = routes(after(lengths, *ff_z[1:]))
        qkv_w = after(qkv_w, rows)
        half = len(PLANE) // 2
        qkv_w = [qkv_w] + other_core([qkv_w[:half], qkv_w[half:]])
        blocks = [after(jnp.stack([own, expert_x]), *ff_z[1:])]
        blocks.append(lax.ppermute(blocks[0], "z", ring))
        mine = jnp.stack(ff_z)
        ffw = [mine] + plane_swaps([mine] * len(PLANE))
        tokens_in = after(tokens, rows)
        gb_in = []
    else:
        qkv_w = [gather_whole(w_qkv)]
        ffw = [gather_whole(w_out), gather_whole(w_in), gather_whole(w_down)]
        small = jnp.concatenate([w_router, norm_gain, norm_bias], axis=1)
        small = lax.all_gather(small.astype(BF16), AXES)
        route = small[:, :, :rc].reshape(share, d, rc).transpose(0, 2, 1).reshape(experts, d)
        route = jnp.pad(route, ((0, LANES - experts), (0, 0)))
        gb = small[:n_hid, :, rc:].reshape(d, 6).T.astype(F32)
        gb = jnp.pad(gb, ((0, 2), (0, 0)))
        gb_in = [gb]
        tokens_in = tokens
        rows, cols = routes(lengths)
        blocks = [jnp.stack([piece_of(x_at), swap(piece_of(1 - x_at), ("x",))])]
        blocks.append(lax.ppermute(blocks[0], "z", ring))

    out_shape = [sds((toks, 3 * d), BF16), sds((toks, d), BF16)]
    scratch = [pltpu.VMEM((d, 3 * d), BF16)]
    if stacked:
        out_shape += [sds((8, d), F32), sds((LANES, d), BF16)]
        scratch += [pltpu.VMEM((share, d, LANES), BF16)]
    out = call(
        functools.partial(attend_kernel, sizes, stacked, rc),
        "attend",
        K["attend"],
        out_shape,
        [smem()] + ["late"] * 3 + [vmem()] * len(gb_in) + [anywhere()] * len(qkv_w),
        ["early"] * 2 + [vmem()] * (len(out_shape) - 2),
        scratch + [dma((2,))],
    )(me, tokens_in, cols, rows, *gb_in, *qkv_w)
    qkv, attended = out[:2]
    if stacked:
        gb, route = out[2:]
        ffw = [ffw[0]] + [after(t, attended, *(blocks[-1:] if K["ringff"] else [])) for t in ffw[1:]]
        ffw = ffw + other_core(ffw)
    ups, downs = blocks, [blocks[0]]
    while len(ups) <= n_up:
        ups.append(lax.ppermute(after(ups[-1], attended), "z", ring))
    while len(downs) <= n_down:
        downs.append(lax.ppermute(after(downs[-1], attended), "z", down))
    blocks = ups + downs[:0:-1]

    f_scratch = [pltpu.VMEM((d, d), BF16), pltpu.VMEM((d, ff), BF16), pltpu.VMEM((ff, d), BF16)]
    pair = [pltpu.VMEM((experts, capacity, d), BF16)] * 2
    after_attn, layer_two, gates, send = call(
        functools.partial(feed_kernel, sizes, stacked),
        "feed",
        K["feed"],
        [sds((toks, d), F32), sds((toks, d), F32), sds((toks, LANES), F32)]
        + [sds((experts, 2, capacity, d), BF16)],
        [smem()] + ["late"] * 2 + [vmem()] + ["late"] * 4 + [anywhere()] * len(ffw),
        ["early"] * 3 + [anywhere()],
        f_scratch + [dma((3,))] + pair + [dma((2,))],
    )(me, tokens, attended, gb, cols, rows, route, cotangent, *ffw)
    recv = exchange(send)
    gate = call(gate_kernel, "gate", K["gate"], sds((8, LANES), F32), [anywhere()] * (n_ring - 1), vmem())(*blocks[1:])
    block = [sds((n_ring, slots, 2 * f), BF16)]
    out = call(
        functools.partial(expert_kernel, n_ring),
        "experts",
        K["experts"],
        [sds(recv.shape, BF16)] + block * 2,
        [anywhere()] * (2 + n_ring),
        [anywhere()] + ["early"] * 2,
        pair
        + [pltpu.VMEM((n_ring, d, 2 * f), BF16), pltpu.VMEM((n_ring, 2 * f, d), BF16)]
        + [pltpu.VMEM((slots, d), F32)] * 2
        + [dma((2,)), dma((n_ring,))],
    )(gate, recv, *blocks)
    hids, pre_grads = out[1:]
    back = exchange(out[0])

    def expert_grads(places, recv):
        n = len(places)
        blocks = [pltpu.VMEM((n, slots, 2 * f), BF16)] * 2 + [pltpu.VMEM((n, 2, 2 * d, f), BF16)]
        return call(
            functools.partial(expert_grad_kernel, places),
            "expert_grads",
            K["expert_grads"] * n,
            [sds((2, 2 * d, f), BF16)] * n,
            [anywhere()] * 3,
            [anywhere()] * n,
            pair + blocks + [dma((2,)), dma((n,)), dma((n,))],
        )(recv, hids, pre_grads)

    far_grads = expert_grads([1], recv)
    moving = lax.ppermute(far_grads[0], "z", ring)
    rest = expert_grads([s % n_ring for s in range(2, n_ring + 1)], after(recv, far_grads[0]))
    prob_shapes = [sds((d // LANES // 2, 2 * MAXLEN, k1 - k0), F32) for _, k0, k1 in head_blocks(toks)] * 2
    probs = call(
        probs_kernel, "probs", K["probs"], prob_shapes, [vmem()] * 3, ["early"] * len(prob_shapes)
    )(cols, rows, after(qkv, rest[0]))
    hidden, slope = call(
        functools.partial(hidden_kernel, sizes, stacked),
        "hidden",
        K["hidden"],
        [sds((ff // 512, toks, 512), BF16), sds((ff // 512, toks, 512), F32)],
        [smem()] + [vmem()] * 2 + [anywhere()] * (len(OFFSETS) if stacked else 1),
        ["early"] * 2,
        [pltpu.VMEM((d, ff), BF16), dma((1,))],
    )(me, after(after_attn, rest[0]), gb, *(ffw if stacked else ffw[1:2]))

    if stacked:
        ff_cols, qkv_cols = ffw[0].shape[-1] + LANES, qkv_w[0].shape[-1]
        ff_out = [sds((n_ring, rows_dev, ff_cols), BF16)] * len(OFFSETS)
        qkv_out = [sds((n_ring, rows_dev, qkv_cols), BF16)] * len(OFFSETS)
    else:
        ff_out = [sds((d, d), BF16), sds((d, ff), BF16), sds((ff, d), BF16), sds((d, LANES), BF16)]
        qkv_out = [sds((d, 3 * d), BF16), sds((d, LANES), BF16)]
    out = call(
        functools.partial(feed_back_kernel, sizes, stacked),
        "feed_back",
        K["feed_back"],
        [sds((toks, d), BF16), sds((toks, d), F32), sds((toks, d), BF16)] + ff_out,
        [smem()] + ["late"] * 4 + [vmem()] + ["late"] * 5 + [anywhere()] * (1 + len(ffw)),
        ["early"] * 3 + [anywhere()] * len(ff_out),
        f_scratch + f_scratch + [pltpu.VMEM((d, LANES), BF16)] + pair + [dma((2,)), dma((3,)), dma((1,))],
    )(me, cols, cotangent, gates, layer_two, gb, route, after_attn, hidden, slope, attended, after(back, probs[0]), *ffw)
    layer_out, after_grad, att_grad = out[:3]
    ff_grads = out[3:]
    step = n_ring - 2

    def add_on(moving, mine, weight):
        n, shape = 4, (4, mine.shape[0] * mine.shape[1] // 4, mine.shape[2])
        scratch = [pltpu.VMEM(shape, BF16)] * 3 + [dma((3, n))]
        return call(add_kernel, "add", weight, sds(mine.shape, BF16), [anywhere()] * 2, anywhere(), scratch)(moving, mine)

    for t in range(step - 1):
        if K["tie_ring1"]:
            moving = after(moving, after_grad)
        moving = lax.ppermute(add_on(moving, rest[t], K["add1"]), "z", ring)
    if stacked:
        ff_far = other_core(ff_grads[len(PLANE) :])
    half = d // 2
    n_prob = len(probs) // 2
    acc = [pltpu.VMEM((toks, half), F32)] * 3
    if stacked:
        ff_sums = add_core(ff_grads, ff_far, "sum_ff", True)
        ff_got = [lax.all_to_all(ff_sums[0], ("y", "x"), split_axis=0, concat_axis=0, tiled=True)]
        att_grad = after(att_grad, ff_sums[0])
    first_half = call(
        functools.partial(attend_back_first_kernel, n_prob),
        "attend_back_first",
        K["first"],
        [sds((3, toks, half), BF16)],
        ["late"] * (2 + n_prob),
        [vmem()],
        acc,
    )(*probs[:n_prob], qkv, att_grad)[0]
    att_grad = after(att_grad, first_half)
    out = call(
        functools.partial(attend_back_kernel, sizes, stacked, n_prob),
        "attend_back",
        K["attend_back"],
        [sds((toks, d), F32)] + qkv_out,
        [smem(), "late", vmem()] + ["late"] * (4 + n_prob) + [anywhere()] * len(qkv_w),
        ["early"] + [anywhere()] * len(qkv_out),
        [pltpu.VMEM((d, 3 * d), BF16)]
        + acc
        + [pltpu.VMEM((d, 3 * d), BF16), pltpu.VMEM((d, LANES), BF16), dma((2,))],
    )(me, tokens, gb, *probs[n_prob:], qkv, att_grad, after_grad, first_half, *qkv_w)
    grad_tokens = out[0]
    qkv_grads = out[1:]

    e_at = lax.axis_index("y") * sizes["c"] + lax.axis_index("c")
    if step:
        if K["tie_ring2"]:
            moving = after(moving, grad_tokens)
        moving = lax.ppermute(add_on(moving, rest[step - 1], K["add2"]), "z", ring)
    if stacked:
        qkv_sums = add_core(qkv_grads, other_core(qkv_grads[len(PLANE) :]), "sum_qkv")
        qkv_got = plane_swaps(qkv_sums)
        z_shape = (n_ring, rows_dev, ff_cols)
        ff_send = call(
            sum_plane_kernel,
            "sum_plane",
            K["sum_plane"],
            sds(z_shape, BF16),
            [smem(), vmem()],
            anywhere(),
            [pltpu.VMEM(z_shape, BF16), dma((n_ring,))],
        )(me, ff_got[0])
        qkv_got = [after(v, ff_send) for v in qkv_got]
        moving = after(moving, *qkv_got)
        ff_got = lax.all_to_all(ff_send, "z", split_axis=0, concat_axis=0, tiled=True)
        qkv_mine, qkv_parts_z = add_plane(qkv_sums[0], qkv_got)
        qkv_got = z_swaps(qkv_parts_z)
    other = swap((moving[1].astype(F32) + rest[-1][1].astype(F32)).astype(BF16), ("x",))
    grad_up, grad_edown = call(
        finish_experts_kernel,
        "finish_experts",
        K["finish"],
        [sds(expert_up.shape, F32), sds(expert_down.shape, F32)],
        [smem()] + [anywhere()] * 2 + ["late"],
        ["early"] * 2,
        [pltpu.VMEM((2 * d, f), BF16)] * 2 + [dma((2,))],
    )(me, moving, rest[-1], other)
    if stacked and K["tie_x"] == 1:
        qkv_got = [after(v, grad_up) for v in qkv_got]

    if stacked:
        shapes = [v.shape for v in (w_out, w_in, w_down, w_qkv)]
        shapes += [v.shape[::-1] for v in (w_router, norm_gain, norm_bias)]
        grad_out, grad_in, grad_down, grad_qkv, grad_router, grad_gain, grad_bias = call(
            functools.partial(finish_kernel, n_ring, rc, route_columns(sizes)),
            "finish",
            K["finish"],
            [sds(v, F32) for v in shapes],
            [smem()] + [vmem()] * (1 + n_ring),
            [vmem()] * len(shapes),
        )(e_at.reshape(1).astype(jnp.int32), ff_got, qkv_mine, *qkv_got)
        grad_router, grad_gain, grad_bias = grad_router.T, grad_gain.T, grad_bias.T
    else:
        grad_out, grad_in, grad_down = (reduce_whole(g) for g in ff_grads[:3])
        grad_qkv = reduce_whole(qkv_grads[0])
        small_ff, small_qkv = (
            lax.psum(lax.psum_scatter(g.astype(F32), ("z", "x"), scatter_dimension=0, tiled=True), ("y", "c"))
            for g in (ff_grads[3], qkv_grads[1])
        )
        grad_router = lax.dynamic_slice_in_dim(small_ff, e_at * rc, rc, axis=1)
        n_route = route_columns(sizes)
        gains, biases = small_ff[:, n_route : n_route + 2], small_ff[:, n_route + 2 : n_route + 4]
        grad_gain = jnp.concatenate([small_qkv[:, 0:1], gains], axis=1)
        grad_bias = jnp.concatenate([small_qkv[:, 1:2], biases], axis=1)
    return (
        layer_out,
        grad_tokens,
        grad_gain,
        grad_bias,
        grad_qkv,
        grad_out,
        grad_in,
        grad_down,
        grad_router,
        grad_up,
        grad_edown,
    )


def solution(mesh):
    n_exp, n_hid = mesh.shape["expert"], mesh.shape["hidden"]
    sizes = {"y": n_exp // 2, "c": 2, "z": n_hid // 2, "x": 2}
    fine = Mesh(mesh.devices.reshape(tuple(sizes[a] for a in AXES)), AXES)
    both, exp, hid = AXES, ("y", "c"), ("z", "x")
    return jax.shard_map(
        functools.partial(local, sizes),
        mesh=fine,
        in_specs=(
            P(both, None),
            P(both, None),
            P(both, None),
            P(),
            P(hid, None),
            P(hid, None),
            P(hid, exp),
            P(hid, exp),
            P(hid, exp),
            P(hid, exp),
            P(hid, exp),
            P(exp, None, hid),
            P(exp, hid, None),
            P(both, None),
        ),
        out_specs=(
            P(both, None),
            P(both, None),
            P(hid, None),
            P(hid, None),
            P(hid, exp),
            P(hid, exp),
            P(hid, exp),
            P(hid, exp),
            P(hid, exp),
            P(exp, None, hid),
            P(exp, hid, None),
        ),
        check_vma=False,
    )
```

```python
import functools
import math

import jax
import jax.numpy as jnp
from jax import lax
from jax.experimental import pallas as pl
from jax.experimental.pallas import tpu as pltpu
from jax.sharding import Mesh, PartitionSpec as P

HEAD_DIM = 64
MAXLEN = 128
LANES = 128
EPSILON = 1e-05
FILL_SCORE = -1000000000.0
AXES = ("y", "c", "z", "x")
VMEM_BYTES = 56 * 1024 * 1024
SMALL_BYTES = 24 * 1024 * 1024
GELU_A = math.sqrt(2.0 / math.pi)
GELU_B = 0.044715

F32 = jnp.float32
BF16 = jnp.bfloat16

NN = (((1,), (0,)), ((), ()))
NT = (((1,), (1,)), ((), ()))
TN = (((0,), (0,)), ((), ()))


def mm(a, b, dims=NN):
    return lax.dot_general(a, b, dims, preferred_element_type=F32)


def gelu(v):
    t = jnp.tanh(GELU_A * (v + GELU_B * (v * v * v)))
    return 0.5 * v * (1.0 + t)


def gelu_both(v):
    v2 = v * v
    t = jnp.tanh(GELU_A * (v + GELU_B * (v2 * v)))
    half = 0.5 * (1.0 + t)
    slope = half + 0.5 * v * (1.0 - t * t) * (GELU_A + (3.0 * GELU_A * GELU_B) * v2)
    return v * half, slope


def norm_parts(v):
    center = v - jnp.mean(v, axis=-1, keepdims=True)
    r = lax.rsqrt(jnp.mean(center * center, axis=-1, keepdims=True) + EPSILON)
    return center * r, r


def norm_back(xhat, r, gain, h):
    hg = h * gain
    inner = jnp.mean(hg * xhat, axis=-1, keepdims=True)
    dv = r * (hg - jnp.mean(hg, axis=-1, keepdims=True) - xhat * inner)
    return dv, jnp.sum(h * xhat, axis=0, keepdims=True), jnp.sum(h, axis=0, keepdims=True)


K = dict(scale=0.35, routes=60, attend=0.3, feed=3, probs=3, hidden=6, experts=18, expert_grads=3, feed_back=20, first=4, attend_back=9, add1=2, add2=14, sum_ff=2, sum_qkv=3, sum_plane=0.3, finish=0.3, pack=3, gate=60, ring1=1, ringff=0, tie_near=1, tie_ffz=1, x_first=0, ff_a2a=1, tie_qkv=1, tie_ring3=1, tie_ring2=1, tie_ring1=1, tie_x=1, tie_ffc=1)


def cost(us):
    return pl.CostEstimate(flops=int(K["scale"] * us * 1.15e9), bytes_accessed=0, transcendentals=0)


def vmem():
    return pl.BlockSpec(memory_space=pltpu.VMEM)


class Late:
    def __init__(self, ref, buffer, sem):
        self.buffer, self.shape, self.dtype = buffer, buffer.shape, buffer.dtype
        self.copy = pltpu.make_async_copy(ref, buffer, sem)
        self.copy.start()
        self.waited = False

    def ready(self):
        if not self.waited:
            self.copy.wait()
            self.waited = True
        return self.buffer

    finish = ready

    def __getitem__(self, at):
        return self.ready()[at]


class Early:
    def __init__(self, ref, buffer, sem):
        self.buffer, self.shape, self.dtype = buffer, buffer.shape, buffer.dtype
        self.ref, self.sem = ref, sem
        self.copy = pltpu.make_async_copy(buffer, ref, sem)
        self.sent = False

    def send(self):
        self.copy.start()
        self.sent = True

    def part(self, i):
        pltpu.make_async_copy(self.buffer.at[i], self.ref.at[i], self.sem).start()
        self.sent = True

    def finish(self):
        if not self.sent:
            self.send()
        self.copy.wait()

    def __setitem__(self, at, value):
        self.buffer[at] = value


def call(kernel, name, us, out_shape, in_specs, out_specs, scratch=(), vmem_bytes=VMEM_BYTES):
    single = not isinstance(out_shape, list)
    outs, out_specs = ([out_shape], [out_specs]) if single else (out_shape, out_specs)
    specs = list(in_specs) + list(out_specs)

    def run(*args):
        arrays = list(args) + outs
        moving = [i for i, spec in enumerate(specs) if spec in ("late", "early")]

        def body(*refs):
            refs = list(refs)
            buffers, sems = refs[len(specs) + len(scratch) : -1], refs[-1]
            for j, i in enumerate(moving):
                kind = Late if specs[i] == "late" else Early
                refs[i] = kind(refs[i], buffers[j], sems.at[j])
            kernel(*refs[: len(specs) + len(scratch)])
            for i in moving:
                refs[i].finish()

        buffers = [pltpu.VMEM(arrays[i].shape, arrays[i].dtype) for i in moving]
        places = [anywhere() if spec in ("late", "early") else spec for spec in specs]
        results = pl.pallas_call(
            body,
            out_shape=outs,
            in_specs=places[: len(in_specs)],
            out_specs=places[len(in_specs) :],
            scratch_shapes=list(scratch) + buffers + [pltpu.SemaphoreType.DMA((max(len(moving), 1),))],
            compiler_params=pltpu.CompilerParams(vmem_limit_bytes=vmem_bytes),
            cost_estimate=cost(us),
            name=name,
        )(*args)
        return results[0] if single else results

    return run


def smem():
    return pl.BlockSpec(memory_space=pltpu.SMEM)


def anywhere():
    return pl.BlockSpec(memory_space=pl.ANY)


PLANE = ((0, 0), (0, 1), (1, 0), (1, 1))
OFFSETS = tuple((c, y, x) for c in (0, 1) for y, x in PLANE)


def move_pieces(sizes, me_ref, stacks, parts, sem, inward, placed=False):
    at = {axis: me_ref[i] for i, axis in enumerate(AXES)}
    for (dc, dy, dx), stack in zip(OFFSETS, stacks):
        y = dy if placed else lax.bitwise_xor(at["y"], dy)
        x = dx if placed else lax.bitwise_xor(at["x"], dx)
        e = y * sizes["c"] + lax.bitwise_xor(at["c"], dc)

        @pl.loop(0, sizes["z"])
        def _(dz):
            h = lax.bitwise_xor(at["z"], dz) * sizes["x"] + x
            for whole, rows, cols, first, folds in parts:
                step = rows // folds
                for i in range(folds):
                    piece = stack.at[dz, :, pl.ds(first + i * cols, cols)]
                    top = pl.multiple_of(h * rows + i * step, step)
                    if len(whole.shape) == 3:
                        block = whole.at[e, pl.ds(top, step), :]
                    elif whole.shape[1] == cols:
                        block = whole.at[pl.ds(top, step), :]
                    else:
                        block = whole.at[pl.ds(top, step), pl.ds(pl.multiple_of(e * cols, cols), cols)]
                    src, dst = (piece, block) if inward else (block, piece)
                    pltpu.make_async_copy(src, dst, sem).start()


def wait_all(ref, sem):
    pltpu.make_async_copy(ref, ref, sem).wait()


def routes_kernel(capacity, experts, len_row, task_row, table, rows_out, cols_out):
    sents = len_row.shape[1]
    tasks = table.shape[0]
    toks = rows_out.shape[1]
    f = lambda v: v.astype(F32)
    i0 = lax.broadcasted_iota(jnp.int32, (sents, sents), 0)
    i1 = lax.broadcasted_iota(jnp.int32, (sents, sents), 1)
    turn = lambda row: jnp.sum(jnp.where(i0 == i1, row, 0.0), axis=1, keepdims=True)
    len_r, task_r = f(len_row[...]), f(task_row[...])
    len_c, task_c = turn(len_r), turn(task_r)
    ends_row = jnp.sum(jnp.where(i0 <= i1, len_c, 0.0), axis=0, keepdims=True)
    ends_col = jnp.sum(jnp.where(i1 <= i0, len_r, 0.0), axis=1, keepdims=True)
    starts_row = ends_row - len_r
    starts_col = ends_col - len_c
    t0 = lax.broadcasted_iota(jnp.int32, (tasks, tasks), 0)
    t1 = lax.broadcasted_iota(jnp.int32, (tasks, tasks), 1)
    table_c = [f(table[:, c : c + 1]) for c in range(2)]
    table_r = [jnp.sum(jnp.where(t0 == t1, v, 0.0), axis=0, keepdims=True) for v in table_c]
    tok = f(lax.broadcasted_iota(jnp.int32, (toks, sents), 0))
    sent = lax.broadcasted_iota(jnp.int32, (toks, sents), 1)
    hot = (tok >= starts_row) & (tok < ends_row)
    seg_c = jnp.sum(jnp.where(hot, f(sent), 0.0), axis=1, keepdims=True)
    own = jnp.sum(jnp.where(hot, task_r, 0.0), axis=1, keepdims=True)
    thot = f(lax.broadcasted_iota(jnp.int32, (toks, tasks), 1)) == own
    pair_c = [
        jnp.sum(jnp.where(thot, table_r[c], 0.0), axis=1, keepdims=True)
        for c in range(2)
    ]
    tok = f(lax.broadcasted_iota(jnp.int32, (sents, toks), 1))
    sent = lax.broadcasted_iota(jnp.int32, (sents, toks), 0)
    hot = (tok >= starts_col) & (tok < ends_col)
    seg_r = jnp.sum(jnp.where(hot, f(sent), 0.0), axis=0, keepdims=True)
    own = jnp.sum(jnp.where(hot, task_c, 0.0), axis=0, keepdims=True)
    thot = f(lax.broadcasted_iota(jnp.int32, (tasks, toks), 0)) == own
    pair_r = [
        jnp.sum(jnp.where(thot, table_c[c], 0.0), axis=0, keepdims=True)
        for c in range(2)
    ]
    a0 = lax.broadcasted_iota(jnp.int32, (toks, toks), 0)
    a1 = lax.broadcasted_iota(jnp.int32, (toks, toks), 1)
    upper = (a0 < a1).astype(BF16)
    lower = (a1 < a0).astype(BF16)
    er = f(lax.broadcasted_iota(jnp.int32, (experts, toks), 0))
    ec = f(lax.broadcasted_iota(jnp.int32, (toks, experts), 1))
    hot_r = [(er == pair_r[c]).astype(F32) for c in range(2)]
    hot_c = [(ec == pair_c[c]).astype(F32) for c in range(2)]
    before_r = [mm(hot_r[c].astype(BF16), upper) for c in range(2)]
    before_c = [mm(lower, hot_c[c].astype(BF16)) for c in range(2)]
    before_r[1] = before_r[1] + jnp.sum(hot_r[0], axis=1, keepdims=True)
    before_c[1] = before_c[1] + jnp.sum(hot_c[0], axis=0, keepdims=True)
    place = lambda pair, rank: jnp.where(rank < capacity, pair * capacity + rank, -1.0)
    slot_r = [place(pair_r[c], jnp.sum(hot_r[c] * before_r[c], axis=0, keepdims=True)) for c in range(2)]
    slot_c = [place(pair_c[c], jnp.sum(hot_c[c] * before_c[c], axis=1, keepdims=True)) for c in range(2)]
    at = lax.broadcasted_iota(jnp.int32, rows_out.shape, 0)
    rows_out[...] = jnp.where(
        at == 0, seg_r, jnp.where(at == 1, slot_r[0], slot_r[1])
    ).astype(jnp.int32)
    at = lax.broadcasted_iota(jnp.int32, cols_out.shape, 1)
    packed = jnp.where(at == 0, seg_c, 0.0)
    for j, v in enumerate((pair_c[0], pair_c[1], slot_c[0], slot_c[1])):
        packed = jnp.where(at == j + 1, v, packed)
    cols_out[...] = packed.astype(jnp.int32)


def find_routes(lengths, task_ids, expert_table, toks, experts, capacity):
    return call(
        functools.partial(routes_kernel, capacity, experts),
        "routes",
        K["routes"],
        [jax.ShapeDtypeStruct((8, toks), jnp.int32), jax.ShapeDtypeStruct((toks, 8), jnp.int32)],
        [vmem()] * 3,
        [vmem()] * 2,
    )(lengths, task_ids, expert_table)


def pack_kernel(me_ref, out_ref, in_ref, down_ref, up_ref, edown_ref, ff_out, own_out, other_out):
    d, f = up_ref.shape[1:]
    x = me_ref[AXES.index("x")]
    for out, e in ((other_out, 1 - x), (own_out, x)):
        out[0:d, :] = up_ref[e].astype(BF16)
        for b in range(d // f):
            out[d + b * f : d + (b + 1) * f, :] = edown_ref[e, :, b * f : (b + 1) * f].astype(BF16)
        out.send()
    rows, at = out_ref.shape[0], 0
    for ref in (out_ref, in_ref):
        ff_out[:, at : at + ref.shape[1]] = ref[...].astype(BF16)
        at += ref.shape[1]
    cols = down_ref.shape[1]
    for i in range(down_ref.shape[0] // rows):
        ff_out[:, at + i * cols : at + (i + 1) * cols] = down_ref[i * rows : (i + 1) * rows, :].astype(BF16)


def add_kernel(a_ref, b_ref, out_ref, a_s, b_s, out_s, sems):
    n = a_s.shape[0]
    parts = a_ref.shape[0]
    rows = a_ref.shape[1] // (n // parts)
    at = [(i // (n // parts), pl.ds(i % (n // parts) * rows, rows)) for i in range(n)]
    gets = []
    for i, (p, row) in enumerate(at):
        gets.append([pltpu.make_async_copy(ref.at[p, row, :], s.at[i], sems.at[j, i]) for j, (ref, s) in enumerate(((a_ref, a_s), (b_ref, b_s)))])
        for copy in gets[-1]:
            copy.start()
    puts = []
    for i, (p, row) in enumerate(at):
        for copy in gets[i]:
            copy.wait()
        out_s[i] = (a_s[i].astype(F32) + b_s[i].astype(F32)).astype(out_s.dtype)
        puts.append(pltpu.make_async_copy(out_s.at[i], out_ref.at[p, row, :], sems.at[2, i]))
        puts[-1].start()
    for copy in puts:
        copy.wait()


def sum_cores_kernel(placed, me_ref, *refs):
    n = len(PLANE)
    near, far, outs = refs[:n], refs[n : 2 * n], refs[2 * n :]
    if placed:
        send_ref, send_s, sems = outs
        puts = []
        for i, (dy, dx) in enumerate(PLANE):
            at = lax.bitwise_xor(me_ref[AXES.index("y")], dy) * 2 + lax.bitwise_xor(me_ref[AXES.index("x")], dx)
            send_s[i] = (near[i][...].astype(F32) + far[i][...].astype(F32)).astype(BF16)
            puts.append(pltpu.make_async_copy(send_s.at[i], send_ref.at[at], sems.at[i]))
            puts[-1].start()
        for copy in puts:
            copy.wait()
    else:
        for i in range(1, n):
            outs[i][...] = (near[i][...].astype(F32) + far[i][...].astype(F32)).astype(BF16)
        outs[0][...] = near[0][...].astype(F32) + far[0][...].astype(F32)


def sum_plane_kernel(me_ref, got_ref, send_ref, send_s, sems):
    n = got_ref.shape[1]
    puts = []
    for k in range(n):
        total = got_ref[0, k].astype(F32)
        for i in range(1, got_ref.shape[0]):
            total = total + got_ref[i, k].astype(F32)
        send_s[k] = total.astype(BF16)
        at = lax.bitwise_xor(me_ref[AXES.index("z")], k)
        puts.append(pltpu.make_async_copy(send_s.at[k], send_ref.at[at], sems.at[k]))
        puts[-1].start()
    for copy in puts:
        copy.wait()


def finish_experts_kernel(me_ref, moving_ref, mine_ref, other_ref, gup_ref, gdown_ref, a_s, b_s, sems):
    gets = [pltpu.make_async_copy(ref.at[0], v, sems.at[i]) for i, (ref, v) in enumerate(((moving_ref, a_s), (mine_ref, b_s)))]
    for copy in gets:
        copy.start()
    d, f = gup_ref.shape[1:]
    x = me_ref[AXES.index("x")]

    def put(value, e):
        gup_ref.buffer[e] = value[:d]
        gup_ref.part(e)
        for b in range(d // f):
            gdown_ref.buffer[e, :, b * f : (b + 1) * f] = value[d + b * f : d + (b + 1) * f]
        gdown_ref.part(e)

    for copy in gets:
        copy.wait()
    put(a_s[...].astype(F32) + b_s[...].astype(F32), x)
    put(other_ref[...].astype(F32), 1 - x)


def total_of(refs):
    total = refs[0][...].astype(F32)
    for v in refs[1:]:
        total = total + v[...].astype(F32)
    return total


def finish_kernel(n_z, route_cols, n_route, e_ref, *refs):
    gout_ref, gin_ref, gdown_ref, gqkv_ref, grouter_ref, ggain_ref, gbias_ref = refs[1 + n_z :]
    total = total_of([refs[0].at[k] for k in range(n_z)])
    at = 0
    for ref in (gout_ref, gin_ref):
        ref[...] = total[:, at : at + ref.shape[1]]
        at += ref.shape[1]
    rows, cols = total.shape[0], gdown_ref.shape[1]
    for i in range(gdown_ref.shape[0] // rows):
        gdown_ref[i * rows : (i + 1) * rows, :] = total[:, at : at + cols]
        at += cols
    small = total[:, at:].T
    total = total_of(refs[1 : 1 + n_z])
    cols = gqkv_ref.shape[1]
    gqkv_ref[...] = total[:, 0:cols]
    first = total[:, cols:].T
    at = lax.broadcasted_iota(jnp.int32, small.shape, 0)
    pick = lambda i: jnp.sum(jnp.where(at == i, small, 0.0), axis=0, keepdims=True)
    for j in range(route_cols):
        grouter_ref[j : j + 1, :] = pick(e_ref[0] * route_cols + j)
    for ref, i in ((ggain_ref, 0), (gbias_ref, 1)):
        ref[0:1, :] = first[i : i + 1]
        ref[1:3, :] = small[n_route + 2 * i : n_route + 2 * i + 2]


def head_blocks(toks):
    n = toks // MAXLEN
    return [(i * MAXLEN, max(i - 1, 0) * MAXLEN, min(i + 2, n) * MAXLEN) for i in range(n)]


def two_heads(block, low_half):
    zero = jnp.zeros_like(block)
    return jnp.concatenate([jnp.where(low_half, block, zero), jnp.where(low_half, zero, block)], axis=0)


def pick_heads(stacked, low_half):
    n = stacked.shape[0] // 2
    return jnp.where(low_half, stacked[:n], stacked[n:])


def probabilities(q2, keys, mask):
    scores = mm(q2, keys, NT) * (1.0 / math.sqrt(HEAD_DIM))
    scores = jnp.where(mask, scores, FILL_SCORE)
    exps = jnp.exp(scores - jnp.max(scores, axis=-1, keepdims=True))
    return exps * (1.0 / jnp.sum(exps, axis=-1, keepdims=True))


def same_sentence(cols_ref, rows_ref, q0, k0, k1):
    seg = cols_ref[q0 : q0 + MAXLEN, 0:1]
    return jnp.concatenate([seg, seg], axis=0) == rows_ref[0:1, k0:k1]


def load_qkv(sizes, me_ref, refs, qkv_w, sem):
    if len(refs) == 1:
        pltpu.make_async_copy(refs[0], qkv_w, sem).start()
        return
    share = sizes["y"] * sizes["c"]
    stacks = [ref.at[i] for ref in refs for i in range(ref.shape[0])]
    parts = [(qkv_w, refs[0].shape[2], qkv_w.shape[1] // share, 0, 1)]
    move_pieces(sizes, me_ref, stacks, parts, sem, True, placed=True)


def load_ff(sizes, me_ref, refs, stacked, wholes, sems):
    if stacked:
        for i, part in enumerate(ff_parts(sizes, refs[0].shape[1], *wholes)):
            move_pieces(sizes, me_ref, refs, [part], sems.at[i], True)
    else:
        for i, (ref, whole) in enumerate(zip(refs, wholes)):
            pltpu.make_async_copy(ref, whole, sems.at[i]).start()


def ff_parts(sizes, rows, out_w, in_w, down_w):
    share = sizes["y"] * sizes["c"]
    oc, ic, dc = out_w.shape[1] // share, in_w.shape[1] // share, down_w.shape[1] // share
    folds = down_w.shape[0] // out_w.shape[0]
    return [
        (out_w, rows, oc, 0, 1),
        (in_w, rows, ic, oc, 1),
        (down_w, rows * folds, dc, oc + ic, folds),
    ]


def unpack_small(small_s, route_cols, experts_rows):
    share, d, _ = small_s.shape
    i0 = lax.broadcasted_iota(jnp.int32, (8, LANES), 0)
    i1 = lax.broadcasted_iota(jnp.int32, (8, LANES), 1)
    gb = mm((i1 == i0 + route_cols).astype(BF16), small_s[0], NT)
    route = None
    for e in range(share):
        i0 = lax.broadcasted_iota(jnp.int32, (experts_rows, LANES), 0)
        i1 = lax.broadcasted_iota(jnp.int32, (experts_rows, LANES), 1)
        pick = ((i0 - e * route_cols == i1) & (i1 < route_cols)).astype(BF16)
        part = mm(pick, small_s[e], NT)
        route = part if route is None else route + part
    return gb, route.astype(BF16)


def attend_kernel(sizes, stacked, route_cols, me_ref, tok_ref, cols_ref, rows_ref, *rest):
    if not stacked:
        gb_in, rest = rest[0], rest[1:]
    n_w = 3 if stacked else 1
    w_refs = rest[:n_w]
    rest = rest[n_w:]
    qkv_ref, att_ref = rest[:2]
    d = tok_ref.shape[1]
    if stacked:
        gb_ref, route_ref, qkv_w, small_s, sems = rest[2:]
        first = qkv_w.shape[1] // (sizes["y"] * sizes["c"])
        stacks = [ref.at[i] for ref in w_refs for i in range(ref.shape[0])]
        move_pieces(sizes, me_ref, stacks, [(small_s, w_refs[0].shape[2], LANES, first, 1)], sems.at[1], True, placed=True)
        load_qkv(sizes, me_ref, w_refs, qkv_w, sems.at[0])
        wait_all(small_s, sems.at[1])
        gb, route = unpack_small(small_s, route_cols, route_ref.shape[0])
        gb_ref[...] = gb
        route_ref[...] = route
    else:
        qkv_w, sems = rest[2:]
        load_qkv(sizes, me_ref, w_refs, qkv_w, sems.at[0])
        gb = gb_in[...]
    xhat, _ = norm_parts(tok_ref[...].astype(F32))
    n1 = (xhat * gb[0:1, :] + gb[3:4, :]).astype(BF16)
    wait_all(qkv_w, sems.at[0])
    for j in range(3):
        qkv_ref[:, j * d : (j + 1) * d] = mm(n1, qkv_w[:, j * d : (j + 1) * d]).astype(BF16)
    qkv_ref.send()
    qkv_ref = qkv_ref.buffer
    low_half = lax.broadcasted_iota(jnp.int32, (MAXLEN, LANES), 1) < HEAD_DIM
    for q0, k0, k1 in head_blocks(tok_ref.shape[0]):
        mask = same_sentence(cols_ref, rows_ref, q0, k0, k1)
        for p in range(d // LANES):
            at = lambda j: slice(j * d + p * LANES, j * d + (p + 1) * LANES)
            q2 = two_heads(qkv_ref[q0 : q0 + MAXLEN, at(0)], low_half)
            prob = probabilities(q2, qkv_ref[k0:k1, at(1)], mask).astype(BF16)
            out = mm(prob, qkv_ref[k0:k1, at(2)])
            att_ref[q0 : q0 + MAXLEN, at(0)] = pick_heads(out, low_half).astype(BF16)


def probs_kernel(cols_ref, rows_ref, qkv_ref, *prob_refs):
    d = qkv_ref.shape[1] // 3
    low_half = lax.broadcasted_iota(jnp.int32, (MAXLEN, LANES), 1) < HEAD_DIM
    n = len(prob_refs) // 2
    for prob_ref, (q0, k0, k1) in zip(zip(prob_refs[:n], prob_refs[n:]), head_blocks(qkv_ref.shape[0])):
        mask = same_sentence(cols_ref, rows_ref, q0, k0, k1)
        pairs = d // LANES
        for p in range(pairs):
            lanes = slice(p * LANES, (p + 1) * LANES)
            q2 = two_heads(qkv_ref[q0 : q0 + MAXLEN, lanes], low_half)
            prob = probabilities(q2, qkv_ref[k0:k1, d + p * LANES : d + (p + 1) * LANES], mask)
            prob_ref[2 * p // pairs][2 * p % pairs // 2] = prob
        for ref in prob_ref:
            ref.send()


def attend_back_blocks(pairs, prob_refs, qkv_ref, atg_ref, dq_s, dk_s, dv_s):
    toks, d = atg_ref.shape
    scale = 1.0 / math.sqrt(HEAD_DIM)
    dk_s[...] = jnp.zeros_like(dk_s)
    dv_s[...] = jnp.zeros_like(dv_s)
    low_half = lax.broadcasted_iota(jnp.int32, (MAXLEN, LANES), 1) < HEAD_DIM
    for prob_ref, (q0, k0, k1) in zip(prob_refs, head_blocks(toks)):
        for i, p in enumerate(pairs):
            at = lambda j: slice(j * d + p * LANES, j * d + (p + 1) * LANES)
            lanes = slice(i * LANES, (i + 1) * LANES)
            q2 = two_heads(qkv_ref[q0 : q0 + MAXLEN, at(0)], low_half)
            keys, values = qkv_ref[k0:k1, at(1)], qkv_ref[k0:k1, at(2)]
            prob = prob_ref[i]
            a2 = two_heads(atg_ref[q0 : q0 + MAXLEN, at(0)], low_half)
            prob_grad = mm(a2, values, NT)
            dv_s[k0:k1, lanes] += mm(prob.astype(BF16), a2, TN)
            inner = jnp.sum(prob_grad * prob, axis=-1, keepdims=True)
            score_grad = (prob * (prob_grad - inner)).astype(BF16)
            dq_s[q0 : q0 + MAXLEN, lanes] = pick_heads(mm(score_grad, keys), low_half)
            dk_s[k0:k1, lanes] += mm(score_grad, q2, TN)
    return [
        (dq_s[...] * scale).astype(BF16),
        (dk_s[...] * scale).astype(BF16),
        dv_s[...].astype(BF16),
    ]


def attend_back_first_kernel(n_prob, *refs):
    prob_refs = refs[:n_prob]
    qkv_ref, atg_ref, out_ref, dq_s, dk_s, dv_s = refs[n_prob:]
    pairs = range(out_ref.shape[2] // LANES)
    grads = attend_back_blocks(pairs, prob_refs, qkv_ref, atg_ref, dq_s, dk_s, dv_s)
    for j in range(3):
        out_ref[j] = grads[j]


def attend_back_kernel(sizes, stacked, n_prob, me_ref, tok_ref, gb_ref, *rest):
    prob_refs = rest[:n_prob]
    qkv_ref, atg_ref, ag_ref, first_ref = rest[n_prob : n_prob + 4]
    rest = rest[n_prob + 4 :]
    n_w = 3 if stacked else 1
    w_refs = rest[:n_w]
    gtok_ref = rest[n_w]
    g_refs = rest[n_w + 1 : -7]
    qkv_w, dq_s, dk_s, dv_s, gqkv_s, small_s, sems = rest[-7:]
    load_qkv(sizes, me_ref, w_refs, qkv_w, sems.at[0])
    d = tok_ref.shape[1]
    pairs = range(first_ref.shape[2] // LANES, d // LANES)
    grads = attend_back_blocks(pairs, prob_refs, qkv_ref, atg_ref, dq_s, dk_s, dv_s)
    grads = [jnp.concatenate([first_ref[j], grads[j]], axis=1) for j in range(3)]
    xhat, r = norm_parts(tok_ref[...].astype(F32))
    n1 = (xhat * gb_ref[0:1, :] + gb_ref[3:4, :]).astype(BF16)
    rows, cols = g_refs[0].shape[1], 3 * d // (sizes["y"] * sizes["c"])
    for j in range(3):
        gqkv_s[:, j * d : (j + 1) * d] = mm(n1, grads[j], TN).astype(BF16)
    if stacked:
        move_pieces(sizes, me_ref, g_refs, [(gqkv_s, rows, cols, 0, 1)], sems.at[1], False)
    else:
        pltpu.make_async_copy(gqkv_s, g_refs[0], sems.at[1]).start()
    wait_all(qkv_w, sems.at[0])
    n1_grad = sum(mm(grads[j], qkv_w[:, j * d : (j + 1) * d], NT) for j in range(3))
    dv, gain, bias = norm_back(xhat, r, gb_ref[0:1, :], n1_grad)
    small_s[...] = as_columns([gain, bias]).astype(BF16)
    if stacked:
        move_pieces(sizes, me_ref, g_refs, [(small_s, rows, LANES, cols, 1)], sems.at[1], False)
    else:
        pltpu.make_async_copy(small_s, g_refs[1], sems.at[1]).start()
    gtok_ref[...] = ag_ref[...] + dv
    for ref in g_refs:
        wait_all(ref, sems.at[1])


def as_columns(rows):
    n = len(rows)
    block = jnp.concatenate(rows + [jnp.zeros((16 - n, rows[0].shape[1]), F32)], axis=0).astype(BF16)
    i0 = lax.broadcasted_iota(jnp.int32, (16, LANES), 0)
    i1 = lax.broadcasted_iota(jnp.int32, (16, LANES), 1)
    return mm(block, (i0 == i1).astype(BF16), TN)


def feed_kernel(sizes, stacked, me_ref, tok_ref, att_ref, gb_ref, cols_ref, rows_ref, route_ref, cot_ref, *rest):
    n_w = len(OFFSETS) if stacked else 3
    w_refs = rest[:n_w]
    rest = rest[n_w:]
    after_ref, two_ref, gate_ref, send_ref = rest[:4]
    x_s, g_s, send_sems = rest[-3:]
    rest = rest[:-3]
    out_w, in_w, down_w, sems = rest[-4:]
    load_ff(sizes, me_ref, w_refs, stacked, (out_w, in_w, down_w), sems)
    ff = in_w.shape[1]
    toks, d = tok_ref.shape
    wait_all(out_w, sems.at[0])
    after = tok_ref[...].astype(F32) + mm(att_ref[...], out_w[...])
    after_ref[...] = after
    after_ref.send()
    xhat, _ = norm_parts(after)
    n2 = (xhat * gb_ref[1:2, :] + gb_ref[4:5, :]).astype(BF16)
    wait_all(in_w, sems.at[1])
    step = 512
    total = None
    for j in range(ff // step):
        hidden = gelu(mm(n2, in_w[:, j * step : (j + 1) * step])).astype(BF16)
        if j == 0:
            wait_all(down_w, sems.at[2])
        part = mm(hidden, down_w[j * step : (j + 1) * step, :])
        total = part if total is None else total + part
    layer_two = after + total
    two_ref[...] = layer_two
    two_ref.send()
    xhat, _ = norm_parts(layer_two)
    n3 = (xhat * gb_ref[2:3, :] + gb_ref[5:6, :]).astype(BF16)
    logits = mm(n3, route_ref[...], NT)
    lane = lax.broadcasted_iota(jnp.int32, logits.shape, 1)
    chosen = [
        jnp.sum(jnp.where(lane == cols_ref[:, c + 1 : c + 2], logits, 0.0), axis=1, keepdims=True)
        for c in range(2)
    ]
    peak = jnp.maximum(chosen[0], chosen[1])
    exps = [jnp.exp(v - peak) for v in chosen]
    gates = [v / (exps[0] + exps[1]) for v in exps]
    lane = lax.broadcasted_iota(jnp.int32, gate_ref.shape, 1)
    gate_ref[...] = jnp.where(lane == 0, gates[0], jnp.where(lane == 1, gates[1], 0.0))
    upstream = cot_ref[...].astype(F32)
    row_grads = [(gates[c] * upstream).astype(BF16) for c in range(2)]
    experts, cap, _ = x_s.shape
    chunk = min(512, experts * cap)
    per = chunk // cap
    sends = [pltpu.make_async_copy(v, send_ref.at[:, i], send_sems.at[i]) for i, v in enumerate((x_s, g_s))]
    hots = []
    for j in range(experts * cap // chunk):
        slot = lax.broadcasted_iota(jnp.int32, (chunk, toks), 0) + j * chunk
        hots.append([(slot == rows_ref[c + 1 : c + 2, :]).astype(BF16) for c in range(2)])
        x_s[j * per : (j + 1) * per] = mm(hots[-1][0] + hots[-1][1], n3).astype(BF16).reshape(per, cap, x_s.shape[2])
    sends[0].start()
    for j, hot in enumerate(hots):
        rows = (mm(hot[0], row_grads[0]) + mm(hot[1], row_grads[1])).astype(BF16)
        g_s[j * per : (j + 1) * per] = rows.reshape(per, cap, g_s.shape[2])
    sends[1].start()
    for copy in sends:
        copy.wait()


def hidden_kernel(sizes, stacked, me_ref, after_ref, gb_ref, *rest):
    n_w = len(OFFSETS) if stacked else 1
    w_refs = rest[:n_w]
    hid_ref, slope_ref, in_w, sems = rest[n_w:]
    d, ff = in_w.shape
    if stacked:
        oc = d // (sizes["y"] * sizes["c"])
        parts = [(in_w, w_refs[0].shape[1], ff // (sizes["y"] * sizes["c"]), oc, 1)]
        move_pieces(sizes, me_ref, w_refs, parts, sems.at[0], True)
    else:
        pltpu.make_async_copy(w_refs[0], in_w, sems.at[0]).start()
    xhat, _ = norm_parts(after_ref[...])
    n2 = (xhat * gb_ref[1:2, :] + gb_ref[4:5, :]).astype(BF16)
    wait_all(in_w, sems.at[0])
    step = 512

    @pl.loop(0, ff // step)
    def _(j):
        hidden, slope = gelu_both(mm(n2, in_w[:, pl.ds(pl.multiple_of(j * step, step), step)]))
        hid_ref.buffer[j] = hidden.astype(BF16)
        hid_ref.part(j)
        slope_ref.buffer[j] = slope
        slope_ref.part(j)


def feed_back_kernel(sizes, stacked, me_ref, cols_ref, cot_ref, gate_ref, two_ref, gb_ref, route_ref, after_ref, hid_ref, slope_ref, att_ref, back_ref, *rest):
    n_w = len(OFFSETS) if stacked else 3
    w_refs = rest[:n_w]
    rest = rest[n_w:]
    lout_ref, ag_ref, atg_ref = rest[:3]
    g_refs = rest[3:-12]
    out_w, in_w, down_w, gout_s, gin_s, gdown_s, small_s, res_s, ing_s, back_sems, wait_sem, sems = rest[-12:]
    gets = [pltpu.make_async_copy(back_ref.at[:, i], v, back_sems.at[i]) for i, v in enumerate((res_s, ing_s))]
    for copy in gets:
        copy.start()
    load_ff(sizes, me_ref, w_refs, stacked, (out_w, in_w, down_w), wait_sem)
    toks, d = after_ref.shape
    ff = in_w.shape[1]
    experts, cap, _ = res_s.shape
    slots = experts * cap
    slot = lax.broadcasted_iota(jnp.int32, (toks, slots), 1)
    hot = [(slot == cols_ref[:, c + 3 : c + 4]).astype(BF16) for c in range(2)]
    gates = [gate_ref[:, c : c + 1] for c in range(2)]
    upstream = cot_ref[...].astype(F32)
    layer_two = two_ref[...]
    xhat3, r3 = norm_parts(layer_two)
    n3 = (xhat3 * gb_ref[2:3, :] + gb_ref[5:6, :]).astype(BF16)
    gets[0].wait()
    results = res_s[...].reshape(slots, d)
    picked = [mm(hot[c], results) for c in range(2)]
    lout_ref[...] = (layer_two + gates[0] * picked[0] + gates[1] * picked[1]).astype(BF16)
    lout_ref.send()
    gate_grad = [jnp.sum(upstream * v, axis=1, keepdims=True) for v in picked]
    mean = gates[0] * gate_grad[0] + gates[1] * gate_grad[1]
    lane = lax.broadcasted_iota(jnp.int32, (toks, LANES), 1)
    logit_grad = sum(
        jnp.where(lane == cols_ref[:, c + 1 : c + 2], gates[c] * (gate_grad[c] - mean), 0.0) for c in range(2)
    ).astype(BF16)
    grad_route = mm(n3, logit_grad, TN)
    gets[1].wait()
    three_grad = mm(hot[0] + hot[1], ing_s[...].reshape(slots, d)) + mm(logit_grad, route_ref[...])
    dv, gain3, bias3 = norm_back(xhat3, r3, gb_ref[2:3, :], three_grad)
    two_grad = upstream + dv
    ffn_grad = two_grad.astype(BF16)
    xhat, r = norm_parts(after_ref[...])
    n2 = (xhat * gb_ref[1:2, :] + gb_ref[4:5, :]).astype(BF16)
    wait_all(down_w, wait_sem.at[2])
    wait_all(in_w, wait_sem.at[1])
    step = 512
    hid_s, slope_s, n2_grad = hid_ref.ready(), slope_ref.ready(), ag_ref.buffer
    n2_grad[...] = jnp.zeros_like(n2_grad)

    @pl.loop(0, ff // step)
    def _(j):
        at = pl.ds(pl.multiple_of(j * step, step), step)
        gdown_s[at, :] = mm(hid_s[j], ffn_grad, TN).astype(BF16)
        pre_grad = (mm(ffn_grad, down_w[at, :], NT) * slope_s[j]).astype(BF16)
        gin_s[:, at] = mm(n2, pre_grad, TN).astype(BF16)
        n2_grad[...] += mm(pre_grad, in_w[:, at], NT)

    if stacked:
        _, rows, width = g_refs[0].shape
        parts = ff_parts(sizes, rows, gout_s, gin_s, gdown_s)
        move_pieces(sizes, me_ref, g_refs, parts[1:], sems.at[0], False)
    else:
        for src, dst in zip((gin_s, gdown_s), g_refs[1:3]):
            pltpu.make_async_copy(src, dst, sems.at[0]).start()
    dv, gain2, bias2 = norm_back(xhat, r, gb_ref[1:2, :], n2_grad[...])
    after_grad = two_grad + dv
    ag_ref[...] = after_grad
    ag_ref.send()
    attn_grad = after_grad.astype(BF16)
    gout_s[...] = mm(att_ref[...], attn_grad, TN).astype(BF16)
    lanes = lax.broadcasted_iota(jnp.int32, (16, LANES), 1)
    lanes = lanes - lax.broadcasted_iota(jnp.int32, (16, LANES), 0)
    norms = jnp.concatenate([gain2, gain3, bias2, bias3, jnp.zeros((12, d), F32)], axis=0).astype(BF16)
    n_route = route_columns(sizes)
    small_s[...] = (grad_route + mm(norms, (lanes == n_route).astype(BF16), TN)).astype(BF16)
    if stacked:
        parts = [parts[0], (small_s, rows, LANES, width - LANES, 1)]
        move_pieces(sizes, me_ref, g_refs, parts, sems.at[0], False)
    else:
        for src, dst in zip((gout_s, small_s), (g_refs[0], g_refs[3])):
            pltpu.make_async_copy(src, dst, sems.at[0]).start()
    wait_all(out_w, wait_sem.at[0])
    atg_ref[...] = mm(attn_grad, out_w[...], NT).astype(BF16)
    for ref in g_refs:
        wait_all(ref, sems.at[0])


def route_columns(sizes):
    return sizes["y"] * sizes["c"] * sizes["x"]


def gate_kernel(*refs):
    refs[-1][...] = jnp.zeros_like(refs[-1])


def expert_kernel(n_ring, gate_ref, recv_ref, *rest):
    w_refs = rest[:n_ring]
    ret_ref = rest[n_ring]
    hid_ref, pg_ref, x_s, g_s, up_s, down_s, acc_s, gacc_s, sems, w_sems = rest[n_ring + 1 :]
    gets = [pltpu.make_async_copy(recv_ref.at[:, i], v, sems.at[i]) for i, v in enumerate((x_s, g_s))]
    gets[0].start()
    per, _, f = w_refs[0].shape
    n_src, cap, d = x_s.shape
    for s in range(n_ring):
        for k in range(per):
            piece = w_refs[s].at[k]
            cols = pl.ds(k * f, f)
            pltpu.make_async_copy(piece.at[pl.ds(0, d), :], up_s.at[s, :, cols], w_sems.at[s]).start()
            for b in range(d // f):
                part = piece.at[pl.ds(d + b * f, f), :]
                pltpu.make_async_copy(part, down_s.at[s, cols, pl.ds(b * f, f)], w_sems.at[s]).start()
        if s == 0:
            gets[1].start()
    rows = n_src * cap
    step = min(512, rows)
    blocks = [(slice(j, j + step), slice(j // cap, (j + step) // cap)) for j in range(0, rows, step)]
    for copy in gets:
        copy.wait()
    acc_s[...] = jnp.zeros_like(acc_s)
    gacc_s[...] = jnp.zeros_like(gacc_s)
    hid_s, pg_s = hid_ref.buffer, pg_ref.buffer

    @pl.loop(0, n_ring)
    def _(s):
        wait_all(up_s.at[s], w_sems.at[s])
        wait_all(down_s.at[s], w_sems.at[s])
        for at, src in blocks:
            x = x_s[src].reshape(step, d)
            hidden, slope = gelu_both(mm(x, up_s[s]))
            hidden = hidden.astype(BF16)
            hid_s[s, at, :] = hidden
            acc_s[at, :] += mm(hidden, down_s[s])
            pre_grad = (mm(g_s[src].reshape(step, d), down_s[s], NT) * slope).astype(BF16)
            pg_s[s, at, :] = pre_grad
            gacc_s[at, :] += mm(pre_grad, up_s[s], NT)
        hid_ref.part(s)
        pg_ref.part(s)

    x_s[...] = acc_s[...].astype(BF16).reshape(x_s.shape)
    g_s[...] = gacc_s[...].astype(BF16).reshape(g_s.shape)
    puts = [pltpu.make_async_copy(v, ret_ref.at[:, i], sems.at[i]) for i, v in enumerate((x_s, g_s))]
    for copy in puts:
        copy.start()
    for copy in puts:
        copy.wait()


def expert_grad_kernel(places, recv_ref, hid_ref, pg_ref, *refs):
    n = len(places)
    out_refs = refs[:n]
    x_s, g_s, hid_s, pg_s, out_s, sems, block_sems, out_sem = refs[n:]
    gets = [pltpu.make_async_copy(recv_ref.at[:, i], v, sems.at[i]) for i, v in enumerate((x_s, g_s))]
    for copy in gets:
        copy.start()
    for s, place in enumerate(places):
        for ref, v in ((pg_ref, pg_s), (hid_ref, hid_s)):
            pltpu.make_async_copy(ref.at[place], v.at[s], block_sems.at[s]).start()
    n_src, cap, d = x_s.shape
    rows = n_src * cap
    _, per, _, f = out_s.shape
    for copy in gets:
        copy.wait()

    @pl.loop(0, n)
    def _(s):
        wait_all(pg_s.at[s], block_sems.at[s])
        wait_all(hid_s.at[s], block_sems.at[s])
        up = mm(x_s[...].reshape(rows, d), pg_s[s], TN).astype(BF16)
        down = mm(hid_s[s], g_s[...].reshape(rows, d), TN).astype(BF16)
        for k in range(per):
            cols = slice(k * f, (k + 1) * f)
            out_s[s, k, 0:d, :] = up[:, cols]
            for b in range(d // f):
                out_s[s, k, d + b * f : d + (b + 1) * f, :] = down[cols, b * f : (b + 1) * f]

    puts = [pltpu.make_async_copy(out_s.at[s], ref, out_sem.at[s]) for s, ref in enumerate(out_refs)]
    for copy in puts:
        copy.start()
    for copy in puts:
        copy.wait()


def local(sizes, tokens, lengths, task_ids, expert_table, norm_gain, norm_bias, w_qkv, w_out, w_in, w_down, w_router, expert_up, expert_down, cotangent):
    toks, d = tokens.shape
    local_experts, _, f = expert_up.shape
    assert local_experts == sizes["x"] == 2
    share = sizes["y"] * sizes["c"]
    n_hid = sizes["z"] * sizes["x"]
    experts = share * local_experts
    capacity = 2 * toks // experts
    slots = experts * capacity
    ff = w_in.shape[1] * share
    rc = w_router.shape[1]
    rows_dev = d // n_hid
    n_ring = sizes["z"]
    ring = [(i, (i + 1) % n_ring) for i in range(n_ring)]
    down = [(j, i) for i, j in ring]
    n_up = n_ring // 2
    n_down = n_ring - 1 - n_up
    stacked = sizes["y"] == sizes["c"] == 2 and all(
        w.shape[1] % LANES == 0 for w in (w_qkv, w_out, w_in, w_down)
    )

    def after(v, *others):
        return lax.optimization_barrier((v,) + others)[0]

    def swap(v, axis, by=1):
        n = math.prod(sizes[a] for a in axis)
        return lax.ppermute(v, axis, [(i, i ^ by) for i in range(n)])

    def gather_z(piece):
        return [piece] + [swap(piece, ("z",), by) for by in range(1, n_ring)]

    def plane_swaps(stacks):
        return [swap(stacks[by], ("y", "x"), by) for by in range(1, len(PLANE))]

    def other_core(stacks):
        return [swap(t, ("c",)) for t in stacks]

    def add_core(near, far, name, placed=False):
        n, shape = len(PLANE), near[0].shape
        outs = [sds((n,) + shape, BF16)] if placed else [sds(shape, F32)] + [sds(shape, BF16)] * (n - 1)
        return call(
            functools.partial(sum_cores_kernel, placed),
            name,
            K[name],
            outs,
            [smem()] + [vmem()] * (2 * n),
            [anywhere()] if placed else [vmem()] * n,
            [pltpu.VMEM((n,) + shape, BF16), dma((n,))] if placed else [],
            SMALL_BYTES,
        )(me, *[v for v in near[:n]], *far)

    def add_plane(mine, got):
        total = sum((v.astype(F32) for v in got), mine)
        return total[0], total[1:].astype(BF16)

    def z_swaps(parts):
        return [swap(parts[by - 1], ("z",), by) for by in range(1, n_ring)]

    def add_z(mine, got):
        return sum((v.astype(F32) for v in got), mine)

    def exchange(v):
        return lax.all_to_all(v, ("y", "c", "x"), split_axis=0, concat_axis=0, tiled=True)

    def gather_whole(w):
        w = lax.all_gather(w.astype(BF16), ("y", "c"), axis=1, tiled=True)
        return lax.all_gather(w, ("z", "x"), axis=0, tiled=True)

    def reduce_whole(g):
        g = lax.psum_scatter(g.astype(F32), ("z", "x"), scatter_dimension=0, tiled=True)
        return lax.psum_scatter(g, ("y", "c"), scatter_dimension=1, tiled=True)

    def sds(shape, dtype):
        return jax.ShapeDtypeStruct(shape, dtype)

    dma = pltpu.SemaphoreType.DMA
    me = jnp.stack([lax.axis_index(a) for a in AXES]).astype(jnp.int32)
    x_at = lax.axis_index("x")

    def piece_of(at):
        up = lax.dynamic_index_in_dim(expert_up, at, 0, keepdims=False)
        down = lax.dynamic_index_in_dim(expert_down, at, 0, keepdims=False)
        return jnp.concatenate(
            [up] + [down[:, b * f : (b + 1) * f] for b in range(d // f)], axis=0
        ).astype(BF16)

    def routes(lengths):
        return find_routes(lengths, task_ids, expert_table, toks, experts, capacity)

    if stacked:
        folds = w_down.shape[0] // rows_dev
        width = w_out.shape[1] + w_in.shape[1] + folds * w_down.shape[1]
        small = jnp.concatenate([w_router, norm_gain, norm_bias], axis=1)
        small = jnp.pad(small, ((0, 0), (0, LANES - small.shape[1])))
        qkv_piece = jnp.concatenate([w_qkv, small], axis=1).astype(BF16)
        ff_piece, own, other = call(
            pack_kernel,
            "pack",
            K["pack"],
            [sds((rows_dev, width), BF16)] + [sds((2 * d, f), BF16)] * 2,
            [smem()] + ["late"] * 5,
            ["early"] * 3,
        )(me, w_out, w_in, w_down, expert_up, expert_down)
        expert_x = swap(other, ("x",))
        qkv_z = gather_z(qkv_piece)
        mine = jnp.stack(qkv_z)
        qkv_w = lax.all_to_all(jnp.stack([mine] * len(PLANE)), ("y", "x"), split_axis=0, concat_axis=0, tiled=True)
        ff_z = gather_z(after(ff_piece, *qkv_z[1:]))
        rows, cols = routes(after(lengths, *ff_z[1:]))
        qkv_w = after(qkv_w, rows)
        half = len(PLANE) // 2
        qkv_w = [qkv_w] + other_core([qkv_w[:half], qkv_w[half:]])
        blocks = [after(jnp.stack([own, expert_x]), *ff_z[1:])]
        blocks.append(lax.ppermute(blocks[0], "z", ring))
        mine = jnp.stack(ff_z)
        ffw = [mine] + plane_swaps([mine] * len(PLANE))
        tokens_in = after(tokens, rows)
        gb_in = []
    else:
        qkv_w = [gather_whole(w_qkv)]
        ffw = [gather_whole(w_out), gather_whole(w_in), gather_whole(w_down)]
        small = jnp.concatenate([w_router, norm_gain, norm_bias], axis=1)
        small = lax.all_gather(small.astype(BF16), AXES)
        route = small[:, :, :rc].reshape(share, d, rc).transpose(0, 2, 1).reshape(experts, d)
        route = jnp.pad(route, ((0, LANES - experts), (0, 0)))
        gb = small[:n_hid, :, rc:].reshape(d, 6).T.astype(F32)
        gb = jnp.pad(gb, ((0, 2), (0, 0)))
        gb_in = [gb]
        tokens_in = tokens
        rows, cols = routes(lengths)
        blocks = [jnp.stack([piece_of(x_at), swap(piece_of(1 - x_at), ("x",))])]
        blocks.append(lax.ppermute(blocks[0], "z", ring))

    out_shape = [sds((toks, 3 * d), BF16), sds((toks, d), BF16)]
    scratch = [pltpu.VMEM((d, 3 * d), BF16)]
    if stacked:
        out_shape += [sds((8, d), F32), sds((LANES, d), BF16)]
        scratch += [pltpu.VMEM((share, d, LANES), BF16)]
    out = call(
        functools.partial(attend_kernel, sizes, stacked, rc),
        "attend",
        K["attend"],
        out_shape,
        [smem()] + ["late"] * 3 + [vmem()] * len(gb_in) + [anywhere()] * len(qkv_w),
        ["early"] * 2 + [vmem()] * (len(out_shape) - 2),
        scratch + [dma((2,))],
    )(me, tokens_in, cols, rows, *gb_in, *qkv_w)
    qkv, attended = out[:2]
    if stacked:
        gb, route = out[2:]
        ffw = [ffw[0]] + [after(t, attended, *(blocks[-1:] if K["ringff"] else [])) for t in ffw[1:]]
        ffw = ffw + other_core(ffw)
    ups, downs = blocks, [blocks[0]]
    while len(ups) <= n_up:
        ups.append(lax.ppermute(after(ups[-1], attended), "z", ring))
    while len(downs) <= n_down:
        downs.append(lax.ppermute(after(downs[-1], attended), "z", down))
    blocks = ups + downs[:0:-1]

    f_scratch = [pltpu.VMEM((d, d), BF16), pltpu.VMEM((d, ff), BF16), pltpu.VMEM((ff, d), BF16)]
    pair = [pltpu.VMEM((experts, capacity, d), BF16)] * 2
    after_attn, layer_two, gates, send = call(
        functools.partial(feed_kernel, sizes, stacked),
        "feed",
        K["feed"],
        [sds((toks, d), F32), sds((toks, d), F32), sds((toks, LANES), F32)]
        + [sds((experts, 2, capacity, d), BF16)],
        [smem()] + ["late"] * 2 + [vmem()] + ["late"] * 4 + [anywhere()] * len(ffw),
        ["early"] * 3 + [anywhere()],
        f_scratch + [dma((3,))] + pair + [dma((2,))],
    )(me, tokens, attended, gb, cols, rows, route, cotangent, *ffw)
    recv = exchange(send)
    gate = call(gate_kernel, "gate", K["gate"], sds((8, LANES), F32), [anywhere()] * (n_ring - 1), vmem())(*blocks[1:])
    block = [sds((n_ring, slots, 2 * f), BF16)]
    out = call(
        functools.partial(expert_kernel, n_ring),
        "experts",
        K["experts"],
        [sds(recv.shape, BF16)] + block * 2,
        [anywhere()] * (2 + n_ring),
        [anywhere()] + ["early"] * 2,
        pair
        + [pltpu.VMEM((n_ring, d, 2 * f), BF16), pltpu.VMEM((n_ring, 2 * f, d), BF16)]
        + [pltpu.VMEM((slots, d), F32)] * 2
        + [dma((2,)), dma((n_ring,))],
    )(gate, recv, *blocks)
    hids, pre_grads = out[1:]
    back = exchange(out[0])

    def expert_grads(places, recv):
        n = len(places)
        blocks = [pltpu.VMEM((n, slots, 2 * f), BF16)] * 2 + [pltpu.VMEM((n, 2, 2 * d, f), BF16)]
        return call(
            functools.partial(expert_grad_kernel, places),
            "expert_grads",
            K["expert_grads"] * n,
            [sds((2, 2 * d, f), BF16)] * n,
            [anywhere()] * 3,
            [anywhere()] * n,
            pair + blocks + [dma((2,)), dma((n,)), dma((n,))],
        )(recv, hids, pre_grads)

    far_grads = expert_grads([1], recv)
    moving = lax.ppermute(far_grads[0], "z", ring)
    rest = expert_grads([s % n_ring for s in range(2, n_ring + 1)], after(recv, far_grads[0]))
    prob_shapes = [sds((d // LANES // 2, 2 * MAXLEN, k1 - k0), F32) for _, k0, k1 in head_blocks(toks)] * 2
    probs = call(
        probs_kernel, "probs", K["probs"], prob_shapes, [vmem()] * 3, ["early"] * len(prob_shapes)
    )(cols, rows, after(qkv, rest[0]))
    hidden, slope = call(
        functools.partial(hidden_kernel, sizes, stacked),
        "hidden",
        K["hidden"],
        [sds((ff // 512, toks, 512), BF16), sds((ff // 512, toks, 512), F32)],
        [smem()] + [vmem()] * 2 + [anywhere()] * (len(OFFSETS) if stacked else 1),
        ["early"] * 2,
        [pltpu.VMEM((d, ff), BF16), dma((1,))],
    )(me, after(after_attn, rest[0]), gb, *(ffw if stacked else ffw[1:2]))

    if stacked:
        ff_cols, qkv_cols = ffw[0].shape[-1] + LANES, qkv_w[0].shape[-1]
        ff_out = [sds((n_ring, rows_dev, ff_cols), BF16)] * len(OFFSETS)
        qkv_out = [sds((n_ring, rows_dev, qkv_cols), BF16)] * len(OFFSETS)
    else:
        ff_out = [sds((d, d), BF16), sds((d, ff), BF16), sds((ff, d), BF16), sds((d, LANES), BF16)]
        qkv_out = [sds((d, 3 * d), BF16), sds((d, LANES), BF16)]
    out = call(
        functools.partial(feed_back_kernel, sizes, stacked),
        "feed_back",
        K["feed_back"],
        [sds((toks, d), BF16), sds((toks, d), F32), sds((toks, d), BF16)] + ff_out,
        [smem()] + ["late"] * 4 + [vmem()] + ["late"] * 5 + [anywhere()] * (1 + len(ffw)),
        ["early"] * 3 + [anywhere()] * len(ff_out),
        f_scratch + f_scratch + [pltpu.VMEM((d, LANES), BF16)] + pair + [dma((2,)), dma((3,)), dma((1,))],
    )(me, cols, cotangent, gates, layer_two, gb, route, after_attn, hidden, slope, attended, after(back, probs[0]), *ffw)
    layer_out, after_grad, att_grad = out[:3]
    ff_grads = out[3:]
    step = n_ring - 2

    def add_on(moving, mine, weight):
        n, shape = 4, (4, mine.shape[0] * mine.shape[1] // 4, mine.shape[2])
        scratch = [pltpu.VMEM(shape, BF16)] * 3 + [dma((3, n))]
        return call(add_kernel, "add", weight, sds(mine.shape, BF16), [anywhere()] * 2, anywhere(), scratch, SMALL_BYTES)(moving, mine)

    for t in range(step - 1):
        if K["tie_ring1"]:
            moving = after(moving, after_grad)
        moving = lax.ppermute(add_on(moving, rest[t], K["add1"]), "z", ring)
    if stacked:
        ff_far = other_core(ff_grads[len(PLANE) :])
    half = d // 2
    n_prob = len(probs) // 2
    acc = [pltpu.VMEM((toks, half), F32)] * 3
    if stacked:
        ff_sums = add_core(ff_grads, ff_far, "sum_ff", True)
        ff_got = [lax.all_to_all(ff_sums[0], ("y", "x"), split_axis=0, concat_axis=0, tiled=True)]
        att_grad = after(att_grad, ff_sums[0])
    first_half = call(
        functools.partial(attend_back_first_kernel, n_prob),
        "attend_back_first",
        K["first"],
        [sds((3, toks, half), BF16)],
        ["late"] * (2 + n_prob),
        [vmem()],
        acc,
    )(*probs[:n_prob], qkv, att_grad)[0]
    att_grad = after(att_grad, first_half)
    out = call(
        functools.partial(attend_back_kernel, sizes, stacked, n_prob),
        "attend_back",
        K["attend_back"],
        [sds((toks, d), F32)] + qkv_out,
        [smem(), "late", vmem()] + ["late"] * (4 + n_prob) + [anywhere()] * len(qkv_w),
        ["early"] + [anywhere()] * len(qkv_out),
        [pltpu.VMEM((d, 3 * d), BF16)]
        + acc
        + [pltpu.VMEM((d, 3 * d), BF16), pltpu.VMEM((d, LANES), BF16), dma((2,))],
    )(me, tokens, gb, *probs[n_prob:], qkv, att_grad, after_grad, first_half, *qkv_w)
    grad_tokens = out[0]
    qkv_grads = out[1:]

    e_at = lax.axis_index("y") * sizes["c"] + lax.axis_index("c")
    if step:
        if K["tie_ring2"]:
            moving = after(moving, grad_tokens)
        moving = lax.ppermute(add_on(moving, rest[step - 1], K["add2"]), "z", ring)
    if stacked:
        qkv_sums = add_core(qkv_grads, other_core(qkv_grads[len(PLANE) :]), "sum_qkv")
        qkv_got = plane_swaps(qkv_sums)
        z_shape = (n_ring, rows_dev, ff_cols)
        ff_send = call(
            sum_plane_kernel,
            "sum_plane",
            K["sum_plane"],
            sds(z_shape, BF16),
            [smem(), vmem()],
            anywhere(),
            [pltpu.VMEM(z_shape, BF16), dma((n_ring,))],
            SMALL_BYTES,
        )(me, ff_got[0])
        qkv_got = [after(v, ff_send) for v in qkv_got]
        moving = after(moving, *qkv_got)
        ff_got = lax.all_to_all(ff_send, "z", split_axis=0, concat_axis=0, tiled=True)
        qkv_mine, qkv_parts_z = add_plane(qkv_sums[0], qkv_got)
        qkv_got = z_swaps(qkv_parts_z)
    other = swap((moving[1].astype(F32) + rest[-1][1].astype(F32)).astype(BF16), ("x",))
    grad_up, grad_edown = call(
        finish_experts_kernel,
        "finish_experts",
        K["finish"],
        [sds(expert_up.shape, F32), sds(expert_down.shape, F32)],
        [smem()] + [anywhere()] * 2 + ["late"],
        ["early"] * 2,
        [pltpu.VMEM((2 * d, f), BF16)] * 2 + [dma((2,))],
        SMALL_BYTES,
    )(me, moving, rest[-1], other)
    if stacked and K["tie_x"] == 1:
        qkv_got = [after(v, grad_up) for v in qkv_got]

    if stacked:
        shapes = [v.shape for v in (w_out, w_in, w_down, w_qkv)]
        shapes += [v.shape[::-1] for v in (w_router, norm_gain, norm_bias)]
        grad_out, grad_in, grad_down, grad_qkv, grad_router, grad_gain, grad_bias = call(
            functools.partial(finish_kernel, n_ring, rc, route_columns(sizes)),
            "finish",
            K["finish"],
            [sds(v, F32) for v in shapes],
            [smem()] + [vmem()] * (1 + n_ring),
            [vmem()] * len(shapes),
            vmem_bytes=SMALL_BYTES,
        )(e_at.reshape(1).astype(jnp.int32), ff_got, qkv_mine, *qkv_got)
        grad_router, grad_gain, grad_bias = grad_router.T, grad_gain.T, grad_bias.T
    else:
        grad_out, grad_in, grad_down = (reduce_whole(g) for g in ff_grads[:3])
        grad_qkv = reduce_whole(qkv_grads[0])
        small_ff, small_qkv = (
            lax.psum(lax.psum_scatter(g.astype(F32), ("z", "x"), scatter_dimension=0, tiled=True), ("y", "c"))
            for g in (ff_grads[3], qkv_grads[1])
        )
        grad_router = lax.dynamic_slice_in_dim(small_ff, e_at * rc, rc, axis=1)
        n_route = route_columns(sizes)
        gains, biases = small_ff[:, n_route : n_route + 2], small_ff[:, n_route + 2 : n_route + 4]
        grad_gain = jnp.concatenate([small_qkv[:, 0:1], gains], axis=1)
        grad_bias = jnp.concatenate([small_qkv[:, 1:2], biases], axis=1)
    return (
        layer_out,
        grad_tokens,
        grad_gain,
        grad_bias,
        grad_qkv,
        grad_out,
        grad_in,
        grad_down,
        grad_router,
        grad_up,
        grad_edown,
    )


def solution(mesh):
    n_exp, n_hid = mesh.shape["expert"], mesh.shape["hidden"]
    sizes = {"y": n_exp // 2, "c": 2, "z": n_hid // 2, "x": 2}
    fine = Mesh(mesh.devices.reshape(tuple(sizes[a] for a in AXES)), AXES)
    both, exp, hid = AXES, ("y", "c"), ("z", "x")
    return jax.shard_map(
        functools.partial(local, sizes),
        mesh=fine,
        in_specs=(
            P(both, None),
            P(both, None),
            P(both, None),
            P(),
            P(hid, None),
            P(hid, None),
            P(hid, exp),
            P(hid, exp),
            P(hid, exp),
            P(hid, exp),
            P(hid, exp),
            P(exp, None, hid),
            P(exp, hid, None),
            P(both, None),
        ),
        out_specs=(
            P(both, None),
            P(both, None),
            P(hid, None),
            P(hid, None),
            P(hid, exp),
            P(hid, exp),
            P(hid, exp),
            P(hid, exp),
            P(hid, exp),
            P(exp, None, hid),
            P(exp, hid, None),
        ),
        check_vma=False,
    )
```

```python
import functools
import math

import jax
import jax.numpy as jnp
from jax import lax
from jax.experimental import pallas as pl
from jax.experimental.pallas import tpu as pltpu
from jax.sharding import Mesh, PartitionSpec as P

HEAD_DIM = 64
MAXLEN = 128
LANES = 128
EPSILON = 1e-05
FILL_SCORE = -1000000000.0
AXES = ("y", "c", "z", "x")
VMEM_BYTES = 56 * 1024 * 1024
SMALL_BYTES = 24 * 1024 * 1024
GELU_A = math.sqrt(2.0 / math.pi)
GELU_B = 0.044715

F32 = jnp.float32
BF16 = jnp.bfloat16

NN = (((1,), (0,)), ((), ()))
NT = (((1,), (1,)), ((), ()))
TN = (((0,), (0,)), ((), ()))


def mm(a, b, dims=NN):
    return lax.dot_general(a, b, dims, preferred_element_type=F32)


def gelu(v):
    t = jnp.tanh(GELU_A * (v + GELU_B * (v * v * v)))
    return 0.5 * v * (1.0 + t)


def gelu_both(v):
    v2 = v * v
    t = jnp.tanh(GELU_A * (v + GELU_B * (v2 * v)))
    half = 0.5 * (1.0 + t)
    slope = half + 0.5 * v * (1.0 - t * t) * (GELU_A + (3.0 * GELU_A * GELU_B) * v2)
    return v * half, slope


def norm_parts(v):
    center = v - jnp.mean(v, axis=-1, keepdims=True)
    r = lax.rsqrt(jnp.mean(center * center, axis=-1, keepdims=True) + EPSILON)
    return center * r, r


def norm_back(xhat, r, gain, h):
    hg = h * gain
    inner = jnp.mean(hg * xhat, axis=-1, keepdims=True)
    dv = r * (hg - jnp.mean(hg, axis=-1, keepdims=True) - xhat * inner)
    return dv, jnp.sum(h * xhat, axis=0, keepdims=True), jnp.sum(h, axis=0, keepdims=True)


K = dict(scale=0.35, routes=60, attend=0.3, feed=3, probs=3, hidden=6, experts=18, expert_grads=3, feed_back=20, first=4, attend_back=9, add1=2, add2=14, sum_ff=2, sum_qkv=3, sum_plane=0.3, finish=0.3, pack=3, gate=60, ring1=1, ringff=0, tie_near=1, tie_ffz=1, x_first=0, ff_a2a=1, tie_qkv=1, tie_ring3=1, tie_ring2=1, tie_ring1=1, tie_x=1, tie_ffc=1)


def cost(us):
    return pl.CostEstimate(flops=int(K["scale"] * us * 1.15e9), bytes_accessed=0, transcendentals=0)


def vmem():
    return pl.BlockSpec(memory_space=pltpu.VMEM)


class Late:
    def __init__(self, ref, buffer, sem):
        self.buffer, self.shape, self.dtype = buffer, buffer.shape, buffer.dtype
        self.copy = pltpu.make_async_copy(ref, buffer, sem)
        self.copy.start()
        self.waited = False

    def ready(self):
        if not self.waited:
            self.copy.wait()
            self.waited = True
        return self.buffer

    finish = ready

    def __getitem__(self, at):
        return self.ready()[at]


class Early:
    def __init__(self, ref, buffer, sem):
        self.buffer, self.shape, self.dtype = buffer, buffer.shape, buffer.dtype
        self.ref, self.sem = ref, sem
        self.copy = pltpu.make_async_copy(buffer, ref, sem)
        self.sent = False

    def send(self):
        self.copy.start()
        self.sent = True

    def part(self, i):
        pltpu.make_async_copy(self.buffer.at[i], self.ref.at[i], self.sem).start()
        self.sent = True

    def finish(self):
        if not self.sent:
            self.send()
        self.copy.wait()

    def __setitem__(self, at, value):
        self.buffer[at] = value


def call(kernel, name, us, out_shape, in_specs, out_specs, scratch=(), vmem_bytes=VMEM_BYTES):
    single = not isinstance(out_shape, list)
    outs, out_specs = ([out_shape], [out_specs]) if single else (out_shape, out_specs)
    specs = list(in_specs) + list(out_specs)

    def run(*args):
        arrays = list(args) + outs
        moving = [i for i, spec in enumerate(specs) if spec in ("late", "early")]

        def body(*refs):
            refs = list(refs)
            buffers, sems = refs[len(specs) + len(scratch) : -1], refs[-1]
            for j, i in enumerate(moving):
                kind = Late if specs[i] == "late" else Early
                refs[i] = kind(refs[i], buffers[j], sems.at[j])
            kernel(*refs[: len(specs) + len(scratch)])
            for i in moving:
                refs[i].finish()

        buffers = [pltpu.VMEM(arrays[i].shape, arrays[i].dtype) for i in moving]
        places = [anywhere() if spec in ("late", "early") else spec for spec in specs]
        results = pl.pallas_call(
            body,
            out_shape=outs,
            in_specs=places[: len(in_specs)],
            out_specs=places[len(in_specs) :],
            scratch_shapes=list(scratch) + buffers + [pltpu.SemaphoreType.DMA((max(len(moving), 1),))],
            compiler_params=pltpu.CompilerParams(vmem_limit_bytes=vmem_bytes),
            cost_estimate=cost(us),
            name=name,
        )(*args)
        return results[0] if single else results

    return run


def smem():
    return pl.BlockSpec(memory_space=pltpu.SMEM)


def anywhere():
    return pl.BlockSpec(memory_space=pl.ANY)


PLANE = ((0, 0), (0, 1), (1, 0), (1, 1))
OFFSETS = tuple((c, y, x) for c in (0, 1) for y, x in PLANE)


def move_pieces(sizes, me_ref, stacks, parts, sem, inward, placed=False):
    at = {axis: me_ref[i] for i, axis in enumerate(AXES)}
    for (dc, dy, dx), stack in zip(OFFSETS, stacks):
        y = dy if placed else lax.bitwise_xor(at["y"], dy)
        x = dx if placed else lax.bitwise_xor(at["x"], dx)
        e = y * sizes["c"] + lax.bitwise_xor(at["c"], dc)

        @pl.loop(0, sizes["z"])
        def _(dz):
            h = lax.bitwise_xor(at["z"], dz) * sizes["x"] + x
            for whole, rows, cols, first, folds in parts:
                step = rows // folds
                for i in range(folds):
                    piece = stack.at[dz, :, pl.ds(first + i * cols, cols)]
                    top = pl.multiple_of(h * rows + i * step, step)
                    if len(whole.shape) == 3:
                        block = whole.at[e, pl.ds(top, step), :]
                    elif whole.shape[1] == cols:
                        block = whole.at[pl.ds(top, step), :]
                    else:
                        block = whole.at[pl.ds(top, step), pl.ds(pl.multiple_of(e * cols, cols), cols)]
                    src, dst = (piece, block) if inward else (block, piece)
                    pltpu.make_async_copy(src, dst, sem).start()


def wait_all(ref, sem):
    pltpu.make_async_copy(ref, ref, sem).wait()


def routes_kernel(capacity, experts, len_row, task_row, table, rows_out, cols_out):
    sents = len_row.shape[1]
    tasks = table.shape[0]
    toks = rows_out.shape[1]
    f = lambda v: v.astype(F32)
    i0 = lax.broadcasted_iota(jnp.int32, (sents, sents), 0)
    i1 = lax.broadcasted_iota(jnp.int32, (sents, sents), 1)
    turn = lambda row: jnp.sum(jnp.where(i0 == i1, row, 0.0), axis=1, keepdims=True)
    len_r, task_r = f(len_row[...]), f(task_row[...])
    len_c, task_c = turn(len_r), turn(task_r)
    ends_row = jnp.sum(jnp.where(i0 <= i1, len_c, 0.0), axis=0, keepdims=True)
    ends_col = jnp.sum(jnp.where(i1 <= i0, len_r, 0.0), axis=1, keepdims=True)
    starts_row = ends_row - len_r
    starts_col = ends_col - len_c
    t0 = lax.broadcasted_iota(jnp.int32, (tasks, tasks), 0)
    t1 = lax.broadcasted_iota(jnp.int32, (tasks, tasks), 1)
    table_c = [f(table[:, c : c + 1]) for c in range(2)]
    table_r = [jnp.sum(jnp.where(t0 == t1, v, 0.0), axis=0, keepdims=True) for v in table_c]
    tok = f(lax.broadcasted_iota(jnp.int32, (toks, sents), 0))
    sent = lax.broadcasted_iota(jnp.int32, (toks, sents), 1)
    hot = (tok >= starts_row) & (tok < ends_row)
    seg_c = jnp.sum(jnp.where(hot, f(sent), 0.0), axis=1, keepdims=True)
    own = jnp.sum(jnp.where(hot, task_r, 0.0), axis=1, keepdims=True)
    thot = f(lax.broadcasted_iota(jnp.int32, (toks, tasks), 1)) == own
    pair_c = [
        jnp.sum(jnp.where(thot, table_r[c], 0.0), axis=1, keepdims=True)
        for c in range(2)
    ]
    tok = f(lax.broadcasted_iota(jnp.int32, (sents, toks), 1))
    sent = lax.broadcasted_iota(jnp.int32, (sents, toks), 0)
    hot = (tok >= starts_col) & (tok < ends_col)
    seg_r = jnp.sum(jnp.where(hot, f(sent), 0.0), axis=0, keepdims=True)
    own = jnp.sum(jnp.where(hot, task_c, 0.0), axis=0, keepdims=True)
    thot = f(lax.broadcasted_iota(jnp.int32, (tasks, toks), 0)) == own
    pair_r = [
        jnp.sum(jnp.where(thot, table_c[c], 0.0), axis=0, keepdims=True)
        for c in range(2)
    ]
    a0 = lax.broadcasted_iota(jnp.int32, (toks, toks), 0)
    a1 = lax.broadcasted_iota(jnp.int32, (toks, toks), 1)
    upper = (a0 < a1).astype(BF16)
    lower = (a1 < a0).astype(BF16)
    er = f(lax.broadcasted_iota(jnp.int32, (experts, toks), 0))
    ec = f(lax.broadcasted_iota(jnp.int32, (toks, experts), 1))
    hot_r = [(er == pair_r[c]).astype(F32) for c in range(2)]
    hot_c = [(ec == pair_c[c]).astype(F32) for c in range(2)]
    before_r = [mm(hot_r[c].astype(BF16), upper) for c in range(2)]
    before_c = [mm(lower, hot_c[c].astype(BF16)) for c in range(2)]
    before_r[1] = before_r[1] + jnp.sum(hot_r[0], axis=1, keepdims=True)
    before_c[1] = before_c[1] + jnp.sum(hot_c[0], axis=0, keepdims=True)
    place = lambda pair, rank: jnp.where(rank < capacity, pair * capacity + rank, -1.0)
    slot_r = [place(pair_r[c], jnp.sum(hot_r[c] * before_r[c], axis=0, keepdims=True)) for c in range(2)]
    slot_c = [place(pair_c[c], jnp.sum(hot_c[c] * before_c[c], axis=1, keepdims=True)) for c in range(2)]
    at = lax.broadcasted_iota(jnp.int32, rows_out.shape, 0)
    rows_out[...] = jnp.where(
        at == 0, seg_r, jnp.where(at == 1, slot_r[0], slot_r[1])
    ).astype(jnp.int32)
    at = lax.broadcasted_iota(jnp.int32, cols_out.shape, 1)
    packed = jnp.where(at == 0, seg_c, 0.0)
    for j, v in enumerate((pair_c[0], pair_c[1], slot_c[0], slot_c[1])):
        packed = jnp.where(at == j + 1, v, packed)
    cols_out[...] = packed.astype(jnp.int32)


def find_routes(lengths, task_ids, expert_table, toks, experts, capacity):
    return call(
        functools.partial(routes_kernel, capacity, experts),
        "routes",
        K["routes"],
        [jax.ShapeDtypeStruct((8, toks), jnp.int32), jax.ShapeDtypeStruct((toks, 8), jnp.int32)],
        [vmem()] * 3,
        [vmem()] * 2,
    )(lengths, task_ids, expert_table)


def pack_kernel(me_ref, out_ref, in_ref, down_ref, up_ref, edown_ref, ff_out, own_out, other_out):
    d, f = up_ref.shape[1:]
    x = me_ref[AXES.index("x")]
    for out, e in ((other_out, 1 - x), (own_out, x)):
        out[0:d, :] = up_ref[e].astype(BF16)
        for b in range(d // f):
            out[d + b * f : d + (b + 1) * f, :] = edown_ref[e, :, b * f : (b + 1) * f].astype(BF16)
        out.send()
    rows, at = out_ref.shape[0], 0
    for ref in (out_ref, in_ref):
        ff_out[:, at : at + ref.shape[1]] = ref[...].astype(BF16)
        at += ref.shape[1]
    cols = down_ref.shape[1]
    for i in range(down_ref.shape[0] // rows):
        ff_out[:, at + i * cols : at + (i + 1) * cols] = down_ref[i * rows : (i + 1) * rows, :].astype(BF16)


def add_kernel(a_ref, b_ref, out_ref, a_s, b_s, out_s, sems):
    n = a_s.shape[0]
    parts = a_ref.shape[0]
    rows = a_ref.shape[1] // (n // parts)
    at = [(i // (n // parts), pl.ds(i % (n // parts) * rows, rows)) for i in range(n)]
    gets = []
    for i, (p, row) in enumerate(at):
        gets.append([pltpu.make_async_copy(ref.at[p, row, :], s.at[i], sems.at[j, i]) for j, (ref, s) in enumerate(((a_ref, a_s), (b_ref, b_s)))])
        for copy in gets[-1]:
            copy.start()
    puts = []
    for i, (p, row) in enumerate(at):
        for copy in gets[i]:
            copy.wait()
        out_s[i] = (a_s[i].astype(F32) + b_s[i].astype(F32)).astype(out_s.dtype)
        puts.append(pltpu.make_async_copy(out_s.at[i], out_ref.at[p, row, :], sems.at[2, i]))
        puts[-1].start()
    for copy in puts:
        copy.wait()


def sum_cores_kernel(placed, me_ref, *refs):
    n = len(PLANE)
    near, far, outs = refs[:n], refs[n : 2 * n], refs[2 * n :]
    if placed:
        send_ref, send_s, sems = outs
        puts = []
        for i, (dy, dx) in enumerate(PLANE):
            at = lax.bitwise_xor(me_ref[AXES.index("y")], dy) * 2 + lax.bitwise_xor(me_ref[AXES.index("x")], dx)
            send_s[i] = (near[i][...].astype(F32) + far[i][...].astype(F32)).astype(BF16)
            puts.append(pltpu.make_async_copy(send_s.at[i], send_ref.at[at], sems.at[i]))
            puts[-1].start()
        for copy in puts:
            copy.wait()
    else:
        for i in range(1, n):
            outs[i][...] = (near[i][...].astype(F32) + far[i][...].astype(F32)).astype(BF16)
        outs[0][...] = near[0][...].astype(F32) + far[0][...].astype(F32)


def sum_plane_kernel(me_ref, got_ref, send_ref, send_s, sems):
    n = got_ref.shape[1]
    puts = []
    for k in range(n):
        total = got_ref[0, k].astype(F32)
        for i in range(1, got_ref.shape[0]):
            total = total + got_ref[i, k].astype(F32)
        send_s[k] = total.astype(BF16)
        at = lax.bitwise_xor(me_ref[AXES.index("z")], k)
        puts.append(pltpu.make_async_copy(send_s.at[k], send_ref.at[at], sems.at[k]))
        puts[-1].start()
    for copy in puts:
        copy.wait()


def finish_experts_kernel(me_ref, moving_ref, mine_ref, other_ref, gup_ref, gdown_ref, a_s, b_s, sems):
    gets = [pltpu.make_async_copy(ref.at[0], v, sems.at[i]) for i, (ref, v) in enumerate(((moving_ref, a_s), (mine_ref, b_s)))]
    for copy in gets:
        copy.start()
    d, f = gup_ref.shape[1:]
    x = me_ref[AXES.index("x")]

    def put(value, e):
        gup_ref.buffer[e] = value[:d]
        gup_ref.part(e)
        for b in range(d // f):
            gdown_ref.buffer[e, :, b * f : (b + 1) * f] = value[d + b * f : d + (b + 1) * f]
        gdown_ref.part(e)

    for copy in gets:
        copy.wait()
    put(a_s[...].astype(F32) + b_s[...].astype(F32), x)
    put(other_ref[...].astype(F32), 1 - x)


def total_of(refs):
    total = refs[0][...].astype(F32)
    for v in refs[1:]:
        total = total + v[...].astype(F32)
    return total


def finish_kernel(n_z, route_cols, n_route, e_ref, *refs):
    gout_ref, gin_ref, gdown_ref, gqkv_ref, grouter_ref, ggain_ref, gbias_ref = refs[1 + n_z :]
    total = total_of([refs[0].at[k] for k in range(n_z)])
    at = 0
    for ref in (gout_ref, gin_ref):
        ref[...] = total[:, at : at + ref.shape[1]]
        at += ref.shape[1]
    rows, cols = total.shape[0], gdown_ref.shape[1]
    for i in range(gdown_ref.shape[0] // rows):
        gdown_ref[i * rows : (i + 1) * rows, :] = total[:, at : at + cols]
        at += cols
    small = total[:, at:].T
    total = total_of(refs[1 : 1 + n_z])
    cols = gqkv_ref.shape[1]
    gqkv_ref[...] = total[:, 0:cols]
    first = total[:, cols:].T
    at = lax.broadcasted_iota(jnp.int32, small.shape, 0)
    pick = lambda i: jnp.sum(jnp.where(at == i, small, 0.0), axis=0, keepdims=True)
    for j in range(route_cols):
        grouter_ref[j : j + 1, :] = pick(e_ref[0] * route_cols + j)
    for ref, i in ((ggain_ref, 0), (gbias_ref, 1)):
        ref[0:1, :] = first[i : i + 1]
        ref[1:3, :] = small[n_route + 2 * i : n_route + 2 * i + 2]


def head_blocks(toks):
    n = toks // MAXLEN
    return [(i * MAXLEN, max(i - 1, 0) * MAXLEN, min(i + 2, n) * MAXLEN) for i in range(n)]


def two_heads(block, low_half):
    zero = jnp.zeros_like(block)
    return jnp.concatenate([jnp.where(low_half, block, zero), jnp.where(low_half, zero, block)], axis=0)


def pick_heads(stacked, low_half):
    n = stacked.shape[0] // 2
    return jnp.where(low_half, stacked[:n], stacked[n:])


def probabilities(q2, keys, mask):
    scores = mm(q2, keys, NT) * (1.0 / math.sqrt(HEAD_DIM))
    scores = jnp.where(mask, scores, FILL_SCORE)
    exps = jnp.exp(scores - jnp.max(scores, axis=-1, keepdims=True))
    return exps * (1.0 / jnp.sum(exps, axis=-1, keepdims=True))


def same_sentence(cols_ref, rows_ref, q0, k0, k1):
    seg = cols_ref[q0 : q0 + MAXLEN, 0:1]
    return jnp.concatenate([seg, seg], axis=0) == rows_ref[0:1, k0:k1]


def load_qkv(sizes, me_ref, refs, qkv_w, sem):
    if len(refs) == 1:
        pltpu.make_async_copy(refs[0], qkv_w, sem).start()
        return
    share = sizes["y"] * sizes["c"]
    stacks = [ref.at[i] for ref in refs for i in range(ref.shape[0])]
    parts = [(qkv_w, refs[0].shape[2], qkv_w.shape[1] // share, 0, 1)]
    move_pieces(sizes, me_ref, stacks, parts, sem, True, placed=True)


def load_ff(sizes, me_ref, refs, stacked, wholes, sems):
    if stacked:
        for i, part in enumerate(ff_parts(sizes, refs[0].shape[1], *wholes)):
            move_pieces(sizes, me_ref, refs, [part], sems.at[i], True)
    else:
        for i, (ref, whole) in enumerate(zip(refs, wholes)):
            pltpu.make_async_copy(ref, whole, sems.at[i]).start()


def ff_parts(sizes, rows, out_w, in_w, down_w):
    share = sizes["y"] * sizes["c"]
    oc, ic, dc = out_w.shape[1] // share, in_w.shape[1] // share, down_w.shape[1] // share
    folds = down_w.shape[0] // out_w.shape[0]
    return [
        (out_w, rows, oc, 0, 1),
        (in_w, rows, ic, oc, 1),
        (down_w, rows * folds, dc, oc + ic, folds),
    ]


def unpack_small(small_s, route_cols, experts_rows):
    share, d, _ = small_s.shape
    i0 = lax.broadcasted_iota(jnp.int32, (8, LANES), 0)
    i1 = lax.broadcasted_iota(jnp.int32, (8, LANES), 1)
    gb = mm((i1 == i0 + route_cols).astype(BF16), small_s[0], NT)
    route = None
    for e in range(share):
        i0 = lax.broadcasted_iota(jnp.int32, (experts_rows, LANES), 0)
        i1 = lax.broadcasted_iota(jnp.int32, (experts_rows, LANES), 1)
        pick = ((i0 - e * route_cols == i1) & (i1 < route_cols)).astype(BF16)
        part = mm(pick, small_s[e], NT)
        route = part if route is None else route + part
    return gb, route.astype(BF16)


def attend_kernel(sizes, stacked, route_cols, me_ref, tok_ref, cols_ref, rows_ref, *rest):
    if not stacked:
        gb_in, rest = rest[0], rest[1:]
    n_w = 3 if stacked else 1
    w_refs = rest[:n_w]
    rest = rest[n_w:]
    qkv_ref, att_ref = rest[:2]
    d = tok_ref.shape[1]
    if stacked:
        gb_ref, route_ref, qkv_w, small_s, sems = rest[2:]
        first = qkv_w.shape[1] // (sizes["y"] * sizes["c"])
        stacks = [ref.at[i] for ref in w_refs for i in range(ref.shape[0])]
        move_pieces(sizes, me_ref, stacks, [(small_s, w_refs[0].shape[2], LANES, first, 1)], sems.at[1], True, placed=True)
        load_qkv(sizes, me_ref, w_refs, qkv_w, sems.at[0])
        wait_all(small_s, sems.at[1])
        gb, route = unpack_small(small_s, route_cols, route_ref.shape[0])
        gb_ref[...] = gb
        route_ref[...] = route
    else:
        qkv_w, sems = rest[2:]
        load_qkv(sizes, me_ref, w_refs, qkv_w, sems.at[0])
        gb = gb_in[...]
    xhat, _ = norm_parts(tok_ref[...].astype(F32))
    n1 = (xhat * gb[0:1, :] + gb[3:4, :]).astype(BF16)
    wait_all(qkv_w, sems.at[0])
    for j in range(3):
        qkv_ref[:, j * d : (j + 1) * d] = mm(n1, qkv_w[:, j * d : (j + 1) * d]).astype(BF16)
    qkv_ref.send()
    qkv_ref = qkv_ref.buffer
    low_half = lax.broadcasted_iota(jnp.int32, (MAXLEN, LANES), 1) < HEAD_DIM
    for q0, k0, k1 in head_blocks(tok_ref.shape[0]):
        mask = same_sentence(cols_ref, rows_ref, q0, k0, k1)
        for p in range(d // LANES):
            at = lambda j: slice(j * d + p * LANES, j * d + (p + 1) * LANES)
            q2 = two_heads(qkv_ref[q0 : q0 + MAXLEN, at(0)], low_half)
            prob = probabilities(q2, qkv_ref[k0:k1, at(1)], mask).astype(BF16)
            out = mm(prob, qkv_ref[k0:k1, at(2)])
            att_ref[q0 : q0 + MAXLEN, at(0)] = pick_heads(out, low_half).astype(BF16)


def probs_kernel(cols_ref, rows_ref, qkv_ref, *prob_refs):
    d = qkv_ref.shape[1] // 3
    low_half = lax.broadcasted_iota(jnp.int32, (MAXLEN, LANES), 1) < HEAD_DIM
    n = len(prob_refs) // 2
    for prob_ref, (q0, k0, k1) in zip(zip(prob_refs[:n], prob_refs[n:]), head_blocks(qkv_ref.shape[0])):
        mask = same_sentence(cols_ref, rows_ref, q0, k0, k1)
        pairs = d // LANES
        for p in range(pairs):
            lanes = slice(p * LANES, (p + 1) * LANES)
            q2 = two_heads(qkv_ref[q0 : q0 + MAXLEN, lanes], low_half)
            prob = probabilities(q2, qkv_ref[k0:k1, d + p * LANES : d + (p + 1) * LANES], mask)
            prob_ref[2 * p // pairs][2 * p % pairs // 2] = prob
        for ref in prob_ref:
            ref.send()


def attend_back_blocks(pairs, prob_refs, qkv_ref, atg_ref, dq_s, dk_s, dv_s):
    toks, d = atg_ref.shape
    scale = 1.0 / math.sqrt(HEAD_DIM)
    dk_s[...] = jnp.zeros_like(dk_s)
    dv_s[...] = jnp.zeros_like(dv_s)
    low_half = lax.broadcasted_iota(jnp.int32, (MAXLEN, LANES), 1) < HEAD_DIM
    for prob_ref, (q0, k0, k1) in zip(prob_refs, head_blocks(toks)):
        for i, p in enumerate(pairs):
            at = lambda j: slice(j * d + p * LANES, j * d + (p + 1) * LANES)
            lanes = slice(i * LANES, (i + 1) * LANES)
            q2 = two_heads(qkv_ref[q0 : q0 + MAXLEN, at(0)], low_half)
            keys, values = qkv_ref[k0:k1, at(1)], qkv_ref[k0:k1, at(2)]
            prob = prob_ref[i]
            a2 = two_heads(atg_ref[q0 : q0 + MAXLEN, at(0)], low_half)
            prob_grad = mm(a2, values, NT)
            dv_s[k0:k1, lanes] += mm(prob.astype(BF16), a2, TN)
            inner = jnp.sum(prob_grad * prob, axis=-1, keepdims=True)
            score_grad = (prob * (prob_grad - inner)).astype(BF16)
            dq_s[q0 : q0 + MAXLEN, lanes] = pick_heads(mm(score_grad, keys), low_half)
            dk_s[k0:k1, lanes] += mm(score_grad, q2, TN)
    return [
        (dq_s[...] * scale).astype(BF16),
        (dk_s[...] * scale).astype(BF16),
        dv_s[...].astype(BF16),
    ]


def attend_back_first_kernel(n_prob, *refs):
    qkv_ref, atg_ref = refs[:2]
    prob_refs = refs[2 : 2 + n_prob]
    out_ref, dq_s, dk_s, dv_s = refs[2 + n_prob :]
    pairs = range(out_ref.shape[2] // LANES)
    grads = attend_back_blocks(pairs, prob_refs, qkv_ref, atg_ref, dq_s, dk_s, dv_s)
    for j in range(3):
        out_ref[j] = grads[j]


def attend_back_kernel(sizes, stacked, n_prob, me_ref, gb_ref, qkv_ref, atg_ref, *rest):
    prob_refs = rest[:n_prob]
    first_ref, tok_ref, ag_ref = rest[n_prob : n_prob + 3]
    rest = rest[n_prob + 3 :]
    n_w = 3 if stacked else 1
    w_refs = rest[:n_w]
    gtok_ref = rest[n_w]
    g_refs = rest[n_w + 1 : -7]
    qkv_w, dq_s, dk_s, dv_s, gqkv_s, small_s, sems = rest[-7:]
    load_qkv(sizes, me_ref, w_refs, qkv_w, sems.at[0])
    d = tok_ref.shape[1]
    pairs = range(first_ref.shape[2] // LANES, d // LANES)
    grads = attend_back_blocks(pairs, prob_refs, qkv_ref, atg_ref, dq_s, dk_s, dv_s)
    grads = [jnp.concatenate([first_ref[j], grads[j]], axis=1) for j in range(3)]
    xhat, r = norm_parts(tok_ref[...].astype(F32))
    n1 = (xhat * gb_ref[0:1, :] + gb_ref[3:4, :]).astype(BF16)
    rows, cols = g_refs[0].shape[1], 3 * d // (sizes["y"] * sizes["c"])
    for j in range(3):
        gqkv_s[:, j * d : (j + 1) * d] = mm(n1, grads[j], TN).astype(BF16)
    if stacked:
        move_pieces(sizes, me_ref, g_refs, [(gqkv_s, rows, cols, 0, 1)], sems.at[1], False)
    else:
        pltpu.make_async_copy(gqkv_s, g_refs[0], sems.at[1]).start()
    wait_all(qkv_w, sems.at[0])
    n1_grad = sum(mm(grads[j], qkv_w[:, j * d : (j + 1) * d], NT) for j in range(3))
    dv, gain, bias = norm_back(xhat, r, gb_ref[0:1, :], n1_grad)
    small_s[...] = as_columns([gain, bias]).astype(BF16)
    if stacked:
        move_pieces(sizes, me_ref, g_refs, [(small_s, rows, LANES, cols, 1)], sems.at[1], False)
    else:
        pltpu.make_async_copy(small_s, g_refs[1], sems.at[1]).start()
    gtok_ref[...] = ag_ref[...] + dv
    for ref in g_refs:
        wait_all(ref, sems.at[1])


def as_columns(rows):
    n = len(rows)
    block = jnp.concatenate(rows + [jnp.zeros((16 - n, rows[0].shape[1]), F32)], axis=0).astype(BF16)
    i0 = lax.broadcasted_iota(jnp.int32, (16, LANES), 0)
    i1 = lax.broadcasted_iota(jnp.int32, (16, LANES), 1)
    return mm(block, (i0 == i1).astype(BF16), TN)


def feed_kernel(sizes, stacked, me_ref, tok_ref, att_ref, gb_ref, cols_ref, rows_ref, route_ref, cot_ref, *rest):
    n_w = len(OFFSETS) if stacked else 3
    w_refs = rest[:n_w]
    rest = rest[n_w:]
    after_ref, two_ref, gate_ref, send_ref = rest[:4]
    x_s, g_s, send_sems = rest[-3:]
    rest = rest[:-3]
    out_w, in_w, down_w, sems = rest[-4:]
    load_ff(sizes, me_ref, w_refs, stacked, (out_w, in_w, down_w), sems)
    ff = in_w.shape[1]
    toks, d = tok_ref.shape
    wait_all(out_w, sems.at[0])
    after = tok_ref[...].astype(F32) + mm(att_ref[...], out_w[...])
    after_ref[...] = after
    after_ref.send()
    xhat, _ = norm_parts(after)
    n2 = (xhat * gb_ref[1:2, :] + gb_ref[4:5, :]).astype(BF16)
    wait_all(in_w, sems.at[1])
    step = 512
    total = None
    for j in range(ff // step):
        hidden = gelu(mm(n2, in_w[:, j * step : (j + 1) * step])).astype(BF16)
        if j == 0:
            wait_all(down_w, sems.at[2])
        part = mm(hidden, down_w[j * step : (j + 1) * step, :])
        total = part if total is None else total + part
    layer_two = after + total
    two_ref[...] = layer_two
    two_ref.send()
    xhat, _ = norm_parts(layer_two)
    n3 = (xhat * gb_ref[2:3, :] + gb_ref[5:6, :]).astype(BF16)
    logits = mm(n3, route_ref[...], NT)
    lane = lax.broadcasted_iota(jnp.int32, logits.shape, 1)
    chosen = [
        jnp.sum(jnp.where(lane == cols_ref[:, c + 1 : c + 2], logits, 0.0), axis=1, keepdims=True)
        for c in range(2)
    ]
    peak = jnp.maximum(chosen[0], chosen[1])
    exps = [jnp.exp(v - peak) for v in chosen]
    gates = [v / (exps[0] + exps[1]) for v in exps]
    lane = lax.broadcasted_iota(jnp.int32, gate_ref.shape, 1)
    gate_ref[...] = jnp.where(lane == 0, gates[0], jnp.where(lane == 1, gates[1], 0.0))
    upstream = cot_ref[...].astype(F32)
    row_grads = [(gates[c] * upstream).astype(BF16) for c in range(2)]
    experts, cap, _ = x_s.shape
    chunk = min(512, experts * cap)
    per = chunk // cap
    sends = [pltpu.make_async_copy(v, send_ref.at[:, i], send_sems.at[i]) for i, v in enumerate((x_s, g_s))]
    hots = []
    for j in range(experts * cap // chunk):
        slot = lax.broadcasted_iota(jnp.int32, (chunk, toks), 0) + j * chunk
        hots.append([(slot == rows_ref[c + 1 : c + 2, :]).astype(BF16) for c in range(2)])
        x_s[j * per : (j + 1) * per] = mm(hots[-1][0] + hots[-1][1], n3).astype(BF16).reshape(per, cap, x_s.shape[2])
    sends[0].start()
    for j, hot in enumerate(hots):
        rows = (mm(hot[0], row_grads[0]) + mm(hot[1], row_grads[1])).astype(BF16)
        g_s[j * per : (j + 1) * per] = rows.reshape(per, cap, g_s.shape[2])
    sends[1].start()
    for copy in sends:
        copy.wait()


def hidden_kernel(sizes, stacked, me_ref, after_ref, gb_ref, *rest):
    n_w = len(OFFSETS) if stacked else 1
    w_refs = rest[:n_w]
    hid_ref, slope_ref, in_w, sems = rest[n_w:]
    d, ff = in_w.shape
    if stacked:
        oc = d // (sizes["y"] * sizes["c"])
        parts = [(in_w, w_refs[0].shape[1], ff // (sizes["y"] * sizes["c"]), oc, 1)]
        move_pieces(sizes, me_ref, w_refs, parts, sems.at[0], True)
    else:
        pltpu.make_async_copy(w_refs[0], in_w, sems.at[0]).start()
    xhat, _ = norm_parts(after_ref[...])
    n2 = (xhat * gb_ref[1:2, :] + gb_ref[4:5, :]).astype(BF16)
    wait_all(in_w, sems.at[0])
    step = 512

    @pl.loop(0, ff // step)
    def _(j):
        hidden, slope = gelu_both(mm(n2, in_w[:, pl.ds(pl.multiple_of(j * step, step), step)]))
        hid_ref.buffer[j] = hidden.astype(BF16)
        hid_ref.part(j)
        slope_ref.buffer[j] = slope
        slope_ref.part(j)


def feed_back_kernel(sizes, stacked, me_ref, cols_ref, cot_ref, gate_ref, two_ref, gb_ref, route_ref, after_ref, hid_ref, slope_ref, att_ref, back_ref, *rest):
    n_w = len(OFFSETS) if stacked else 3
    w_refs = rest[:n_w]
    rest = rest[n_w:]
    lout_ref, ag_ref, atg_ref = rest[:3]
    g_refs = rest[3:-12]
    out_w, in_w, down_w, gout_s, gin_s, gdown_s, small_s, res_s, ing_s, back_sems, wait_sem, sems = rest[-12:]
    gets = [pltpu.make_async_copy(back_ref.at[:, i], v, back_sems.at[i]) for i, v in enumerate((res_s, ing_s))]
    for copy in gets:
        copy.start()
    load_ff(sizes, me_ref, w_refs, stacked, (out_w, in_w, down_w), wait_sem)
    toks, d = after_ref.shape
    ff = in_w.shape[1]
    experts, cap, _ = res_s.shape
    slots = experts * cap
    slot = lax.broadcasted_iota(jnp.int32, (toks, slots), 1)
    hot = [(slot == cols_ref[:, c + 3 : c + 4]).astype(BF16) for c in range(2)]
    gates = [gate_ref[:, c : c + 1] for c in range(2)]
    upstream = cot_ref[...].astype(F32)
    layer_two = two_ref[...]
    xhat3, r3 = norm_parts(layer_two)
    n3 = (xhat3 * gb_ref[2:3, :] + gb_ref[5:6, :]).astype(BF16)
    gets[0].wait()
    results = res_s[...].reshape(slots, d)
    picked = [mm(hot[c], results) for c in range(2)]
    lout_ref[...] = (layer_two + gates[0] * picked[0] + gates[1] * picked[1]).astype(BF16)
    lout_ref.send()
    gate_grad = [jnp.sum(upstream * v, axis=1, keepdims=True) for v in picked]
    mean = gates[0] * gate_grad[0] + gates[1] * gate_grad[1]
    lane = lax.broadcasted_iota(jnp.int32, (toks, LANES), 1)
    logit_grad = sum(
        jnp.where(lane == cols_ref[:, c + 1 : c + 2], gates[c] * (gate_grad[c] - mean), 0.0) for c in range(2)
    ).astype(BF16)
    grad_route = mm(n3, logit_grad, TN)
    gets[1].wait()
    three_grad = mm(hot[0] + hot[1], ing_s[...].reshape(slots, d)) + mm(logit_grad, route_ref[...])
    dv, gain3, bias3 = norm_back(xhat3, r3, gb_ref[2:3, :], three_grad)
    two_grad = upstream + dv
    ffn_grad = two_grad.astype(BF16)
    xhat, r = norm_parts(after_ref[...])
    n2 = (xhat * gb_ref[1:2, :] + gb_ref[4:5, :]).astype(BF16)
    wait_all(down_w, wait_sem.at[2])
    wait_all(in_w, wait_sem.at[1])
    step = 512
    hid_s, slope_s, n2_grad = hid_ref.ready(), slope_ref.ready(), ag_ref.buffer
    n2_grad[...] = jnp.zeros_like(n2_grad)

    @pl.loop(0, ff // step)
    def _(j):
        at = pl.ds(pl.multiple_of(j * step, step), step)
        gdown_s[at, :] = mm(hid_s[j], ffn_grad, TN).astype(BF16)
        pre_grad = (mm(ffn_grad, down_w[at, :], NT) * slope_s[j]).astype(BF16)
        gin_s[:, at] = mm(n2, pre_grad, TN).astype(BF16)
        n2_grad[...] += mm(pre_grad, in_w[:, at], NT)

    if stacked:
        _, rows, width = g_refs[0].shape
        parts = ff_parts(sizes, rows, gout_s, gin_s, gdown_s)
        move_pieces(sizes, me_ref, g_refs, parts[1:], sems.at[0], False)
    else:
        for src, dst in zip((gin_s, gdown_s), g_refs[1:3]):
            pltpu.make_async_copy(src, dst, sems.at[0]).start()
    dv, gain2, bias2 = norm_back(xhat, r, gb_ref[1:2, :], n2_grad[...])
    after_grad = two_grad + dv
    ag_ref[...] = after_grad
    ag_ref.send()
    attn_grad = after_grad.astype(BF16)
    gout_s[...] = mm(att_ref[...], attn_grad, TN).astype(BF16)
    lanes = lax.broadcasted_iota(jnp.int32, (16, LANES), 1)
    lanes = lanes - lax.broadcasted_iota(jnp.int32, (16, LANES), 0)
    norms = jnp.concatenate([gain2, gain3, bias2, bias3, jnp.zeros((12, d), F32)], axis=0).astype(BF16)
    n_route = route_columns(sizes)
    small_s[...] = (grad_route + mm(norms, (lanes == n_route).astype(BF16), TN)).astype(BF16)
    if stacked:
        parts = [parts[0], (small_s, rows, LANES, width - LANES, 1)]
        move_pieces(sizes, me_ref, g_refs, parts, sems.at[0], False)
    else:
        for src, dst in zip((gout_s, small_s), (g_refs[0], g_refs[3])):
            pltpu.make_async_copy(src, dst, sems.at[0]).start()
    wait_all(out_w, wait_sem.at[0])
    atg_ref[...] = mm(attn_grad, out_w[...], NT).astype(BF16)
    for ref in g_refs:
        wait_all(ref, sems.at[0])


def route_columns(sizes):
    return sizes["y"] * sizes["c"] * sizes["x"]


def gate_kernel(*refs):
    refs[-1][...] = jnp.zeros_like(refs[-1])


def expert_kernel(n_ring, gate_ref, recv_ref, *rest):
    w_refs = rest[:n_ring]
    ret_ref = rest[n_ring]
    hid_ref, pg_ref, x_s, g_s, up_s, down_s, acc_s, gacc_s, sems, w_sems = rest[n_ring + 1 :]
    gets = [pltpu.make_async_copy(recv_ref.at[:, i], v, sems.at[i]) for i, v in enumerate((x_s, g_s))]
    gets[0].start()
    per, _, f = w_refs[0].shape
    n_src, cap, d = x_s.shape
    for s in range(n_ring):
        for k in range(per):
            piece = w_refs[s].at[k]
            cols = pl.ds(k * f, f)
            pltpu.make_async_copy(piece.at[pl.ds(0, d), :], up_s.at[s, :, cols], w_sems.at[s]).start()
            for b in range(d // f):
                part = piece.at[pl.ds(d + b * f, f), :]
                pltpu.make_async_copy(part, down_s.at[s, cols, pl.ds(b * f, f)], w_sems.at[s]).start()
        if s == 0:
            gets[1].start()
    rows = n_src * cap
    step = min(512, rows)
    blocks = [(slice(j, j + step), slice(j // cap, (j + step) // cap)) for j in range(0, rows, step)]
    for copy in gets:
        copy.wait()
    acc_s[...] = jnp.zeros_like(acc_s)
    gacc_s[...] = jnp.zeros_like(gacc_s)
    hid_s, pg_s = hid_ref.buffer, pg_ref.buffer

    @pl.loop(0, n_ring)
    def _(s):
        wait_all(up_s.at[s], w_sems.at[s])
        wait_all(down_s.at[s], w_sems.at[s])
        for at, src in blocks:
            x = x_s[src].reshape(step, d)
            hidden, slope = gelu_both(mm(x, up_s[s]))
            hidden = hidden.astype(BF16)
            hid_s[s, at, :] = hidden
            acc_s[at, :] += mm(hidden, down_s[s])
            pre_grad = (mm(g_s[src].reshape(step, d), down_s[s], NT) * slope).astype(BF16)
            pg_s[s, at, :] = pre_grad
            gacc_s[at, :] += mm(pre_grad, up_s[s], NT)
        hid_ref.part(s)
        pg_ref.part(s)

    x_s[...] = acc_s[...].astype(BF16).reshape(x_s.shape)
    g_s[...] = gacc_s[...].astype(BF16).reshape(g_s.shape)
    puts = [pltpu.make_async_copy(v, ret_ref.at[:, i], sems.at[i]) for i, v in enumerate((x_s, g_s))]
    for copy in puts:
        copy.start()
    for copy in puts:
        copy.wait()


def expert_grad_kernel(places, recv_ref, hid_ref, pg_ref, *refs):
    n = len(places)
    out_refs = refs[:n]
    x_s, g_s, hid_s, pg_s, out_s, sems, block_sems, out_sem = refs[n:]
    gets = [pltpu.make_async_copy(recv_ref.at[:, i], v, sems.at[i]) for i, v in enumerate((x_s, g_s))]
    for copy in gets:
        copy.start()
    for s, place in enumerate(places):
        for ref, v in ((pg_ref, pg_s), (hid_ref, hid_s)):
            pltpu.make_async_copy(ref.at[place], v.at[s], block_sems.at[s]).start()
    n_src, cap, d = x_s.shape
    rows = n_src * cap
    _, per, _, f = out_s.shape
    for copy in gets:
        copy.wait()

    @pl.loop(0, n)
    def _(s):
        wait_all(pg_s.at[s], block_sems.at[s])
        wait_all(hid_s.at[s], block_sems.at[s])
        up = mm(x_s[...].reshape(rows, d), pg_s[s], TN).astype(BF16)
        down = mm(hid_s[s], g_s[...].reshape(rows, d), TN).astype(BF16)
        for k in range(per):
            cols = slice(k * f, (k + 1) * f)
            out_s[s, k, 0:d, :] = up[:, cols]
            for b in range(d // f):
                out_s[s, k, d + b * f : d + (b + 1) * f, :] = down[cols, b * f : (b + 1) * f]

    puts = [pltpu.make_async_copy(out_s.at[s], ref, out_sem.at[s]) for s, ref in enumerate(out_refs)]
    for copy in puts:
        copy.start()
    for copy in puts:
        copy.wait()


def local(sizes, tokens, lengths, task_ids, expert_table, norm_gain, norm_bias, w_qkv, w_out, w_in, w_down, w_router, expert_up, expert_down, cotangent):
    toks, d = tokens.shape
    local_experts, _, f = expert_up.shape
    assert local_experts == sizes["x"] == 2
    share = sizes["y"] * sizes["c"]
    n_hid = sizes["z"] * sizes["x"]
    experts = share * local_experts
    capacity = 2 * toks // experts
    slots = experts * capacity
    ff = w_in.shape[1] * share
    rc = w_router.shape[1]
    rows_dev = d // n_hid
    n_ring = sizes["z"]
    ring = [(i, (i + 1) % n_ring) for i in range(n_ring)]
    down = [(j, i) for i, j in ring]
    n_up = n_ring // 2
    n_down = n_ring - 1 - n_up
    stacked = sizes["y"] == sizes["c"] == 2 and all(
        w.shape[1] % LANES == 0 for w in (w_qkv, w_out, w_in, w_down)
    )

    def after(v, *others):
        return lax.optimization_barrier((v,) + others)[0]

    def swap(v, axis, by=1):
        n = math.prod(sizes[a] for a in axis)
        return lax.ppermute(v, axis, [(i, i ^ by) for i in range(n)])

    def gather_z(piece):
        return [piece] + [swap(piece, ("z",), by) for by in range(1, n_ring)]

    def plane_swaps(stacks):
        return [swap(stacks[by], ("y", "x"), by) for by in range(1, len(PLANE))]

    def other_core(stacks):
        return [swap(t, ("c",)) for t in stacks]

    def add_core(near, far, name, placed=False):
        n, shape = len(PLANE), near[0].shape
        outs = [sds((n,) + shape, BF16)] if placed else [sds(shape, F32)] + [sds(shape, BF16)] * (n - 1)
        return call(
            functools.partial(sum_cores_kernel, placed),
            name,
            K[name],
            outs,
            [smem()] + [vmem()] * (2 * n),
            [anywhere()] if placed else [vmem()] * n,
            [pltpu.VMEM((n,) + shape, BF16), dma((n,))] if placed else [],
            SMALL_BYTES,
        )(me, *[v for v in near[:n]], *far)

    def add_plane(mine, got):
        total = sum((v.astype(F32) for v in got), mine)
        return total[0], total[1:].astype(BF16)

    def z_swaps(parts):
        return [swap(parts[by - 1], ("z",), by) for by in range(1, n_ring)]

    def add_z(mine, got):
        return sum((v.astype(F32) for v in got), mine)

    def exchange(v):
        return lax.all_to_all(v, ("y", "c", "x"), split_axis=0, concat_axis=0, tiled=True)

    def gather_whole(w):
        w = lax.all_gather(w.astype(BF16), ("y", "c"), axis=1, tiled=True)
        return lax.all_gather(w, ("z", "x"), axis=0, tiled=True)

    def reduce_whole(g):
        g = lax.psum_scatter(g.astype(F32), ("z", "x"), scatter_dimension=0, tiled=True)
        return lax.psum_scatter(g, ("y", "c"), scatter_dimension=1, tiled=True)

    def sds(shape, dtype):
        return jax.ShapeDtypeStruct(shape, dtype)

    dma = pltpu.SemaphoreType.DMA
    me = jnp.stack([lax.axis_index(a) for a in AXES]).astype(jnp.int32)
    x_at = lax.axis_index("x")

    def piece_of(at):
        up = lax.dynamic_index_in_dim(expert_up, at, 0, keepdims=False)
        down = lax.dynamic_index_in_dim(expert_down, at, 0, keepdims=False)
        return jnp.concatenate(
            [up] + [down[:, b * f : (b + 1) * f] for b in range(d // f)], axis=0
        ).astype(BF16)

    def routes(lengths):
        return find_routes(lengths, task_ids, expert_table, toks, experts, capacity)

    if stacked:
        folds = w_down.shape[0] // rows_dev
        width = w_out.shape[1] + w_in.shape[1] + folds * w_down.shape[1]
        small = jnp.concatenate([w_router, norm_gain, norm_bias], axis=1)
        small = jnp.pad(small, ((0, 0), (0, LANES - small.shape[1])))
        qkv_piece = jnp.concatenate([w_qkv, small], axis=1).astype(BF16)
        ff_piece, own, other = call(
            pack_kernel,
            "pack",
            K["pack"],
            [sds((rows_dev, width), BF16)] + [sds((2 * d, f), BF16)] * 2,
            [smem()] + ["late"] * 5,
            ["early"] * 3,
        )(me, w_out, w_in, w_down, expert_up, expert_down)
        expert_x = swap(other, ("x",))
        qkv_z = gather_z(qkv_piece)
        mine = jnp.stack(qkv_z)
        qkv_w = lax.all_to_all(jnp.stack([mine] * len(PLANE)), ("y", "x"), split_axis=0, concat_axis=0, tiled=True)
        ff_z = gather_z(after(ff_piece, *qkv_z[1:]))
        rows, cols = routes(after(lengths, *ff_z[1:]))
        qkv_w = after(qkv_w, rows)
        half = len(PLANE) // 2
        qkv_w = [qkv_w] + other_core([qkv_w[:half], qkv_w[half:]])
        blocks = [after(jnp.stack([own, expert_x]), *ff_z[1:])]
        blocks.append(lax.ppermute(blocks[0], "z", ring))
        mine = jnp.stack(ff_z)
        ffw = [mine] + plane_swaps([mine] * len(PLANE))
        tokens_in = after(tokens, rows)
        gb_in = []
    else:
        qkv_w = [gather_whole(w_qkv)]
        ffw = [gather_whole(w_out), gather_whole(w_in), gather_whole(w_down)]
        small = jnp.concatenate([w_router, norm_gain, norm_bias], axis=1)
        small = lax.all_gather(small.astype(BF16), AXES)
        route = small[:, :, :rc].reshape(share, d, rc).transpose(0, 2, 1).reshape(experts, d)
        route = jnp.pad(route, ((0, LANES - experts), (0, 0)))
        gb = small[:n_hid, :, rc:].reshape(d, 6).T.astype(F32)
        gb = jnp.pad(gb, ((0, 2), (0, 0)))
        gb_in = [gb]
        tokens_in = tokens
        rows, cols = routes(lengths)
        blocks = [jnp.stack([piece_of(x_at), swap(piece_of(1 - x_at), ("x",))])]
        blocks.append(lax.ppermute(blocks[0], "z", ring))

    out_shape = [sds((toks, 3 * d), BF16), sds((toks, d), BF16)]
    scratch = [pltpu.VMEM((d, 3 * d), BF16)]
    if stacked:
        out_shape += [sds((8, d), F32), sds((LANES, d), BF16)]
        scratch += [pltpu.VMEM((share, d, LANES), BF16)]
    out = call(
        functools.partial(attend_kernel, sizes, stacked, rc),
        "attend",
        K["attend"],
        out_shape,
        [smem()] + ["late"] * 3 + [vmem()] * len(gb_in) + [anywhere()] * len(qkv_w),
        ["early"] * 2 + [vmem()] * (len(out_shape) - 2),
        scratch + [dma((2,))],
    )(me, tokens_in, cols, rows, *gb_in, *qkv_w)
    qkv, attended = out[:2]
    if stacked:
        gb, route = out[2:]
        ffw = [ffw[0]] + [after(t, attended, *(blocks[-1:] if K["ringff"] else [])) for t in ffw[1:]]
        ffw = ffw + other_core(ffw)
    ups, downs = blocks, [blocks[0]]
    while len(ups) <= n_up:
        ups.append(lax.ppermute(after(ups[-1], attended), "z", ring))
    while len(downs) <= n_down:
        downs.append(lax.ppermute(after(downs[-1], attended), "z", down))
    blocks = ups + downs[:0:-1]

    f_scratch = [pltpu.VMEM((d, d), BF16), pltpu.VMEM((d, ff), BF16), pltpu.VMEM((ff, d), BF16)]
    pair = [pltpu.VMEM((experts, capacity, d), BF16)] * 2
    after_attn, layer_two, gates, send = call(
        functools.partial(feed_kernel, sizes, stacked),
        "feed",
        K["feed"],
        [sds((toks, d), F32), sds((toks, d), F32), sds((toks, LANES), F32)]
        + [sds((experts, 2, capacity, d), BF16)],
        [smem()] + ["late"] * 2 + [vmem()] + ["late"] * 4 + [anywhere()] * len(ffw),
        ["early"] * 3 + [anywhere()],
        f_scratch + [dma((3,))] + pair + [dma((2,))],
    )(me, tokens, attended, gb, cols, rows, route, cotangent, *ffw)
    recv = exchange(send)
    gate = call(gate_kernel, "gate", K["gate"], sds((8, LANES), F32), [anywhere()] * (n_ring - 1), vmem())(*blocks[1:])
    block = [sds((n_ring, slots, 2 * f), BF16)]
    out = call(
        functools.partial(expert_kernel, n_ring),
        "experts",
        K["experts"],
        [sds(recv.shape, BF16)] + block * 2,
        [anywhere()] * (2 + n_ring),
        [anywhere()] + ["early"] * 2,
        pair
        + [pltpu.VMEM((n_ring, d, 2 * f), BF16), pltpu.VMEM((n_ring, 2 * f, d), BF16)]
        + [pltpu.VMEM((slots, d), F32)] * 2
        + [dma((2,)), dma((n_ring,))],
    )(gate, recv, *blocks)
    hids, pre_grads = out[1:]
    back = exchange(out[0])

    def expert_grads(places, recv):
        n = len(places)
        blocks = [pltpu.VMEM((n, slots, 2 * f), BF16)] * 2 + [pltpu.VMEM((n, 2, 2 * d, f), BF16)]
        return call(
            functools.partial(expert_grad_kernel, places),
            "expert_grads",
            K["expert_grads"] * n,
            [sds((2, 2 * d, f), BF16)] * n,
            [anywhere()] * 3,
            [anywhere()] * n,
            pair + blocks + [dma((2,)), dma((n,)), dma((n,))],
        )(recv, hids, pre_grads)

    far_grads = expert_grads([1], recv)
    moving = lax.ppermute(far_grads[0], "z", ring)
    rest = expert_grads([s % n_ring for s in range(2, n_ring + 1)], after(recv, far_grads[0]))
    prob_shapes = [sds((d // LANES // 2, 2 * MAXLEN, k1 - k0), F32) for _, k0, k1 in head_blocks(toks)] * 2
    probs = call(
        probs_kernel, "probs", K["probs"], prob_shapes, [vmem()] * 3, ["early"] * len(prob_shapes)
    )(cols, rows, after(qkv, rest[0]))
    hidden, slope = call(
        functools.partial(hidden_kernel, sizes, stacked),
        "hidden",
        K["hidden"],
        [sds((ff // 512, toks, 512), BF16), sds((ff // 512, toks, 512), F32)],
        [smem()] + [vmem()] * 2 + [anywhere()] * (len(OFFSETS) if stacked else 1),
        ["early"] * 2,
        [pltpu.VMEM((d, ff), BF16), dma((1,))],
    )(me, after(after_attn, rest[0]), gb, *(ffw if stacked else ffw[1:2]))

    if stacked:
        ff_cols, qkv_cols = ffw[0].shape[-1] + LANES, qkv_w[0].shape[-1]
        ff_out = [sds((n_ring, rows_dev, ff_cols), BF16)] * len(OFFSETS)
        qkv_out = [sds((n_ring, rows_dev, qkv_cols), BF16)] * len(OFFSETS)
    else:
        ff_out = [sds((d, d), BF16), sds((d, ff), BF16), sds((ff, d), BF16), sds((d, LANES), BF16)]
        qkv_out = [sds((d, 3 * d), BF16), sds((d, LANES), BF16)]
    out = call(
        functools.partial(feed_back_kernel, sizes, stacked),
        "feed_back",
        K["feed_back"],
        [sds((toks, d), BF16), sds((toks, d), F32), sds((toks, d), BF16)] + ff_out,
        [smem()] + ["late"] * 4 + [vmem()] + ["late"] * 5 + [anywhere()] * (1 + len(ffw)),
        ["early"] * 3 + [anywhere()] * len(ff_out),
        f_scratch + f_scratch + [pltpu.VMEM((d, LANES), BF16)] + pair + [dma((2,)), dma((3,)), dma((1,))],
    )(me, cols, cotangent, gates, layer_two, gb, route, after_attn, hidden, slope, attended, after(back, probs[0]), *ffw)
    layer_out, after_grad, att_grad = out[:3]
    ff_grads = out[3:]
    step = n_ring - 2

    def add_on(moving, mine, weight):
        n, shape = 4, (4, mine.shape[0] * mine.shape[1] // 4, mine.shape[2])
        scratch = [pltpu.VMEM(shape, BF16)] * 3 + [dma((3, n))]
        return call(add_kernel, "add", weight, sds(mine.shape, BF16), [anywhere()] * 2, anywhere(), scratch, SMALL_BYTES)(moving, mine)

    for t in range(step - 1):
        if K["tie_ring1"]:
            moving = after(moving, after_grad)
        moving = lax.ppermute(add_on(moving, rest[t], K["add1"]), "z", ring)
    if stacked:
        ff_far = other_core(ff_grads[len(PLANE) :])
    half = d // 2
    n_prob = len(probs) // 2
    acc = [pltpu.VMEM((toks, half), F32)] * 3
    if stacked:
        ff_sums = add_core(ff_grads, ff_far, "sum_ff", True)
        ff_got = [lax.all_to_all(ff_sums[0], ("y", "x"), split_axis=0, concat_axis=0, tiled=True)]
        att_grad = after(att_grad, ff_sums[0])
    first_half = call(
        functools.partial(attend_back_first_kernel, n_prob),
        "attend_back_first",
        K["first"],
        [sds((3, toks, half), BF16)],
        ["late"] * (2 + n_prob),
        [vmem()],
        acc,
    )(qkv, att_grad, *probs[:n_prob])[0]
    att_grad = after(att_grad, first_half)
    out = call(
        functools.partial(attend_back_kernel, sizes, stacked, n_prob),
        "attend_back",
        K["attend_back"],
        [sds((toks, d), F32)] + qkv_out,
        [smem(), vmem()] + ["late"] * (5 + n_prob) + [anywhere()] * len(qkv_w),
        ["early"] + [anywhere()] * len(qkv_out),
        [pltpu.VMEM((d, 3 * d), BF16)]
        + acc
        + [pltpu.VMEM((d, 3 * d), BF16), pltpu.VMEM((d, LANES), BF16), dma((2,))],
    )(me, gb, qkv, att_grad, *probs[n_prob:], first_half, tokens, after_grad, *qkv_w)
    grad_tokens = out[0]
    qkv_grads = out[1:]

    e_at = lax.axis_index("y") * sizes["c"] + lax.axis_index("c")
    if step:
        if K["tie_ring2"]:
            moving = after(moving, grad_tokens)
        moving = lax.ppermute(add_on(moving, rest[step - 1], K["add2"]), "z", ring)
    if stacked:
        qkv_sums = add_core(qkv_grads, other_core(qkv_grads[len(PLANE) :]), "sum_qkv")
        qkv_got = plane_swaps(qkv_sums)
        z_shape = (n_ring, rows_dev, ff_cols)
        ff_send = call(
            sum_plane_kernel,
            "sum_plane",
            K["sum_plane"],
            sds(z_shape, BF16),
            [smem(), vmem()],
            anywhere(),
            [pltpu.VMEM(z_shape, BF16), dma((n_ring,))],
            SMALL_BYTES,
        )(me, ff_got[0])
        qkv_got = [after(v, ff_send) for v in qkv_got]
        moving = after(moving, *qkv_got)
        ff_got = lax.all_to_all(ff_send, "z", split_axis=0, concat_axis=0, tiled=True)
        qkv_mine, qkv_parts_z = add_plane(qkv_sums[0], qkv_got)
        qkv_got = z_swaps(qkv_parts_z)
    other = swap((moving[1].astype(F32) + rest[-1][1].astype(F32)).astype(BF16), ("x",))
    grad_up, grad_edown = call(
        finish_experts_kernel,
        "finish_experts",
        K["finish"],
        [sds(expert_up.shape, F32), sds(expert_down.shape, F32)],
        [smem()] + [anywhere()] * 2 + ["late"],
        ["early"] * 2,
        [pltpu.VMEM((2 * d, f), BF16)] * 2 + [dma((2,))],
        SMALL_BYTES,
    )(me, moving, rest[-1], other)
    if stacked and K["tie_x"] == 1:
        qkv_got = [after(v, grad_up) for v in qkv_got]

    if stacked:
        shapes = [v.shape for v in (w_out, w_in, w_down, w_qkv)]
        shapes += [v.shape[::-1] for v in (w_router, norm_gain, norm_bias)]
        grad_out, grad_in, grad_down, grad_qkv, grad_router, grad_gain, grad_bias = call(
            functools.partial(finish_kernel, n_ring, rc, route_columns(sizes)),
            "finish",
            K["finish"],
            [sds(v, F32) for v in shapes],
            [smem()] + [vmem()] * (1 + n_ring),
            [vmem()] * len(shapes),
            vmem_bytes=SMALL_BYTES,
        )(e_at.reshape(1).astype(jnp.int32), ff_got, qkv_mine, *qkv_got)
        grad_router, grad_gain, grad_bias = grad_router.T, grad_gain.T, grad_bias.T
    else:
        grad_out, grad_in, grad_down = (reduce_whole(g) for g in ff_grads[:3])
        grad_qkv = reduce_whole(qkv_grads[0])
        small_ff, small_qkv = (
            lax.psum(lax.psum_scatter(g.astype(F32), ("z", "x"), scatter_dimension=0, tiled=True), ("y", "c"))
            for g in (ff_grads[3], qkv_grads[1])
        )
        grad_router = lax.dynamic_slice_in_dim(small_ff, e_at * rc, rc, axis=1)
        n_route = route_columns(sizes)
        gains, biases = small_ff[:, n_route : n_route + 2], small_ff[:, n_route + 2 : n_route + 4]
        grad_gain = jnp.concatenate([small_qkv[:, 0:1], gains], axis=1)
        grad_bias = jnp.concatenate([small_qkv[:, 1:2], biases], axis=1)
    return (
        layer_out,
        grad_tokens,
        grad_gain,
        grad_bias,
        grad_qkv,
        grad_out,
        grad_in,
        grad_down,
        grad_router,
        grad_up,
        grad_edown,
    )


def solution(mesh):
    n_exp, n_hid = mesh.shape["expert"], mesh.shape["hidden"]
    sizes = {"y": n_exp // 2, "c": 2, "z": n_hid // 2, "x": 2}
    fine = Mesh(mesh.devices.reshape(tuple(sizes[a] for a in AXES)), AXES)
    both, exp, hid = AXES, ("y", "c"), ("z", "x")
    return jax.shard_map(
        functools.partial(local, sizes),
        mesh=fine,
        in_specs=(
            P(both, None),
            P(both, None),
            P(both, None),
            P(),
            P(hid, None),
            P(hid, None),
            P(hid, exp),
            P(hid, exp),
            P(hid, exp),
            P(hid, exp),
            P(hid, exp),
            P(exp, None, hid),
            P(exp, hid, None),
            P(both, None),
        ),
        out_specs=(
            P(both, None),
            P(both, None),
            P(hid, None),
            P(hid, None),
            P(hid, exp),
            P(hid, exp),
            P(hid, exp),
            P(hid, exp),
            P(hid, exp),
            P(exp, None, hid),
            P(exp, hid, None),
        ),
        check_vma=False,
    )
```
